32 devices in a mesh: exp: 16 (over z, y, x), rep: 2 (over core).
Axes of the slice: x: 2, y: 2, z: 4, core: 2. Of those that a mesh axis runs over, the one named last changes fastest.
Arguments:
- latent: bfloat16 [32, 16, 64], P('exp'), may hold values from -6 to 6
- stem_weight: bfloat16 [144, 1536], replicated, may hold values from -0.5 to 0.5
- norm_gain: float32 [1536], replicated, may hold values from 0.4 to 1.6
- router_weight: bfloat16 [1536, 8], replicated, may hold values from -0.15625 to 0.15625
- routes: int32 [2048, 2], P('exp'), may hold values from 0 to 7, all different within a row; in each aligned block of 128 rows (0 to 127, 128 to 255, ...) at most 40 rows name the same one
- gate_weight: bfloat16 [1536, 24576], P('rep', 'exp'), may hold values from -0.15625 to 0.15625
- up_weight: bfloat16 [1536, 24576], P('rep', 'exp'), may hold values from -0.15625 to 0.15625
- down_weight: bfloat16 [24576, 1536], P('exp', 'rep'), may hold values from -0.109375 to 0.109375
- grad_mixed: bfloat16 [2048, 1536], P('exp'), may hold values from -6 to 6
Outputs:
- mixed: bfloat16 [2048, 1536], P('exp')
- grad_latent: float32 [32, 16, 64], P('exp')
- grad_gate: float32 [1536, 24576], P('rep', 'exp')
- grad_up: float32 [1536, 24576], P('rep', 'exp')
- grad_down: float32 [24576, 1536], P('exp', 'rep')
The draws below stay inside these ranges and needn't reach their ends.
Inputs may be any that keep to these rules, and one draw needn't show every extreme that they name: `routes`: A token's 2 experts differ. Within the 128 tokens of one device, no expert is named more than 40 times, and in every draw some device's tokens name some expert exactly 40 times.
All inputs are finite; a program needn't handle non-finite values.
Results may differ from the reference program's by a relative error of at most 0.023.
Values may be sent and summed in bfloat16 or wider, within the bound.
No kernel may reach another device: no remote copies, remote signals or barrier semaphores. Data moves between devices by JAX's collectives and lax.ppermute only.
A program may use at most 128 MiB of HBM per device.

```python
import math
import jax
import jax.numpy as jnp
import numpy as np
from jax import lax

D = 1536
EXPERTS = 8
FF = 3072
TOPK = 2
C_IN = 16
WID = 64
TOK_DEV = 128
CAP = 40
SUB = 20
SHARDS = 2
HID = 1536
HGT = 32
TOKENS = 2048
N_EXP = 16
N_REP = 2


def shard_levels(stream_key, shape, shards, least, largest):
    def one(axis_at, shards_of):
        heights = jax.random.uniform(jax.random.fold_in(jax.random.fold_in(stream_key, 6), axis_at), (shards_of,), jnp.float32, least / len(shards), largest / len(shards))
        return jnp.repeat(jnp.exp(heights), shape[axis_at] // shards_of).reshape((-1,) + (1,) * (len(shape) - axis_at - 1))

    loudness = one(*shards[0])
    for cut in shards[1:]:
        loudness = loudness * one(*cut)
    return loudness


def assign_block(stream_key, own, number, rows, amount, top, bound, skew):
    ranking = jax.random.permutation(stream_key, amount)
    packed, ordinary = portions_of(amount, rows * top, bound, skew, True), portions_of(amount, rows * top, bound, skew, False)
    places = jnp.arange(amount)

    def named(tallies, offset_by):
        used = int((tallies > 0).sum())
        fixed = max(1, used // 4)
        passed = fixed + (places - fixed + offset_by * (used - fixed)) % max(1, amount - fixed)
        return jnp.zeros((amount,), jnp.int32).at[ranking[jnp.where(places < fixed, places, passed)]].set(jnp.asarray(tallies, jnp.int32))

    tallies = jnp.where(number % 4 == 0, named(packed, number // 4), named(ordinary, number - number // 4 - 1))
    mixed = jax.random.permutation(jax.random.fold_in(own, 3), amount)
    giver, sink = mixed[0:amount // 2 * 2:2], mixed[1:amount // 2 * 2:2]
    room = jnp.minimum(tallies[giver] - 1, bound - tallies[sink]) // 2
    room = jnp.where((giver == ranking[0]) | (sink == ranking[0]) | (tallies[sink] == 0), 0, jnp.maximum(room, 0))
    passed = jax.random.randint(jax.random.fold_in(own, 4), (amount // 2,), 0, 1 << 20) % (room + 1)
    tallies = tallies.at[giver].add(-passed).at[sink].add(passed)
    labels = jnp.searchsorted(jnp.cumsum(tallies), jnp.arange(rows * top), side="right").astype(jnp.int32)
    listing = labels.reshape(top, rows).T
    listing = listing[jax.random.permutation(jax.random.fold_in(own, 1), rows)]
    offset_by = jax.random.randint(jax.random.fold_in(own, 2), (rows, 1), 0, top)
    return jnp.take_along_axis(listing, (jnp.arange(top)[None, :] + offset_by) % top, axis=1)


def portions_of(count, total, most, lean, full):
    portions = [(1 << 20) // math.isqrt(grade ** lean) + 1 for grade in range(1, count + 1)]
    largest = most if full else min(most, max(-(-total // count), total * portions[0] // sum(portions)))
    least = 1 if total - largest >= count - 1 else 0
    given, spare = [largest] + [least] * (count - 1), total - largest - least * (count - 1)
    while spare > 0:
        movable = [i for i in range(1, count) if given[i] < largest] or [i for i in range(1, count) if given[i] < most]
        mass, remaining = sum([portions[i] for i in movable]), spare
        for i in movable:
            addition = min(most - given[i], max(1, remaining * portions[i] // mass), spare)
            given[i] = given[i] + addition
            spare = spare - addition
    return np.array(given)


def gaussian(rng, shape, spread, reach, shards=(), held_as=jnp.bfloat16):
    array = jax.random.normal(rng, shape, jnp.float32) * spread
    if len(shards) > 0:
        array = shard_levels(rng, shape, shards, -0.22, 0.18) * array
    return jnp.clip(array, min=-reach, max=reach).astype(held_as)


def setup_inputs(seed: int = 0) -> dict:
    key_of = jax.random.split(jax.random.key(seed), 10)
    latent = gaussian(key_of[0], (HGT, C_IN, WID), 1.0, 6.0, ((0, 16),))
    stem_weight = gaussian(key_of[1], (9 * C_IN, D), (9 * C_IN) ** -0.5, 0.5)
    norm_gain = jnp.clip(1.0 + 0.12 * jax.random.normal(key_of[2], (D,), jnp.float32), 0.4, 1.6)
    router_weight = gaussian(key_of[3], (D, EXPERTS), D ** -0.5, 0.15625)
    routes_keys = jax.random.split(jax.random.fold_in(key_of[4], 1), TOKENS // TOK_DEV)
    routes_turns = jax.random.permutation(jax.random.fold_in(key_of[4], 3), TOKENS // TOK_DEV)
    routes = jax.vmap(lambda own, number: assign_block(jax.random.fold_in(key_of[4], 2), own, number, TOK_DEV, EXPERTS, TOPK, CAP, 2))(routes_keys, routes_turns).reshape((TOKENS, TOPK))
    gate_weight = gaussian(key_of[5], (D, EXPERTS * FF), D ** -0.5, 0.15625, ((0, 2), (1, 16)))
    up_weight = gaussian(key_of[6], (D, EXPERTS * FF), D ** -0.5, 0.15625, ((0, 2), (1, 16)))
    down_weight = gaussian(key_of[7], (EXPERTS * FF, D), FF ** -0.5, 0.109375, ((0, 16), (1, 2)))
    grad_mixed = gaussian(key_of[8], (TOKENS, D), 1.0, 6.0, ((0, 16),))
    return dict(latent=latent, stem_weight=stem_weight, norm_gain=norm_gain, router_weight=router_weight, routes=routes, gate_weight=gate_weight, up_weight=up_weight, down_weight=down_weight, grad_mixed=grad_mixed)


def rms_norm(values, gain):
    return values * lax.rsqrt(lax.optimization_barrier(jnp.mean(values * values, axis=-1, keepdims=True)) + 1e-06) * gain

def gating(picked):
    chosen = jax.nn.sigmoid(picked)
    return chosen / lax.optimization_barrier(jnp.sum(chosen, axis=-1, keepdims=True))

def rounded(values):
    return lax.optimization_barrier(values.astype(jnp.bfloat16)).astype(jnp.float32)

def per_expert(items):
    rows, grads, gate_w, up_w, down_w = items
    count = rows.shape[0]
    gate_value = gate_w.astype(jnp.float32)
    up_value = up_w.astype(jnp.float32)
    down_value = down_w.astype(jnp.float32)
    pre_gate = jnp.dot(rows, gate_w, preferred_element_type=jnp.float32)
    pre_up = jnp.dot(rows, up_w, preferred_element_type=jnp.float32)
    sigma = jax.nn.sigmoid(pre_gate)
    hidden = rounded(pre_gate * sigma * pre_up)
    partial_value = jnp.einsum('rsh,shd->rsd', hidden.reshape(count, SHARDS, HID), down_value.reshape(SHARDS, HID, D))
    slot_out = lax.optimization_barrier(jnp.sum(rounded(partial_value), axis=1)).astype(jnp.bfloat16)
    grad_hidden = jnp.dot(grads, down_w.T, preferred_element_type=jnp.float32)
    grad_gate_pre = rounded(grad_hidden * pre_up * sigma * (1.0 + pre_gate * (1.0 - sigma)))
    grad_up_pre = rounded(grad_hidden * pre_gate * sigma)
    back_partial = jnp.einsum('rsh,dsh->rsd', grad_gate_pre.reshape(count, SHARDS, HID), gate_value.reshape(D, SHARDS, HID))
    back_partial = back_partial + jnp.einsum('rsh,dsh->rsd', grad_up_pre.reshape(count, SHARDS, HID), up_value.reshape(D, SHARDS, HID))
    slot_back = lax.optimization_barrier(jnp.sum(rounded(back_partial), axis=1)).astype(jnp.bfloat16)
    rows_grouped = rows.astype(jnp.float32).reshape(N_EXP, N_REP, SUB, D)
    grads_grouped = grads.astype(jnp.float32).reshape(N_EXP, N_REP, SUB, D)
    term_gate = lax.optimization_barrier(jnp.sum(rounded(jnp.einsum('igqd,igqf->gdf', rows_grouped, grad_gate_pre.reshape(N_EXP, N_REP, SUB, FF))), axis=0))
    term_up = lax.optimization_barrier(jnp.sum(rounded(jnp.einsum('igqd,igqf->gdf', rows_grouped, grad_up_pre.reshape(N_EXP, N_REP, SUB, FF))), axis=0))
    term_down = lax.optimization_barrier(jnp.sum(rounded(jnp.einsum('igqf,igqd->gfd', hidden.reshape(N_EXP, N_REP, SUB, FF), grads_grouped)), axis=0))
    return (slot_out, slot_back, term_gate, term_up, term_down)

def reference(latent, stem_weight, norm_gain, router_weight, routes, gate_weight, up_weight, down_weight, grad_mixed):
    padded = jnp.pad(latent, ((1, 1), (0, 0), (1, 1)))
    pieces = jnp.stack([padded[i:i + HGT, :, j:j + WID] for i in range(3) for j in range(3)], axis=0)
    patches = jnp.transpose(pieces, (1, 3, 0, 2)).reshape(TOKENS, 9 * C_IN)
    stem = jnp.dot(patches, stem_weight, preferred_element_type=jnp.float32).astype(jnp.bfloat16)
    stem_value = stem.astype(jnp.float32)
    normed = rms_norm(stem_value, norm_gain).astype(jnp.bfloat16)
    logits = jnp.dot(normed, router_weight, preferred_element_type=jnp.float32)
    picked = jnp.take_along_axis(logits, routes, axis=1)
    gates = gating(picked)
    upstream = grad_mixed.astype(jnp.float32)
    grad_rows = (gates[:, :, None] * upstream[:, None, :]).astype(jnp.bfloat16).reshape(-1, D)
    blocks = routes.reshape(N_EXP, TOK_DEV * TOPK)
    onehot = (blocks[..., None] == jnp.arange(EXPERTS, dtype=jnp.int32)).astype(jnp.int32)
    position = lax.optimization_barrier(jnp.sum(onehot * (jnp.cumsum(onehot, axis=1) - 1), axis=-1))
    source_index = jnp.arange(N_EXP, dtype=jnp.int32)[:, None]
    slot_index = ((blocks * N_EXP + source_index) * CAP + position).reshape(-1).astype(jnp.int32)
    total_slots = EXPERTS * N_EXP * CAP
    per_slots = N_EXP * CAP
    slot_in = jnp.zeros((total_slots, D), jnp.bfloat16).at[slot_index].set(jnp.repeat(normed, TOPK, axis=0))
    slot_grad = jnp.zeros((total_slots, D), jnp.bfloat16).at[slot_index].set(grad_rows)
    slot_in = slot_in.reshape(EXPERTS, per_slots, D)
    slot_grad = slot_grad.reshape(EXPERTS, per_slots, D)
    gate_stack = gate_weight.reshape(D, EXPERTS, FF).transpose(1, 0, 2)
    up_stack = up_weight.reshape(D, EXPERTS, FF).transpose(1, 0, 2)
    down_stack = down_weight.reshape(EXPERTS, FF, D)
    results = lax.map(per_expert, (slot_in, slot_grad, gate_stack, up_stack, down_stack))
    slot_out = results[0].reshape(total_slots, D).astype(jnp.float32)
    slot_back = results[1].reshape(total_slots, D).astype(jnp.float32)
    expert_out = slot_out[slot_index].reshape(TOKENS, TOPK, D)
    expert_back = slot_back[slot_index].reshape(TOKENS, TOPK, D)
    mixed = (stem_value + lax.optimization_barrier(jnp.sum(gates[:, :, None] * expert_out, axis=1))).astype(jnp.bfloat16)
    grad_gates = lax.optimization_barrier(jnp.sum(upstream[:, None, :] * expert_out, axis=-1))
    _, gate_pull = jax.vjp(gating, picked)
    grad_picked = gate_pull(grad_gates)[0]
    selector = (routes[:, :, None] == jnp.arange(EXPERTS, dtype=jnp.int32)).astype(jnp.float32)
    grad_logits = lax.optimization_barrier(jnp.sum(selector * grad_picked[:, :, None], axis=1))
    grad_normed = lax.optimization_barrier(jnp.sum(expert_back, axis=1)) + jnp.dot(grad_logits, router_weight.astype(jnp.float32).T, precision=lax.Precision.HIGHEST)
    _, norm_pull = jax.vjp(lambda values: rms_norm(values, norm_gain), stem_value)
    grad_stem = (upstream + norm_pull(grad_normed)[0]).astype(jnp.bfloat16)
    projected = jnp.dot(grad_stem, stem_weight.T, preferred_element_type=jnp.float32).reshape(HGT, WID, 9, C_IN)
    shifted = jnp.pad(projected, ((1, 1), (1, 1), (0, 0), (0, 0)))
    terms = [shifted[2 - i:2 - i + HGT, 2 - j:2 - j + WID, 3 * i + j, :] for i in range(3) for j in range(3)]
    grad_latent = lax.optimization_barrier(jnp.sum(jnp.stack(terms, axis=0), axis=0)).transpose(0, 2, 1)
    grad_gate = results[2].transpose(1, 0, 2).reshape(D, EXPERTS * FF)
    grad_up = results[3].transpose(1, 0, 2).reshape(D, EXPERTS * FF)
    grad_down = results[4].reshape(EXPERTS * FF, D)
    return (mixed, grad_latent, grad_gate, grad_up, grad_down)
```

```python
import jax
import jax.numpy as jnp
from jax import lax
from jax.sharding import PartitionSpec as P

CAP = 40
F32 = jnp.float32
BF16 = jnp.bfloat16


def dot(a, b, contract, batch=((), ())):
    return lax.dot_general(a, b, (contract, batch), preferred_element_type=F32)


def other_core(values):
    return lax.ppermute(values, "rep", [(0, 1), (1, 0)])


def core_sum(values, wire=BF16):
    if lax.axis_size("rep") == 2:
        return values + other_core(values.astype(wire)).astype(F32)
    return lax.psum(values, "rep")


def core_join(values):
    if lax.axis_size("rep") == 2:
        other = other_core(values)
        first = lax.axis_index("rep") == 0
        return jnp.concatenate(
            [jnp.where(first, values, other), jnp.where(first, other, values)], axis=1
        )
    return lax.all_gather(values, "rep", axis=1, tiled=True)


def exchange(values):
    return lax.all_to_all(values, "exp", split_axis=0, concat_axis=0, tiled=True)


def column_keep(count, width, j):
    column = jnp.arange(count, dtype=jnp.int32) % width + (j - 1)
    return ((column >= 0) & (column < width))[None, :]


def patches_of(cells, width):
    count = cells.shape[1]
    padded = jnp.pad(cells, ((0, 0), (width + 1, width + 1)))
    pieces = []
    for i in range(3):
        for j in range(3):
            start = i * width + j
            piece = padded[:, start : start + count]
            pieces.append(jnp.where(column_keep(count, width, j), piece, 0))
    return jnp.concatenate(pieces, axis=0)


def patches_sum(terms, width):
    channels, count = terms.shape[0] // 9, terms.shape[1]
    padded = jnp.pad(terms, ((0, 0), (width + 1, width + 1)))
    total = 0.0
    for i in range(3):
        for j in range(3):
            start = (2 - i) * width + (2 - j)
            k = 3 * i + j
            piece = padded[k * channels : (k + 1) * channels, start : start + count]
            total = total + jnp.where(column_keep(count, width, 2 - j), piece, 0)
    return total


def selection(named):
    tokens = named.shape[-1]
    order = jnp.arange(tokens, dtype=jnp.int32)
    before = (order[:, None] <= order[None, :]).astype(BF16)
    flat = named.astype(BF16).reshape(-1, tokens)
    place = (dot(flat, before, ((1,), (0,))).astype(jnp.int32) - 1).reshape(named.shape)
    slot = jnp.arange(CAP, dtype=jnp.int32)[:, None]
    return ((place[..., None, :] == slot) & named[..., None, :]).astype(BF16)


def local(
    latent,
    stem_weight,
    norm_gain,
    router_weight,
    routes,
    gate_weight,
    up_weight,
    down_weight,
    grad_mixed,
):
    rows_here, channels, width = latent.shape
    half, hid = gate_weight.shape
    model_width = stem_weight.shape[1]
    experts = router_weight.shape[1]
    top = routes.shape[1]
    tok = rows_here * width
    blocks = lax.axis_size("exp")
    shards = blocks // experts
    slots = blocks * CAP
    me = lax.axis_index("exp")
    mine = me // shards
    column = lax.axis_index("rep") * half

    cells = latent.transpose(1, 0, 2).reshape(channels, tok)
    routes_t = routes.T
    payload = jnp.concatenate([cells, routes_t.astype(BF16)], axis=0)
    image = exchange(jnp.broadcast_to(payload[None], (blocks,) + payload.shape))

    gain_here = lax.dynamic_slice_in_dim(norm_gain, column, half)
    stem_here = lax.dynamic_slice_in_dim(stem_weight, column, half, 1)
    router_here = lax.dynamic_slice_in_dim(router_weight, column, half, 0).astype(F32)
    cot = lax.dynamic_slice_in_dim(grad_mixed, column, half, 1)
    experts_range = jnp.arange(experts, dtype=jnp.int32)
    own_named = jnp.any(routes_t[None] == experts_range[:, None, None], axis=1)
    own_sel = selection(own_named)
    cot_slots = dot(own_sel.reshape(experts * CAP, tok), cot, ((1,), (0,))).astype(BF16)
    cot_slots = jnp.repeat(cot_slots.reshape(experts, CAP, half), shards, axis=0)
    slot_cot = exchange(cot_slots).reshape(slots, half)

    lat_all = image[:, :channels].transpose(1, 0, 2).reshape(channels, blocks * tok)
    routes_all = image[:, channels:].astype(jnp.int32)
    sel = selection(jnp.any(routes_all == mine, axis=1))
    patches = patches_of(lat_all, width)
    slot_patches = dot(
        sel, patches.reshape(-1, blocks, tok), ((2,), (2,)), ((0,), (1,))
    ).astype(BF16)
    stem = dot(slot_patches.reshape(slots, -1), stem_weight, ((1,), (0,))).astype(BF16)
    value = stem.astype(F32)
    scale = lax.rsqrt(jnp.mean(value * value, axis=-1, keepdims=True) + 1e-06)
    normed = (value * scale * norm_gain).astype(BF16)
    logits = dot(normed, router_weight, ((1,), (0,)))
    other = (jnp.sum(routes_all, axis=1) - mine).astype(BF16)
    slot_other = dot(sel, other, ((2,), (1,)), ((0,), (0,))).astype(jnp.int32).reshape(slots, 1)
    is_mine = (experts_range == mine)[None, :].astype(F32)
    is_other = (experts_range[None, :] == slot_other).astype(F32)
    sig_mine = jax.nn.sigmoid(jnp.sum(logits * is_mine, axis=1, keepdims=True))
    sig_other = jax.nn.sigmoid(jnp.sum(logits * is_other, axis=1, keepdims=True))
    gate = sig_mine / (sig_mine + sig_other)
    rest = sig_other / (sig_mine + sig_other)
    normed_here = lax.dynamic_slice_in_dim(normed, column, half, 1)
    value_here = lax.dynamic_slice_in_dim(stem, column, half, 1).astype(F32)
    stem_back = dot(stem, stem_weight, ((1,), (1,)))

    pre_gate = core_sum(dot(normed_here, gate_weight, ((1,), (0,))))
    pre_up = core_sum(dot(normed_here, up_weight, ((1,), (0,))))
    sigma = jax.nn.sigmoid(pre_gate)
    hidden = (pre_gate * sigma * pre_up).astype(BF16)
    part = dot(hidden, down_weight, ((1,), (0,)))
    returned = exchange((gate * part).astype(BF16).reshape(blocks, CAP, half))

    slot_grad = (gate * slot_cot.astype(F32)).astype(BF16)
    grad_hidden = core_sum(dot(slot_grad, down_weight, ((1,), (1,))))
    grad_gate_pre = (grad_hidden * pre_up * sigma * (1.0 + pre_gate * (1.0 - sigma))).astype(BF16)
    grad_up_pre = (grad_hidden * pre_gate * sigma).astype(BF16)
    back = dot(grad_gate_pre, gate_weight, ((1,), (1,)))
    back = back + dot(grad_up_pre, up_weight, ((1,), (1,)))

    grad_gates = core_sum(jnp.sum(slot_cot.astype(F32) * part, axis=1), F32)[:, None]
    to_mine = grad_gates * gate * rest * (1.0 - sig_mine)
    to_other = -grad_gates * gate * rest * (1.0 - sig_other)
    grad_logits = to_mine * is_mine + to_other * is_other
    grad_normed = back + lax.dot_general(
        grad_logits, router_here, (((1,), (1,)), ((), ())), precision=lax.Precision.HIGHEST
    )
    scaled = gain_here * grad_normed
    along = jnp.sum(value_here * scaled, axis=1, keepdims=True) * scale**3 / model_width
    projected = dot((scale * scaled).astype(BF16), stem_here, ((1,), (1,))) - along * stem_back
    terms = dot(
        projected.astype(BF16).reshape(blocks, CAP, -1), sel, ((1,), (1,)), ((0,), (0,))
    )
    own_terms = dot(stem_here, cot, ((1,), (1,)))
    here = (jnp.arange(blocks, dtype=jnp.int32) == me).astype(F32)[:, None, None]
    terms = (terms + here * own_terms).transpose(1, 0, 2).reshape(-1, blocks * tok)
    lat_terms = patches_sum(terms, width).reshape(channels, blocks, tok).transpose(1, 0, 2)
    lat_sum = jnp.sum(exchange(lat_terms), axis=0)
    lat_sum = core_sum(lat_sum, F32)
    grad_latent = lat_sum.reshape(channels, rows_here, width).transpose(1, 0, 2)

    grad_gate = dot(normed_here, grad_gate_pre, ((0,), (0,)))
    grad_up = dot(normed_here, grad_up_pre, ((0,), (0,)))
    grad_down = dot(hidden, slot_grad, ((0,), (0,)))

    own_patches = lax.dynamic_slice_in_dim(patches, me * tok, tok, 1)
    own_stem = dot(own_patches, stem_here, ((0,), (0,))).astype(BF16).astype(F32)
    taken = jnp.repeat(own_sel, shards, axis=0).reshape(slots, tok)
    mixed = own_stem + dot(taken, returned.reshape(slots, half), ((0,), (0,)))
    mixed = core_join(mixed.astype(BF16))
    return (mixed, grad_latent, grad_gate, grad_up, grad_down)


def solution(mesh):
    return jax.shard_map(
        local,
        mesh=mesh,
        in_specs=(
            P("exp", None, None),
            P(),
            P(),
            P(),
            P("exp", None),
            P("rep", "exp"),
            P("rep", "exp"),
            P("exp", "rep"),
            P("exp", None),
        ),
        out_specs=(
            P("exp", None),
            P("exp", None, None),
            P("rep", "exp"),
            P("rep", "exp"),
            P("exp", "rep"),
        ),
        check_vma=False,
    )
```

```python
import functools

import jax
import jax.numpy as jnp
from jax import lax
from jax.experimental import pallas as pl
from jax.experimental.pallas import tpu as pltpu
from jax.sharding import PartitionSpec as P

CAP = 40
LANES = 128
GROUP = 16
F32 = jnp.float32
BF16 = jnp.bfloat16
MIB = 1024 * 1024


def dot(a, b, contract, batch=((), ())):
    return lax.dot_general(a, b, (contract, batch), preferred_element_type=F32)


def mm(a, b):
    return dot(a, b, ((1,), (0,)))


def mm_t(a, b):
    return dot(a, b, ((1,), (1,)))


def t_mm(a, b):
    return dot(a, b, ((0,), (0,)))


def call(kernel, flops, moved, mib=12, **kw):
    return pl.pallas_call(
        kernel,
        compiler_params=pltpu.CompilerParams(vmem_limit_bytes=mib * MIB),
        cost_estimate=pl.CostEstimate(flops=flops, bytes_accessed=moved, transcendentals=0),
        **kw,
    )


def whole(shape):
    return pl.BlockSpec(shape, lambda *_: (0,) * len(shape))


def rows(count, columns, at=0):
    return pl.BlockSpec((count, columns), lambda g, *_: (g, at))


def shape_of(shape, dtype):
    return jax.ShapeDtypeStruct(shape, dtype)


def lane_column(shape, width):
    return lax.broadcasted_iota(jnp.int32, shape, 1) % width


def shifted(window, shift, start, count):
    size = window.shape[1]
    return pltpu.roll(window, (-shift) % size, 1)[:, start : start + count]


def other_core(values):
    return lax.ppermute(values, "rep", [(0, 1), (1, 0)])


def other_shard(values):
    return lax.ppermute(values, "exp", [(i, i ^ 1) for i in range(lax.axis_size("exp"))])


def exchange(values):
    count = lax.axis_size("exp")
    shards = count // values.shape[0]
    groups = None
    if shards > 1:
        groups = [[s + shards * e for e in range(values.shape[0])] for s in range(shards)]
    return lax.all_to_all(
        values, "exp", split_axis=0, concat_axis=0, tiled=True, axis_index_groups=groups
    )


def hbm():
    return pl.BlockSpec(memory_space=pl.ANY)


def vmem():
    return pl.BlockSpec(memory_space=pltpu.VMEM)


def fast(shape, dtype):
    return pltpu.VMEM(shape, dtype)


def near(values):
    return pltpu.with_memory_space_constraint(values, pltpu.VMEM)


def far_off(values):
    return pltpu.with_memory_space_constraint(values, pltpu.HBM)


def kernel_call(kernel, flops, moved, operands, outs, name, mib=12, place=None, steps=1, scratch=(), specs=None, out_specs=None):
    specs = specs or [vmem() for _ in operands]
    out_specs = out_specs or [vmem() for _ in outs]
    return call(
        kernel,
        flops,
        moved,
        mib,
        grid_spec=pltpu.PrefetchScalarGridSpec(
            num_scalar_prefetch=0 if place is None else 1,
            grid=(steps,),
            in_specs=specs,
            out_specs=out_specs,
            scratch_shapes=list(scratch),
        ),
        out_shape=outs,
        name=name,
    )(*(() if place is None else (place,)), *operands)


def tiles_of(columns):
    return -(-columns // LANES)


def stacked(values):
    columns = values.shape[1]
    spare = tiles_of(columns) * LANES - columns
    if spare:
        values = jnp.concatenate([values, jnp.zeros((values.shape[0], spare), F32)], axis=1)
    parts = [values[:, k * LANES : (k + 1) * LANES] for k in range(tiles_of(columns))]
    return jnp.concatenate(parts, axis=0)


def pack_kernel(shards, half, place_ref, latent_ref, routes_ref, cot_ref, out_ref, taken_ref, here_ref):
    rows_here, channels, width = latent_ref.shape
    tok = rows_here * width
    experts = out_ref.shape[0] // shards
    cells = jnp.concatenate([latent_ref[r].astype(F32) for r in range(rows_here)], axis=1)
    routes = routes_ref[...].astype(F32)
    payload = jnp.concatenate([cells, routes], axis=0)
    cot = cot_ref[...]
    if cot.shape[1] != half:
        cot = jnp.where(place_ref[2] == 0, cot[:, :half], cot[:, half:])
    here_ref[...] = cot
    expert = lax.broadcasted_iota(jnp.int32, (experts, tok), 0).astype(F32)
    named = jnp.where((expert == routes[0:1]) | (expert == routes[1:2]), 1.0, 0.0)
    first = lax.broadcasted_iota(jnp.int32, (tok, tok), 0)
    second = lax.broadcasted_iota(jnp.int32, (tok, tok), 1)
    before = jnp.where(first <= second, 1.0, 0.0).astype(BF16)
    at = mm(named.astype(BF16), before) - 1.0
    slot = lax.broadcasted_iota(jnp.int32, (CAP, tok), 0).astype(F32)
    sel = [
        jnp.where((at[e : e + 1] == slot) & (named[e : e + 1] > 0.0), 1.0, 0.0)
        for e in range(experts)
    ]
    cots = mm(jnp.concatenate(sel, axis=0).astype(BF16), cot)
    taken_ref[...] = jnp.concatenate([one for one in sel for _ in range(shards)], axis=0).astype(BF16)
    for e in range(experts):
        slots = stacked(cots[e * CAP : (e + 1) * CAP])
        packed = jnp.concatenate([slots, payload], axis=0).astype(BF16)
        for n in range(shards):
            out_ref[e * shards + n] = packed


def pack(place, latent, routes_t, cot, experts, shards, half):
    rows_here, channels, width = latent.shape
    top, tok = routes_t.shape
    blocks = experts * shards
    depth = tiles_of(half) * CAP + channels + top
    operands = [latent, routes_t, cot]
    return kernel_call(
        functools.partial(pack_kernel, shards, half),
        2 * blocks * CAP * tok * half,
        4 * blocks * depth * LANES,
        [far_off(a) for a in operands],
        [
            shape_of((blocks, depth, LANES), BF16),
            pltpu.HBM((blocks * CAP, tok), BF16),
            pltpu.HBM((tok, half), BF16),
        ],
        "pack",
        place=place,
        specs=[whole(a.shape) for a in operands],
        out_specs=[
            whole((blocks, depth, LANES)),
            whole((blocks * CAP, tok)),
            whole((tok, half)),
        ],
    )


def unpacked(ref, columns):
    tiles = tiles_of(columns)
    blocks = ref.shape[0]
    held = [ref[b, : tiles * CAP, :].astype(F32) for b in range(blocks)]
    parts = [
        jnp.concatenate([one[k * CAP : (k + 1) * CAP] for one in held], axis=0)
        for k in range(tiles)
    ]
    return jnp.concatenate(parts, axis=1)[:, :columns]


def unpack_kernel(packed_ref, cot_ref, image_ref):
    cot_ref[...] = unpacked(packed_ref, cot_ref.shape[1]).astype(BF16)
    top = packed_ref.shape[1] - image_ref.shape[1]
    for b in range(packed_ref.shape[0]):
        image_ref[b] = packed_ref[b, top:, :]


def unpack(packed, half, lines):
    blocks, _, tok = packed.shape
    return kernel_call(
        unpack_kernel,
        0,
        4 * packed.size,
        [near(packed)],
        [fast((blocks * CAP, half), BF16), fast((blocks, lines, tok), BF16)],
        "unpack",
    )


def weave_kernel(place_ref, same_ref, other_ref, after_ref, out_ref):
    even = (place_ref[1] & 1) == 0
    for e in range(same_ref.shape[0]):
        same, other = same_ref[e], other_ref[e]
        out_ref[2 * e] = jnp.where(even, same, other)
        out_ref[2 * e + 1] = jnp.where(even, other, same)


def weave(place, same, other, after):
    shape = (2 * same.shape[0],) + same.shape[1:]
    return kernel_call(
        weave_kernel,
        0,
        8 * same.size,
        [near(same), near(other), near(after)],
        [fast(shape, same.dtype)],
        "weave",
        place=place,
    )[0]


def sum_kernel(a_ref, b_ref, out_ref):
    out_ref[...] = (a_ref[...].astype(F32) + b_ref[...].astype(F32)).astype(out_ref.dtype)


def add_up(a, b):
    return kernel_call(
        sum_kernel, a.size, 6 * a.size, [near(a), near(b)], [fast(a.shape, a.dtype)], "add_up"
    )[0]


def pack_back_kernel(paired, place_ref, a_ref, b_ref, c_ref, terms_ref, out_ref):
    total = a_ref[...].astype(F32) + b_ref[...].astype(F32)
    if paired:
        total = total + c_ref[...].astype(F32)
    side = place_ref[1] & 1
    for b in range(out_ref.shape[0]):
        slots = stacked(total[b * CAP : (b + 1) * CAP])
        if paired:
            terms = [terms_ref[2 * b + side], terms_ref[2 * b + 1 - side]]
        else:
            terms = [terms_ref[b]]
        out_ref[b] = jnp.concatenate([slots] + terms, axis=0).astype(BF16)


def pack_back(place, a, b, c, terms, paired):
    blocks, channels, tok = terms.shape
    depth = tiles_of(a.shape[1]) * CAP + channels
    if paired:
        blocks, depth = blocks // 2, depth + channels
    return kernel_call(
        functools.partial(pack_back_kernel, paired),
        a.size,
        8 * a.size,
        [near(a), near(b), near(c), near(terms)],
        [shape_of((blocks, depth, LANES), BF16)],
        "pack_back",
        place=place,
    )[0]


PIECES = 4


def pieces(source, target, sem, at=0):
    deep = source.shape[0] // PIECES
    bands = [pl.ds(k * deep, deep) for k in range(PIECES)]
    return [
        pltpu.make_async_copy(source.at[band, :], target.at[band, :], sem.at[at + k])
        for k, band in enumerate(bands)
    ]


def far_kernel(place_ref, gate_ref, up_ref, down_ref, gate_out, up_out, down_out, sem):
    size = gate_out.shape[1]
    at = pl.multiple_of((1 - place_ref[2]) * size, LANES)
    copies = (
        pieces(gate_ref.at[:, pl.ds(at, size)], gate_out, sem)
        + pieces(up_ref.at[:, pl.ds(at, size)], up_out, sem, PIECES)
        + pieces(down_ref.at[pl.ds(at, size), :], down_out, sem, 2 * PIECES)
    )
    for copy in copies:
        copy.start()
    for copy in copies:
        copy.wait()


def far_weights(place, gate, up, down):
    half, hid = gate.shape
    size = hid // 2
    return kernel_call(
        far_kernel,
        0,
        LANES,
        [far_off(gate), far_off(up), far_off(down)],
        [fast((half, size), BF16), fast((half, size), BF16), fast((size, half), BF16)],
        "far_weights",
        place=place,
        specs=[hbm()] * 3,
        scratch=[pltpu.SemaphoreType.DMA((3 * PIECES,))],
    )


def cuts(lengths):
    start, out = 0, []
    for n in lengths:
        out.append((start, n))
        start += n
    return out


def weights_kernel(parts, experts, place_ref, *refs):
    weights = refs[: 3 * parts]
    stem_in, gain_in, router_in = refs[3 * parts : 3 * parts + 3]
    inner, outer, stem, gain, sem = refs[3 * parts + 3 :]
    gates, ups, downs = weights[:parts], weights[parts : 2 * parts], weights[2 * parts :]
    size = outer.shape[0]
    copies = []

    def copy(source, target):
        copies.extend(pieces(source, target, sem, len(copies)))

    for n, refs_of in enumerate((gates, ups)):
        for ref, (a, depth) in zip(refs_of, cuts([r.shape[0] for r in refs_of])):
            if ref.shape[1] != size:
                ref = ref.at[:, pl.ds(pl.multiple_of(place_ref[2] * size, LANES), size)]
            copy(ref, inner.at[pl.ds(a, depth), pl.ds(n * size, size)])
    for ref, (a, depth) in zip(downs, cuts([r.shape[1] for r in downs])):
        if ref.shape[0] != size:
            ref = ref.at[pl.ds(pl.multiple_of(place_ref[2] * size, LANES), size), :]
        copy(ref, outer.at[:, pl.ds(a, depth)])
    for one in copies:
        one.start()
    wide = router_in[...].astype(F32)
    model = wide.shape[0]
    blank = jnp.zeros((model, LANES - 2 * experts), F32)
    wide = jnp.concatenate([wide, wide, blank], axis=1)
    values, gains = stem_in[...], gain_in[...]
    if parts == 2:
        half = model // 2
        first = place_ref[2] == 0
        wide = jnp.where(first, wide, jnp.concatenate([wide[half:], wide[:half]], axis=0))
        turned = jnp.concatenate([values[:, half:], values[:, :half]], axis=1)
        values = jnp.where(first, values, turned)
        turned = jnp.concatenate([gains[:, half:], gains[:, :half]], axis=1)
        gains = jnp.where(first, gains, turned)
    stem[...] = values
    gain[...] = gains
    inner[:, 2 * size :] = wide.astype(BF16)
    for one in copies:
        one.wait()


def gather_weights(place, stem, gain, router, gate_parts, up_parts, down_parts):
    parts = len(gate_parts)
    model, experts = router.shape
    size = down_parts[-1].shape[0]
    weights = [far_off(w) for p in (gate_parts, up_parts, down_parts) for w in p]
    small = [far_off(stem), far_off(gain), far_off(router)]
    return kernel_call(
        functools.partial(weights_kernel, parts, experts),
        100_000_000_000,
        12 * model * size,
        weights + small,
        [
            fast((model, 2 * size + LANES), BF16),
            fast((size, model), BF16),
            fast(stem.shape, BF16),
            fast(gain.shape, F32),
        ],
        "gather_weights",
        place=place,
        specs=[hbm()] * (3 * parts) + [whole(a.shape) for a in small],
        scratch=[pltpu.SemaphoreType.DMA((3 * parts * PIECES,))],
    )


def join_kernel(place_ref, own_ref, away_ref, a_ref, b_ref, out_ref, latent_ref):
    half = own_ref.shape[1]
    first = place_ref[2] == 0
    own, away = own_ref[...], away_ref[...]
    out_ref[:, :half] = jnp.where(first, own, away)
    out_ref[:, half:] = jnp.where(first, away, own)
    total = a_ref[...] + b_ref[...]
    width = latent_ref.shape[2]
    for r in range(latent_ref.shape[0]):
        latent_ref[r] = total[:, r * width : (r + 1) * width]


def join(place, own, away, a, b, rows_here):
    count, half = own.shape
    channels, tok = a.shape
    return kernel_call(
        join_kernel,
        0,
        8 * count * half,
        [near(own), near(away), near(a), near(b)],
        [
            shape_of((count, 2 * half), BF16),
            shape_of((rows_here, channels, tok // rows_here), F32),
        ],
        "join",
        place=place,
    )


def pair_selection(named):
    lanes = named.shape[1]
    tok = lanes // 2
    first = lax.broadcasted_iota(jnp.int32, (lanes, lanes), 0)
    second = lax.broadcasted_iota(jnp.int32, (lanes, lanes), 1)
    before = ((first <= second) & (first // tok == second // tok)).astype(F32).astype(BF16)
    wide = jnp.broadcast_to(named, (8, lanes)).astype(BF16)
    place = mm(wide, before)[:1]
    lane = lax.broadcasted_iota(jnp.int32, (1, lanes), 1)
    place = place - 1.0 + jnp.where(lane >= tok, float(CAP), 0.0)
    slot = lax.broadcasted_iota(jnp.int32, (2 * CAP, lanes), 0).astype(F32)
    return jnp.where((place == slot) & (named > 0.0), 1.0, 0.0)


def pair_patches(image_ref, top, first, width, channels):
    blocks = image_ref.shape[0]
    before = image_ref[jnp.maximum(first - 1, 0), top : top + channels, :].astype(F32)
    after = image_ref[jnp.minimum(first + 2, blocks - 1), top : top + channels, :].astype(F32)
    window = jnp.concatenate(
        [
            jnp.where(first > 0, before, 0.0),
            image_ref[first, top : top + channels, :].astype(F32),
            image_ref[first + 1, top : top + channels, :].astype(F32),
            jnp.where(first + 2 < blocks, after, 0.0),
        ],
        axis=1,
    )
    tok = image_ref.shape[2]
    column = lane_column((channels, 2 * tok), width)
    pieces = []
    for i in range(3):
        for j in range(3):
            piece = shifted(window, (i - 1) * width + j - 1, tok, 2 * tok)
            source = column + (j - 1)
            pieces.append(jnp.where((source >= 0) & (source < width), piece, 0.0))
    return jnp.concatenate(pieces, axis=0)


def by_side(pairs, even):
    same = [jnp.where(even, p[:CAP], p[CAP:]) for p in pairs]
    other = [jnp.where(even, p[CAP:], p[:CAP]) for p in pairs]
    return same + other


def forward_kernel(
    paired, width, experts, outs, place_ref, image_ref, stem_ref, gain_ref, inner, outer,
    saved_ref, own_out, normed_ref, value_ref, meta_ref, coef_ref, sel_ref, pg_ref, pu_ref, *refs,
):
    out_refs, (own_ref, save_sem) = refs[:-2], refs[-2:]
    step = pl.program_id(0)
    size = outer.shape[0]
    chunk = GROUP * CAP
    here = pl.ds(pl.multiple_of(step * chunk, chunk), chunk)
    top = 0
    channels = image_ref.shape[1] - 2
    mine = place_ref[0].astype(F32)
    even = (place_ref[1] & 1) == 0
    taken, others = [], []
    for q in range(GROUP // 2):
        first = step * GROUP + 2 * q
        lines = [image_ref[first + n, top + channels :, :].astype(F32) for n in range(2)]
        named_by = [jnp.concatenate([line[k : k + 1] for line in lines], axis=1) for k in range(2)]
        named = jnp.where((named_by[0] == mine) | (named_by[1] == mine), 1.0, 0.0)
        sel = pair_selection(named)
        sel_ref[step * (GROUP // 2) + q] = sel.astype(BF16)
        other = named_by[0] + named_by[1] - mine
        others.append(jnp.sum(sel * other, axis=1, keepdims=True))
        patches = pair_patches(image_ref, top, first, width, channels)
        taken.append(mm_t(sel.astype(BF16), patches.astype(BF16)))
    if paired:
        taken, others = by_side(taken, even), by_side(others, even)
    patches = jnp.concatenate(taken, axis=0).astype(BF16)
    other = jnp.concatenate(others, axis=0)
    stem = mm(patches, stem_ref[...]).astype(BF16)
    value_ref[here, :] = stem
    value = stem.astype(F32)
    scale = lax.rsqrt(jnp.mean(value * value, axis=-1, keepdims=True) + 1e-06)
    normed = (value * scale * gain_ref[...]).astype(BF16)
    normed_ref[...] = normed
    save = pltpu.make_async_copy(normed_ref, saved_ref.at[here, :], save_sem.at[0])
    save.start()
    own_save = pltpu.make_async_copy(own_ref, own_out, save_sem.at[1])

    @pl.when(step == 0)
    def _():
        me = place_ref[1]
        first = me // 2 * 2
        tok = image_ref.shape[2]
        own = pair_patches(image_ref, top, first, width, channels)
        own = jnp.where(me == first, own[:, :tok], own[:, tok:]).astype(BF16)
        own_ref[...] = t_mm(own, stem_ref[:, : own_ref.shape[1]]).astype(BF16)
        own_save.start()

    logits = mm(normed, inner[:, 2 * size :])
    lane = lax.broadcasted_iota(jnp.int32, logits.shape, 1)
    again = jnp.where(lane >= experts, lane - experts, lane).astype(F32)
    lane = lane.astype(F32)
    sig_mine = jax.nn.sigmoid(jnp.sum(jnp.where(lane == mine, logits, 0.0), axis=1, keepdims=True))
    sig_other = jax.nn.sigmoid(jnp.sum(jnp.where(lane == other, logits, 0.0), axis=1, keepdims=True))
    gate = sig_mine / (sig_mine + sig_other)
    rest = sig_other / (sig_mine + sig_other)
    both = gate * rest
    coef_ref[here, :] = jnp.where(again == mine, both * (1.0 - sig_mine), 0.0) - jnp.where(
        again == other, both * (1.0 - sig_other), 0.0
    )
    meta_ref[here, :] = jnp.where(lane == 0.0, gate, scale)
    pre_gate = mm(normed, inner[:, :size])
    pre_up = mm(normed, inner[:, size : 2 * size])
    pg_ref[here, :] = pre_gate.astype(BF16)
    pu_ref[here, :] = pre_up.astype(BF16)
    hidden = (pre_gate * jax.nn.sigmoid(pre_gate) * pre_up).astype(BF16)
    part, at = None, None
    for ref, (a, n, b, m) in zip(out_refs, outs):
        if (b, m) != at:
            part, at = gate * mm(hidden, outer[:, b : b + m]), (b, m)
        if n == chunk:
            ref[here, :] = part.astype(BF16)
        else:
            ref[...] = part[a : a + n].astype(BF16)
    save.wait()

    @pl.when(step == 0)
    def _():
        own_save.wait()


def forward(place, image, stem, gain, inner, outer, half, outs, paired, width, experts):
    blocks, _, tok = image.shape
    slots, chunk = blocks * CAP, GROUP * CAP
    model, size = stem.shape[1], outer.shape[0]
    return kernel_call(
        functools.partial(forward_kernel, paired, width, experts, outs),
        2 * slots * model * size * 4,
        slots * (6 * model + 6 * size) + 6 * model * size,
        [near(a) for a in (image, stem, gain, inner, outer)],
        [
            pltpu.HBM((slots, model), BF16),
            pltpu.HBM((tok, half), BF16),
            fast((chunk, model), BF16),
            fast((slots, model), BF16),
            fast((slots, LANES), F32),
            fast((slots, LANES), F32),
            fast((blocks // 2, 2 * CAP, 2 * tok), BF16),
            fast((slots, size), BF16),
            fast((slots, size), BF16),
        ]
        + [fast((slots if n == chunk else n, m), BF16) for _, n, _, m in outs],
        "forward",
        mib=18,
        place=place,
        steps=blocks // GROUP,
        out_specs=[hbm()] * 2 + [vmem()] * (7 + len(outs)),
        scratch=[pltpu.VMEM((tok, half), BF16), pltpu.SemaphoreType.DMA((2,))],
    )


def backward_kernel(
    parts, bands, experts, stem_ref, gain_ref, inner, outer, value_ref, meta_ref, coef_ref, pg_ref, pu_ref,
    *refs,
):
    cot_refs, refs = refs[: parts * bands], refs[parts * bands :]
    saved, refs = refs[: 3 + parts], refs[3 + parts :]
    proj_ref, ggp_ref, gup_ref, hg_ref, sem = refs
    step = pl.program_id(0)
    model = stem_ref.shape[1]
    chunk = GROUP * CAP
    here = pl.ds(pl.multiple_of(step * chunk, chunk), chunk)
    sources = [ggp_ref, gup_ref, hg_ref]
    targets = [ref.at[here, :] for ref in saved[:3]]
    for n, ref in enumerate(cot_refs):
        if bands == 1:
            sources.append(ref.at[here, :])
            targets.append(saved[3 + n].at[here, :])
        else:
            deep = ref.shape[0]
            sources.append(ref)
            targets.append(saved[3 + n // bands].at[pl.ds(n % bands * deep, deep), :])
    saves = [
        pltpu.make_async_copy(a, b, sem.at[n]) for n, (a, b) in enumerate(zip(sources, targets))
    ]
    for save in saves[3:]:
        save.start()
    gate = meta_ref[here, 0:1]
    scale = meta_ref[here, 1:2]
    raw = 0.0
    for k, (a, n) in enumerate(cuts([r.shape[1] for r in cot_refs[::bands]])):
        if bands == 1:
            cot = cot_refs[k][here, :]
        else:
            cot = jnp.concatenate([r[...] for r in cot_refs[k * bands : (k + 1) * bands]], axis=0)
        raw = raw + mm_t(cot, outer[:, a : a + n])
    pre_gate = pg_ref[here, :].astype(F32)
    pre_up = pu_ref[here, :].astype(F32)
    sigma = jax.nn.sigmoid(pre_gate)
    silu = pre_gate * sigma
    hidden = silu * pre_up
    grad_gates = jnp.sum(raw * hidden, axis=1, keepdims=True)
    hg_ref[...] = (gate * hidden).astype(BF16)
    grad_hidden = gate * raw
    ggp = (grad_hidden * pre_up * sigma * (1.0 + pre_gate - silu)).astype(BF16)
    gup = (grad_hidden * silu).astype(BF16)
    ggp_ref[...] = ggp
    gup_ref[...] = gup
    for save in saves[:3]:
        save.start()
    grad_logits = grad_gates * coef_ref[here, :]
    high = grad_logits.astype(BF16)
    low = (grad_logits - high.astype(F32)).astype(BF16)
    lane = lax.broadcasted_iota(jnp.int32, grad_logits.shape, 1)
    mix = jnp.where(lane < experts, high.astype(F32), low.astype(F32)).astype(BF16)
    back = mm_t(jnp.concatenate([ggp, gup, mix], axis=1), inner[...]) * gain_ref[...]
    value = value_ref[here, :].astype(F32)
    along = jnp.sum(back * value, axis=1, keepdims=True) * (scale * scale * scale) / model
    grad = (scale * back - along * value).astype(BF16)
    proj_ref[here, :] = mm_t(grad, stem_ref[...]).astype(BF16)
    for save in saves:
        save.wait()


def backward(stem, gain, inner, outer, acts, cots, experts):
    slots, model = acts[0].shape
    size, chunk = outer.shape[0], GROUP * CAP
    taps = stem.shape[0]
    parts, bands = len(cots), len(cots[0])
    operands = [stem, gain, inner, outer] + list(acts) + [c for part in cots for c in part]
    return kernel_call(
        functools.partial(backward_kernel, parts, bands, experts),
        2 * slots * model * size * 4,
        slots * (4 * model + 12 * size) + 6 * model * size,
        [near(a) for a in operands],
        [pltpu.HBM((slots, size), BF16)] * 3
        + [pltpu.HBM((slots, part[0].shape[1]), BF16) for part in cots]
        + [fast((slots, taps), BF16)],
        "backward",
        mib=20,
        steps=slots // chunk,
        out_specs=[hbm()] * (3 + parts) + [vmem()],
        scratch=[pltpu.VMEM((chunk, size), BF16)] * 3
        + [pltpu.SemaphoreType.DMA((3 + parts * bands,))],
    )


def image_kernel(paired, width, place_ref, proj_ref, sel_ref, stem_ref, cot_ref, out_ref, terms):
    pairs = sel_ref.shape[0]
    tok = cot_ref.shape[0]
    channels = out_ref.shape[1]
    count = 2 * pairs * tok
    own = mm_t(stem_ref[:, : cot_ref.shape[1]], cot_ref[...])
    me = place_ref[1]
    even = (me & 1) == 0
    proj = proj_ref[...].astype(F32)
    for q in range(pairs):
        if paired:
            same = proj[CAP * q : CAP * (q + 1)]
            other = proj[CAP * (pairs + q) : CAP * (pairs + q + 1)]
            both = [jnp.where(even, same, other), jnp.where(even, other, same)]
            pair = jnp.concatenate(both, axis=0)
        else:
            pair = proj[2 * CAP * q : 2 * CAP * (q + 1)]
        block = t_mm(pair.astype(BF16), sel_ref[q])
        terms[:, 2 * q * tok : (2 * q + 1) * tok] = block[:, :tok] + jnp.where(2 * q == me, own, 0.0)
        terms[:, (2 * q + 1) * tok : (2 * q + 2) * tok] = block[:, tok:] + jnp.where(
            2 * q + 1 == me, own, 0.0
        )
    lane = lax.broadcasted_iota(jnp.int32, (channels, count), 1)
    total = jnp.zeros((channels, count), F32)
    for i in range(3):
        for j in range(3):
            k = (3 * i + j) * channels
            shift = (i - 1) * width + j - 1
            piece = pltpu.roll(terms[k : k + channels, :], shift % count, 1)
            column = lane % width + (1 - j)
            token = lane - shift
            keep = (column >= 0) & (column < width) & (token >= 0) & (token < count)
            total = total + jnp.where(keep, piece, 0.0)
    for b in range(2 * pairs):
        out_ref[b] = total[:, b * tok : (b + 1) * tok]


def to_image(place, proj, sel, stem, cot, paired, width, channels):
    pairs = sel.shape[0]
    blocks, tok = 2 * pairs, cot.shape[0]
    taps, half = stem.shape[0], cot.shape[1]
    return kernel_call(
        functools.partial(image_kernel, paired, width),
        2 * proj.shape[0] * 2 * tok * taps,
        4 * taps * blocks * tok,
        [near(a) for a in (proj, sel, stem, cot)],
        [fast((blocks, channels, tok), F32)],
        "to_image",
        place=place,
        scratch=[pltpu.VMEM((taps, blocks * tok), F32)],
    )[0]


def far_grads_kernel(normed, ggp, gup, hg, near_cot, cot, after, gate_out, up_out, down_out, *refs):
    near_v, ggp_v, gup_v, hg_v, near_cot_v, far_v, cot_v, sem = refs
    half = cot.shape[1]
    sources = (normed.at[:, pl.ds(half, half)], ggp, gup, hg, cot, normed.at[:, pl.ds(0, half)], near_cot)
    targets = (far_v, ggp_v, gup_v, hg_v, cot_v, near_v, near_cot_v)
    loads = [pltpu.make_async_copy(a, b, sem.at[n]) for n, (a, b) in enumerate(zip(sources, targets))]
    for load in loads:
        load.start()
    for load in loads[:2]:
        load.wait()
    gate_out[...] = t_mm(far_v[...], ggp_v[...]).astype(BF16)
    loads[2].wait()
    up_out[...] = t_mm(far_v[...], gup_v[...]).astype(BF16)
    loads[3].wait()
    loads[4].wait()
    down_out[...] = t_mm(hg_v[...], cot_v[...]).astype(BF16)
    loads[5].wait()
    loads[6].wait()


def far_grads(normed, ggp, gup, hg, near_cot, cot, after):
    slots, size = ggp.shape
    half = cot.shape[1]
    held = [(slots, half), (slots, size), (slots, size), (slots, size), (slots, half)]
    return kernel_call(
        far_grads_kernel,
        0,
        LANES,
        [far_off(a) for a in (normed, ggp, gup, hg, near_cot, cot)] + [after],
        [fast((half, size), BF16)] * 2
        + [fast((size, half), BF16)]
        + [fast(shape, BF16) for shape in held],
        "far_grads",
        specs=[hbm()] * 7,
        scratch=[
            pltpu.VMEM((slots, half), BF16),
            pltpu.VMEM((slots, half), BF16),
            pltpu.SemaphoreType.DMA((7,)),
        ],
    )


def near_grads_kernel(
    place_ref, normed, ggp, gup, hg, cot, gate_out, up_out, down_out, done_ref, own, own_sem
):
    size = ggp.shape[1]
    here = pl.multiple_of(place_ref[2] * size, LANES)
    places = (
        gate_out.at[:, pl.ds(here, size)],
        up_out.at[:, pl.ds(here, size)],
        down_out.at[pl.ds(here, size), :],
    )
    results = [pieces(own.at[n], a, own_sem, n * PIECES) for n, a in enumerate(places)]
    done_ref[...] = jnp.zeros(done_ref.shape, F32)
    for n, (left, right) in enumerate(((normed, ggp), (normed, gup), (hg, cot))):
        own[n] = t_mm(left[...], right[...])
        for copy in results[n]:
            copy.start()
    for copy in results[0] + results[1] + results[2]:
        copy.wait()


def near_grads(place, normed, ggp, gup, hg, cot):
    slots, size = ggp.shape
    half = cot.shape[1]
    return kernel_call(
        near_grads_kernel,
        100_000_000_000,
        LANES,
        [near(a) for a in (normed, ggp, gup, hg, cot)],
        [pltpu.HBM((half, 2 * size), F32)] * 2
        + [pltpu.HBM((2 * size, half), F32), fast((8, LANES), F32)],
        "near_grads",
        mib=14,
        place=place,
        out_specs=[hbm()] * 3 + [vmem()],
        scratch=[pltpu.VMEM((3, half, size), F32), pltpu.SemaphoreType.DMA((3 * PIECES,))],
    )


def fill_kernel(
    place_ref, gate_in, up_in, down_in, gate_old, up_old, down_old, gate_out, up_out, down_out, wide, sem
):
    size = gate_in.shape[1]
    there = pl.multiple_of((1 - place_ref[2]) * size, LANES)
    places = (
        gate_out.at[:, pl.ds(there, size)],
        up_out.at[:, pl.ds(there, size)],
        down_out.at[pl.ds(there, size), :],
    )
    results = [pieces(wide.at[n], a, sem, n * PIECES) for n, a in enumerate(places)]
    deep = wide.shape[1] // PIECES
    for n, away in enumerate((gate_in, up_in, down_in)):
        for k in range(PIECES):
            wide[n, k * deep : (k + 1) * deep] = away[k * deep : (k + 1) * deep].astype(F32)
            results[n][k].start()
    for copy in results[0] + results[1] + results[2]:
        copy.wait()


def fill(place, away, grads):
    size = away[0].shape[1]
    return pl.pallas_call(
        fill_kernel,
        compiler_params=pltpu.CompilerParams(vmem_limit_bytes=12 * MIB),
        cost_estimate=pl.CostEstimate(
            flops=0, bytes_accessed=LANES, transcendentals=0
        ),
        grid_spec=pltpu.PrefetchScalarGridSpec(
            num_scalar_prefetch=1,
            grid=(1,),
            in_specs=[vmem()] * 3 + [hbm()] * 3,
            out_specs=[hbm()] * 3,
            scratch_shapes=[
                pltpu.VMEM((3,) + away[0].shape, F32),
                pltpu.SemaphoreType.DMA((3 * PIECES,)),
            ],
        ),
        out_shape=[pltpu.HBM(g.shape, F32) for g in grads],
        input_output_aliases={4: 0, 5: 1, 6: 2},
        name="fill",
    )(place, *[near(a) for a in away], *grads)


def weight_grads(place, column, size, normed, ggp, gup, hg, cots, after):
    if lax.axis_size("rep") == 2:
        *far, a, b, c, d, e = far_grads(normed, ggp, gup, hg, cots[0], cots[1], after)
        away = [other_core(f) for f in far]
        *grads, done = near_grads(place, a, b, c, d, e)
        return fill(place, away, grads), done
    grads = []
    for g in (ggp[:, :size], gup[:, :size]):
        term = jnp.roll(t_mm(normed, g).astype(BF16), column, 0)
        grads.append(lax.all_to_all(term, "rep", split_axis=0, concat_axis=1, tiled=True))
    term = jnp.roll(t_mm(hg[:, :size], cots[0]).astype(BF16), column, 1)
    grads.append(lax.all_to_all(term, "rep", split_axis=1, concat_axis=0, tiled=True))
    return [g.astype(F32) for g in grads], jnp.zeros((8, LANES), F32)


def mixed_kernel(stem_ref, taken_ref, back_ref, after_ref, out_ref, *terms_refs):
    half = out_ref.shape[1]
    back = unpacked(back_ref, half).astype(BF16)
    total = stem_ref[...].astype(F32) + t_mm(taken_ref[...], back)
    out_ref[...] = total.astype(BF16)
    top = tiles_of(half) * CAP
    terms = back_ref[0, top:, :].astype(F32)
    for b in range(1, back_ref.shape[0]):
        terms = terms + back_ref[b, top:, :].astype(F32)
    for n, ref in enumerate(terms_refs):
        ref[...] = terms[n * ref.shape[0] : (n + 1) * ref.shape[0]]


def mix(stem, taken, back, after, channels):
    tok, half = stem.shape
    sides = (back.shape[1] - tiles_of(half) * CAP) // channels
    return kernel_call(
        mixed_kernel,
        2 * taken.shape[0] * tok * half,
        2 * back.size,
        [near(a) for a in (stem, taken, back, after)],
        [fast((tok, half), BF16)] + [fast((channels, tok), F32)] * sides,
        "mixed",
    )


def local(
    latent,
    stem_weight,
    norm_gain,
    router_weight,
    routes,
    gate_weight,
    up_weight,
    down_weight,
    grad_mixed,
):
    rows_here, channels, width = latent.shape
    half = gate_weight.shape[0]
    experts = router_weight.shape[1]
    tok = rows_here * width
    blocks = lax.axis_size("exp")
    cores = lax.axis_size("rep")
    shards = blocks // experts
    slots = blocks * CAP
    me = lax.axis_index("exp")
    core = lax.axis_index("rep")
    column = core * half
    place = jnp.stack([me // shards, me, core]).astype(jnp.int32)

    paired = cores == 2 and shards == 2
    given = grad_mixed
    if cores != 2:
        given = lax.dynamic_slice_in_dim(grad_mixed, column, half, 1)
    copies = 1 if paired else shards
    packed, taken, cot = pack(place, latent, routes.T, given, experts, copies, half)
    packed = exchange(packed)

    stem, gain, router = stem_weight, norm_gain[None, :], router_weight
    if cores == 2:
        far = far_weights(place, gate_weight, up_weight, down_weight)
        gate_parts, up_parts, down_parts = [
            (w, other_core(f)) for w, f in zip((gate_weight, up_weight, down_weight), far)
        ]
    else:
        turned = lax.all_to_all(gate_weight, "rep", split_axis=1, concat_axis=0, tiled=True)
        spare = -turned.shape[1] % LANES
        gate_parts = (jnp.pad(jnp.roll(turned, -column, 0), ((0, 0), (0, spare))),)
        turned = lax.all_to_all(up_weight, "rep", split_axis=1, concat_axis=0, tiled=True)
        up_parts = (jnp.pad(jnp.roll(turned, -column, 0), ((0, 0), (0, spare))),)
        turned = lax.all_to_all(down_weight, "rep", split_axis=0, concat_axis=1, tiled=True)
        down_parts = (jnp.pad(jnp.roll(turned, -column, 1), ((0, spare), (0, 0))),)
        stem = jnp.roll(stem, -column, 1)
        gain = jnp.roll(gain, -column, 1)
        router = jnp.roll(router, -column, 0)

    inner, outer, stem, gain = gather_weights(
        place, stem, gain, router, gate_parts, up_parts, down_parts
    )
    same_cot, image = unpack(packed, half, channels + 2)
    if paired:
        image = weave(place, image, other_shard(image), gain)
        cots = [same_cot, other_shard(same_cot)]
        cots = [cots, [other_core(c) for c in cots]]
        outs = [(k * slots // 2, slots // 2, n * half, half) for n in range(2) for k in range(2)]
    elif cores == 2:
        cots = [[same_cot], [other_core(same_cot)]]
        outs = [(0, GROUP * CAP, n * half, half) for n in range(2)]
    else:
        joined = lax.all_gather(same_cot, "rep", axis=1, tiled=True)
        cots = [[jnp.roll(joined, -column, 1)]]
        outs = [(0, GROUP * CAP, 0, stem.shape[1])]
    normed, own_stem, _, value, meta, coef, sel, pg, pu, *outs = forward(
        place, image, stem, gain, inner, outer, half, outs, paired, width, experts
    )
    if paired:
        over = other_shard(add_up(outs[1], other_core(outs[3])))
        own, away = outs[0], other_core(outs[2])
    elif cores == 2:
        own, away = outs[0], other_core(outs[1])
        over = own
    else:
        turned = jnp.roll(outs[0], column, 1)
        own = lax.psum_scatter(turned, "rep", scatter_dimension=1, tiled=True)
        away = over = jnp.zeros_like(own)
    acts = [value, meta, coef, pg, pu]
    ggp, gup, hg, *cots, proj = backward(stem, gain, inner, outer, acts, cots, experts)
    lat_terms = to_image(place, proj, sel, stem, cot, paired, width, channels)

    sent = pack_back(place, own, away, over, lat_terms, paired)
    back = exchange(sent)

    size = gate_weight.shape[1] // cores
    grads, done = weight_grads(place, column, size, normed, ggp, gup, hg, cots, sent)
    grad_gate, grad_up, grad_down = grads

    mixed, *lat_sums = mix(own_stem, taken, back, done, channels)
    lat_sum = lat_sums[0]
    if paired:
        lat_sum = add_up(lat_sum, other_shard(lat_sums[1]))
    if cores == 2:
        mixed, grad_latent = join(
            place, mixed, other_core(mixed), lat_sum, other_core(lat_sum), rows_here
        )
    else:
        mixed = lax.all_gather(mixed, "rep", axis=1, tiled=True)
        lat_sum = lax.psum(lat_sum, "rep")
        grad_latent = lat_sum.reshape(channels, rows_here, width).transpose(1, 0, 2)
    return (mixed, grad_latent, grad_gate, grad_up, grad_down)


def solution(mesh):
    return jax.shard_map(
        local,
        mesh=mesh,
        in_specs=(
            P("exp", None, None),
            P(),
            P(),
            P(),
            P("exp", None),
            P("rep", "exp"),
            P("rep", "exp"),
            P("exp", "rep"),
            P("exp", None),
        ),
        out_specs=(
            P("exp", None),
            P("exp", None, None),
            P("rep", "exp"),
            P("rep", "exp"),
            P("exp", "rep"),
        ),
        check_vma=False,
    )
```

```python
import functools

import jax
import jax.numpy as jnp
from jax import lax
from jax.experimental import pallas as pl
from jax.experimental.pallas import tpu as pltpu
from jax.sharding import PartitionSpec as P

CAP = 40
LANES = 128
GROUP = 16
FORWARD_FLOPS = 100_000_000_000
F32 = jnp.float32
BF16 = jnp.bfloat16
MIB = 1024 * 1024


def dot(a, b, contract, batch=((), ())):
    return lax.dot_general(a, b, (contract, batch), preferred_element_type=F32)


def mm(a, b):
    return dot(a, b, ((1,), (0,)))


def mm_t(a, b):
    return dot(a, b, ((1,), (1,)))


def t_mm(a, b):
    return dot(a, b, ((0,), (0,)))


def call(kernel, flops, moved, mib=12, **kw):
    return pl.pallas_call(
        kernel,
        compiler_params=pltpu.CompilerParams(vmem_limit_bytes=mib * MIB),
        cost_estimate=pl.CostEstimate(flops=flops, bytes_accessed=moved, transcendentals=0),
        **kw,
    )


def whole(shape):
    return pl.BlockSpec(shape, lambda *_: (0,) * len(shape))


def rows(count, columns, at=0):
    return pl.BlockSpec((count, columns), lambda g, *_: (g, at))


def shape_of(shape, dtype):
    return jax.ShapeDtypeStruct(shape, dtype)


def lane_column(shape, width):
    return lax.broadcasted_iota(jnp.int32, shape, 1) % width


def shifted(window, shift, start, count):
    size = window.shape[1]
    return pltpu.roll(window, (-shift) % size, 1)[:, start : start + count]


def other_core(values):
    return lax.ppermute(values, "rep", [(0, 1), (1, 0)])


def other_shard(values):
    return lax.ppermute(values, "exp", [(i, i ^ 1) for i in range(lax.axis_size("exp"))])


def exchange(values):
    count = lax.axis_size("exp")
    shards = count // values.shape[0]
    groups = None
    if shards > 1:
        groups = [[s + shards * e for e in range(values.shape[0])] for s in range(shards)]
    return lax.all_to_all(
        values, "exp", split_axis=0, concat_axis=0, tiled=True, axis_index_groups=groups
    )


def hbm():
    return pl.BlockSpec(memory_space=pl.ANY)


def vmem():
    return pl.BlockSpec(memory_space=pltpu.VMEM)


def fast(shape, dtype):
    return pltpu.VMEM(shape, dtype)


def near(values):
    return pltpu.with_memory_space_constraint(values, pltpu.VMEM)


def far_off(values):
    return pltpu.with_memory_space_constraint(values, pltpu.HBM)


def kernel_call(kernel, flops, moved, operands, outs, name, mib=12, place=None, steps=1, scratch=(), specs=None, out_specs=None):
    specs = specs or [vmem() for _ in operands]
    out_specs = out_specs or [vmem() for _ in outs]
    return call(
        kernel,
        flops,
        moved,
        mib,
        grid_spec=pltpu.PrefetchScalarGridSpec(
            num_scalar_prefetch=0 if place is None else 1,
            grid=(steps,),
            in_specs=specs,
            out_specs=out_specs,
            scratch_shapes=list(scratch),
        ),
        out_shape=outs,
        name=name,
    )(*(() if place is None else (place,)), *operands)


def tiles_of(columns):
    return -(-columns // LANES)


def stacked(values):
    columns = values.shape[1]
    spare = tiles_of(columns) * LANES - columns
    if spare:
        values = jnp.concatenate([values, jnp.zeros((values.shape[0], spare), F32)], axis=1)
    parts = [values[:, k * LANES : (k + 1) * LANES] for k in range(tiles_of(columns))]
    return jnp.concatenate(parts, axis=0)


def pack_kernel(shards, half, place_ref, latent_ref, routes_ref, cot_ref, out_ref, taken_ref, here_ref):
    rows_here, channels, width = latent_ref.shape
    tok = rows_here * width
    experts = out_ref.shape[0] // shards
    cells = jnp.concatenate([latent_ref[r].astype(F32) for r in range(rows_here)], axis=1)
    routes = routes_ref[...].astype(F32)
    payload = jnp.concatenate([cells, routes], axis=0)
    cot = cot_ref[...]
    if cot.shape[1] != half:
        cot = jnp.where(place_ref[2] == 0, cot[:, :half], cot[:, half:])
    here_ref[...] = cot
    expert = lax.broadcasted_iota(jnp.int32, (experts, tok), 0).astype(F32)
    named = jnp.where((expert == routes[0:1]) | (expert == routes[1:2]), 1.0, 0.0)
    first = lax.broadcasted_iota(jnp.int32, (tok, tok), 0)
    second = lax.broadcasted_iota(jnp.int32, (tok, tok), 1)
    before = jnp.where(first <= second, 1.0, 0.0).astype(BF16)
    at = mm(named.astype(BF16), before) - 1.0
    slot = lax.broadcasted_iota(jnp.int32, (CAP, tok), 0).astype(F32)
    sel = [
        jnp.where((at[e : e + 1] == slot) & (named[e : e + 1] > 0.0), 1.0, 0.0)
        for e in range(experts)
    ]
    cots = mm(jnp.concatenate(sel, axis=0).astype(BF16), cot)
    taken_ref[...] = jnp.concatenate([one for one in sel for _ in range(shards)], axis=0).astype(BF16)
    for e in range(experts):
        slots = stacked(cots[e * CAP : (e + 1) * CAP])
        packed = jnp.concatenate([slots, payload], axis=0).astype(BF16)
        for n in range(shards):
            out_ref[e * shards + n] = packed


def pack(place, latent, routes_t, cot, experts, shards, half):
    rows_here, channels, width = latent.shape
    top, tok = routes_t.shape
    blocks = experts * shards
    depth = tiles_of(half) * CAP + channels + top
    operands = [latent, routes_t, cot]
    return kernel_call(
        functools.partial(pack_kernel, shards, half),
        2 * blocks * CAP * tok * half,
        4 * blocks * depth * LANES,
        [far_off(a) for a in operands],
        [
            shape_of((blocks, depth, LANES), BF16),
            pltpu.HBM((blocks * CAP, tok), BF16),
            pltpu.HBM((tok, half), BF16),
        ],
        "pack",
        place=place,
        specs=[whole(a.shape) for a in operands],
        out_specs=[
            whole((blocks, depth, LANES)),
            whole((blocks * CAP, tok)),
            whole((tok, half)),
        ],
    )


def unpacked(ref, columns):
    tiles = tiles_of(columns)
    blocks = ref.shape[0]
    held = [ref[b, : tiles * CAP, :].astype(F32) for b in range(blocks)]
    parts = [
        jnp.concatenate([one[k * CAP : (k + 1) * CAP] for one in held], axis=0)
        for k in range(tiles)
    ]
    return jnp.concatenate(parts, axis=1)[:, :columns]


def unpack_kernel(packed_ref, after_ref, cot_ref, image_ref):
    cot_ref[...] = unpacked(packed_ref, cot_ref.shape[1]).astype(BF16)
    top = packed_ref.shape[1] - image_ref.shape[1]
    for b in range(packed_ref.shape[0]):
        image_ref[b] = packed_ref[b, top:, :]


def unpack(packed, half, lines, after):
    blocks, _, tok = packed.shape
    return kernel_call(
        unpack_kernel,
        100_000_000_000,
        4 * packed.size,
        [near(packed), far_off(after)],
        [fast((blocks * CAP, half), BF16), fast((blocks, lines, tok), BF16)],
        "unpack",
        specs=[vmem(), hbm()],
    )


def weave_kernel(place_ref, same_ref, other_ref, after_ref, then_ref, out_ref):
    even = (place_ref[1] & 1) == 0
    for e in range(same_ref.shape[0]):
        same, other = same_ref[e], other_ref[e]
        out_ref[2 * e] = jnp.where(even, same, other)
        out_ref[2 * e + 1] = jnp.where(even, other, same)


def weave(place, same, other, after, then):
    shape = (2 * same.shape[0],) + same.shape[1:]
    return kernel_call(
        weave_kernel,
        0,
        8 * same.size,
        [near(same), near(other), near(after), near(then)],
        [fast(shape, same.dtype)],
        "weave",
        place=place,
    )[0]


def sum_kernel(a_ref, b_ref, after_ref, out_ref):
    out_ref[...] = (a_ref[...].astype(F32) + b_ref[...].astype(F32)).astype(out_ref.dtype)


def add_up(a, b, after):
    operands = [near(a), near(b), near(after)]
    outs = [fast(a.shape, a.dtype)]
    return kernel_call(sum_kernel, a.size, 6 * a.size, operands, outs, "add_up")[0]


def pack_back_kernel(paired, a_ref, b_ref, c_ref, terms_ref, over_ref, after_ref, out_ref):
    total = a_ref[...].astype(F32) + b_ref[...].astype(F32)
    if paired:
        total = total + c_ref[...].astype(F32)
    for b in range(out_ref.shape[0]):
        slots = stacked(total[b * CAP : (b + 1) * CAP])
        terms = terms_ref[b]
        if paired:
            terms = terms + over_ref[b].astype(F32)
        out_ref[b] = jnp.concatenate([slots, terms], axis=0).astype(BF16)


def pack_back(a, b, c, terms, over, after, paired):
    blocks, channels, tok = terms.shape
    depth = tiles_of(a.shape[1]) * CAP + channels
    return kernel_call(
        functools.partial(pack_back_kernel, paired),
        a.size,
        8 * a.size,
        [near(x) for x in (a, b, c, terms, over, after)],
        [shape_of((blocks, depth, LANES), BF16)],
        "pack_back",
    )[0]


PIECES = 4


def pieces(source, target, sem, at=0):
    deep = source.shape[0] // PIECES
    bands = [pl.ds(k * deep, deep) for k in range(PIECES)]
    return [
        pltpu.make_async_copy(source.at[band, :], target.at[band, :], sem.at[at + k])
        for k, band in enumerate(bands)
    ]


def far_kernel(place_ref, gate_ref, up_ref, down_ref, after_ref, gate_out, up_out, down_out, sem):
    size = gate_out.shape[1]
    at = pl.multiple_of((1 - place_ref[2]) * size, LANES)
    copies = (
        pieces(gate_ref.at[:, pl.ds(at, size)], gate_out, sem)
        + pieces(up_ref.at[:, pl.ds(at, size)], up_out, sem, PIECES)
        + pieces(down_ref.at[pl.ds(at, size), :], down_out, sem, 2 * PIECES)
    )
    for copy in copies:
        copy.start()
    for copy in copies:
        copy.wait()


def far_weights(place, gate, up, down, after):
    half, hid = gate.shape
    size = hid // 2
    return kernel_call(
        far_kernel,
        0,
        LANES,
        [far_off(gate), far_off(up), far_off(down), after],
        [fast((half, size), BF16), fast((half, size), BF16), fast((size, half), BF16)],
        "far_weights",
        place=place,
        specs=[hbm()] * 4,
        scratch=[pltpu.SemaphoreType.DMA((3 * PIECES,))],
    )


def cuts(lengths):
    start, out = 0, []
    for n in lengths:
        out.append((start, n))
        start += n
    return out


def params_kernel(turn, experts, place_ref, stem_in, gain_in, router_in, after, stem, gain, router):
    wide = router_in[...].astype(F32)
    model = wide.shape[0]
    blank = jnp.zeros((model, LANES - 2 * experts), F32)
    wide = jnp.concatenate([wide, wide, blank], axis=1)
    values, gains = stem_in[...], gain_in[...]
    if turn:
        half = model // 2
        first = place_ref[2] == 0
        wide = jnp.where(first, wide, jnp.concatenate([wide[half:], wide[:half]], axis=0))
        turned = jnp.concatenate([values[:, half:], values[:, :half]], axis=1)
        values = jnp.where(first, values, turned)
        turned = jnp.concatenate([gains[:, half:], gains[:, :half]], axis=1)
        gains = jnp.where(first, gains, turned)
    stem[...] = values
    gain[...] = gains
    router[...] = wide.astype(BF16)


def small_params(place, stem, gain, router, after, turn):
    model, experts = router.shape
    small = [far_off(stem), far_off(gain), far_off(router)]
    shapes = [(stem.shape, BF16), (gain.shape, F32), ((model, LANES), BF16)]
    return kernel_call(
        functools.partial(params_kernel, turn, experts),
        0,
        LANES,
        small + [after],
        [pltpu.HBM(*a) for a in shapes],
        "params",
        place=place,
        specs=[whole(a.shape) for a in small] + [hbm()],
        out_specs=[whole(shape) for shape, _ in shapes],
    )


def inner_copies(place_ref, refs, inner, size, at, sem):
    copies = []
    for n, (ref, (a, depth)) in enumerate(zip(refs, cuts([r.shape[0] for r in refs]))):
        if ref.shape[1] != size:
            ref = ref.at[:, pl.ds(pl.multiple_of(place_ref[2] * size, LANES), size)]
        copies += pieces(ref, inner.at[pl.ds(a, depth), pl.ds(at, size)], sem, n * PIECES)
    return copies


def outer_copies(place_ref, refs, outer, sem):
    copies = []
    size = outer.shape[0]
    for n, (ref, (a, depth)) in enumerate(zip(refs, cuts([r.shape[1] for r in refs]))):
        if ref.shape[0] != size:
            ref = ref.at[pl.ds(pl.multiple_of(place_ref[2] * size, LANES), size), :]
        copies += pieces(ref, outer.at[:, pl.ds(a, depth)], sem, n * PIECES)
    return copies


def gather_kernel(parts, place_ref, *refs):
    gates, (stem_in, gain_in, router_in) = refs[:parts], refs[parts : parts + 3]
    stem, gain, inner, small_sem, sem = refs[parts + 3 :]
    size = (inner.shape[1] - LANES) // 2
    copies = [
        pltpu.make_async_copy(stem_in, stem, small_sem.at[0]),
        pltpu.make_async_copy(gain_in, gain, small_sem.at[1]),
        pltpu.make_async_copy(router_in, inner.at[:, pl.ds(2 * size, LANES)], small_sem.at[2]),
    ]
    copies += inner_copies(place_ref, gates, inner, size, 0, sem)
    for copy in copies:
        copy.start()
    for copy in copies:
        copy.wait()


def gather(place, small, gates, size):
    stem, gain, router = small
    model = router.shape[0]
    operands = [far_off(a) for a in list(gates) + list(small)]
    return kernel_call(
        functools.partial(gather_kernel, len(gates)),
        0,
        LANES,
        operands,
        [
            fast(stem.shape, BF16),
            fast(gain.shape, F32),
            fast((model, 2 * size + LANES), BF16),
        ],
        "gather",
        place=place,
        specs=[hbm()] * len(operands),
        scratch=[
            pltpu.SemaphoreType.DMA((3,)),
            pltpu.SemaphoreType.DMA((len(gates) * PIECES,)),
        ],
    )


def join_kernel(place_ref, own_ref, away_ref, a_ref, b_ref, out_ref, latent_ref):
    half = own_ref.shape[1]
    first = place_ref[2] == 0
    own, away = own_ref[...], away_ref[...]
    out_ref[:, :half] = jnp.where(first, own, away)
    out_ref[:, half:] = jnp.where(first, away, own)
    total = a_ref[...] + b_ref[...]
    width = latent_ref.shape[2]
    for r in range(latent_ref.shape[0]):
        latent_ref[r] = total[:, r * width : (r + 1) * width]


def join(place, own, away, a, b, rows_here):
    count, half = own.shape
    channels, tok = a.shape
    return kernel_call(
        join_kernel,
        0,
        8 * count * half,
        [near(own), near(away), near(a), near(b)],
        [
            shape_of((count, 2 * half), BF16),
            shape_of((rows_here, channels, tok // rows_here), F32),
        ],
        "join",
        place=place,
    )


def pair_selection(named):
    lanes = named.shape[1]
    tok = lanes // 2
    first = lax.broadcasted_iota(jnp.int32, (lanes, lanes), 0)
    second = lax.broadcasted_iota(jnp.int32, (lanes, lanes), 1)
    before = ((first <= second) & (first // tok == second // tok)).astype(F32).astype(BF16)
    wide = jnp.broadcast_to(named, (8, lanes)).astype(BF16)
    place = mm(wide, before)[:1]
    lane = lax.broadcasted_iota(jnp.int32, (1, lanes), 1)
    place = place - 1.0 + jnp.where(lane >= tok, float(CAP), 0.0)
    slot = lax.broadcasted_iota(jnp.int32, (2 * CAP, lanes), 0).astype(F32)
    return jnp.where((place == slot) & (named > 0.0), 1.0, 0.0)


def pair_patches(image_ref, top, first, width, channels):
    blocks = image_ref.shape[0]
    before = image_ref[jnp.maximum(first - 1, 0), top : top + channels, :].astype(F32)
    after = image_ref[jnp.minimum(first + 2, blocks - 1), top : top + channels, :].astype(F32)
    window = jnp.concatenate(
        [
            jnp.where(first > 0, before, 0.0),
            image_ref[first, top : top + channels, :].astype(F32),
            image_ref[first + 1, top : top + channels, :].astype(F32),
            jnp.where(first + 2 < blocks, after, 0.0),
        ],
        axis=1,
    )
    tok = image_ref.shape[2]
    column = lane_column((channels, 2 * tok), width)
    pieces = []
    for i in range(3):
        for j in range(3):
            piece = shifted(window, (i - 1) * width + j - 1, tok, 2 * tok)
            source = column + (j - 1)
            pieces.append(jnp.where((source >= 0) & (source < width), piece, 0.0))
    return jnp.concatenate(pieces, axis=0)


def by_side(pairs, even):
    same = [jnp.where(even, p[:CAP], p[CAP:]) for p in pairs]
    other = [jnp.where(even, p[CAP:], p[:CAP]) for p in pairs]
    return same + other


def forward_kernel(
    paired, parts, width, experts, outs, place_ref, image_ref, stem_ref, gain_ref, _, *refs
):
    weights, refs = refs[: 2 * parts], refs[2 * parts :]
    saved_ref, own_out, normed_ref, value_ref, meta_ref, coef_ref, sel_ref, pg_ref, pu_ref = refs[:9]
    hidden_ref, inner, outer, *out_refs = refs[9:-4]
    own_ref, save_sem, up_sem, down_sem = refs[-4:]
    step = pl.program_id(0)
    size = outer.shape[0]
    up_copies = inner_copies(place_ref, weights[:parts], inner, size, size, up_sem)
    down_copies = outer_copies(place_ref, weights[parts:], outer, down_sem)

    def arrive(copies):
        @pl.when(step == 0)
        def _():
            for copy in copies:
                copy.wait()

    @pl.when(step == 0)
    def _():
        for copy in up_copies + down_copies:
            copy.start()

    chunk = GROUP * CAP
    here = pl.ds(pl.multiple_of(step * chunk, chunk), chunk)
    top = 0
    channels = image_ref.shape[1] - 2
    mine = place_ref[0].astype(F32)
    even = (place_ref[1] & 1) == 0
    taken, others = [], []
    for q in range(GROUP // 2):
        first = step * GROUP + 2 * q
        lines = [image_ref[first + n, top + channels :, :].astype(F32) for n in range(2)]
        named_by = [jnp.concatenate([line[k : k + 1] for line in lines], axis=1) for k in range(2)]
        named = jnp.where((named_by[0] == mine) | (named_by[1] == mine), 1.0, 0.0)
        sel = pair_selection(named)
        sel_ref[step * (GROUP // 2) + q] = sel.astype(BF16)
        other = named_by[0] + named_by[1] - mine
        others.append(jnp.sum(sel * other, axis=1, keepdims=True))
        patches = pair_patches(image_ref, top, first, width, channels)
        taken.append(mm_t(sel.astype(BF16), patches.astype(BF16)))
    if paired:
        taken, others = by_side(taken, even), by_side(others, even)
    patches = jnp.concatenate(taken, axis=0).astype(BF16)
    other = jnp.concatenate(others, axis=0)
    stem = mm(patches, stem_ref[...]).astype(BF16)
    value_ref[here, :] = stem
    value = stem.astype(F32)
    scale = lax.rsqrt(jnp.mean(value * value, axis=-1, keepdims=True) + 1e-06)
    normed = (value * scale * gain_ref[...]).astype(BF16)
    normed_ref[...] = normed
    save = pltpu.make_async_copy(normed_ref, saved_ref.at[here, :], save_sem.at[0])
    save.start()
    own_save = pltpu.make_async_copy(own_ref, own_out, save_sem.at[1])

    @pl.when(step == 0)
    def _():
        me = place_ref[1]
        first = me // 2 * 2
        tok = image_ref.shape[2]
        own = pair_patches(image_ref, top, first, width, channels)
        own = jnp.where(me == first, own[:, :tok], own[:, tok:]).astype(BF16)
        own_ref[...] = t_mm(own, stem_ref[:, : own_ref.shape[1]]).astype(BF16)
        own_save.start()

    logits = mm(normed, inner[:, 2 * size :])
    lane = lax.broadcasted_iota(jnp.int32, logits.shape, 1)
    again = jnp.where(lane >= experts, lane - experts, lane).astype(F32)
    lane = lane.astype(F32)
    sig_mine = jax.nn.sigmoid(jnp.sum(jnp.where(lane == mine, logits, 0.0), axis=1, keepdims=True))
    sig_other = jax.nn.sigmoid(jnp.sum(jnp.where(lane == other, logits, 0.0), axis=1, keepdims=True))
    gate = sig_mine / (sig_mine + sig_other)
    rest = sig_other / (sig_mine + sig_other)
    both = gate * rest
    coef_ref[here, :] = jnp.where(again == mine, both * (1.0 - sig_mine), 0.0) - jnp.where(
        again == other, both * (1.0 - sig_other), 0.0
    )
    meta_ref[here, :] = jnp.where(lane == 0.0, gate, scale)
    pre_gate = mm(normed, inner[:, :size])
    arrive(up_copies)
    pre_up = mm(normed, inner[:, size : 2 * size])
    pg_ref[here, :] = pre_gate.astype(BF16)
    pu_ref[here, :] = pre_up.astype(BF16)
    hidden = (pre_gate * jax.nn.sigmoid(pre_gate) * pre_up).astype(BF16)
    hidden_ref[here, :] = hidden
    arrive(down_copies)
    if paired:
        half_rows = chunk // 2
        for ref, (a, n) in zip(out_refs, cuts([r.shape[1] for r in out_refs])):
            part = mm(hidden[half_rows:], outer[:, a : a + n])
            ref[...] = (gate[half_rows:] * part).astype(BF16)
    else:
        for ref, (a, n) in zip(out_refs, cuts([r.shape[1] for r in out_refs])):
            ref[here, :] = (gate * mm(hidden, outer[:, a : a + n])).astype(BF16)
    save.wait()

    @pl.when(step == 0)
    def _():
        own_save.wait()


def forward(place, image, gathered, weights, size, half, columns, paired, width, experts):
    blocks, _, tok = image.shape
    slots, chunk = blocks * CAP, GROUP * CAP
    stem, gain, inner = gathered
    model = stem.shape[1]
    parts = len(weights) // 2
    operands = [near(image), near(stem), near(gain), near(inner)] + [far_off(w) for w in weights]
    outs = [
        pltpu.HBM((slots, model), BF16),
        pltpu.HBM((tok, half), BF16),
        fast((chunk, model), BF16),
        fast((slots, model), BF16),
        fast((slots, LANES), F32),
        fast((slots, LANES), F32),
        fast((blocks // 2, 2 * CAP, 2 * tok), BF16),
        fast((slots, size), BF16),
        fast((slots, size), BF16),
        fast((slots, size), BF16),
        fast(inner.shape, BF16),
        fast((size, model), BF16),
    ]
    outs += [fast((slots // 2 if paired else slots, n), BF16) for n in columns]
    return pl.pallas_call(
        functools.partial(forward_kernel, paired, parts, width, experts, columns),
        compiler_params=pltpu.CompilerParams(vmem_limit_bytes=20 * MIB),
        cost_estimate=pl.CostEstimate(
            flops=FORWARD_FLOPS, bytes_accessed=LANES, transcendentals=0
        ),
        grid_spec=pltpu.PrefetchScalarGridSpec(
            num_scalar_prefetch=1,
            grid=(blocks // GROUP,),
            in_specs=[vmem()] * 4 + [hbm()] * len(weights),
            out_specs=[hbm()] * 2 + [vmem()] * (len(outs) - 2),
            scratch_shapes=[
                pltpu.VMEM((tok, half), BF16),
                pltpu.SemaphoreType.DMA((2,)),
                pltpu.SemaphoreType.DMA((parts * PIECES,)),
                pltpu.SemaphoreType.DMA((parts * PIECES,)),
            ],
        ),
        out_shape=outs,
        input_output_aliases={4: 10},
        name="forward",
    )(place, *operands)


def outputs_kernel(meta_ref, hidden_ref, outer, near_ref, far_ref):
    count, half = near_ref.shape
    gate = meta_ref[:count, 0:1]
    hidden = hidden_ref[:count, :]
    near_ref[...] = (gate * mm(hidden, outer[:, :half])).astype(BF16)
    far_ref[...] = (gate * mm(hidden, outer[:, half:])).astype(BF16)


def outputs(meta, hidden, outer):
    count, half = hidden.shape[0] // 2, outer.shape[1] // 2
    return kernel_call(
        outputs_kernel,
        0,
        LANES,
        [near(meta), near(hidden), near(outer)],
        [fast((count, half), BF16)] * 2,
        "outputs",
    )


def backward_kernel(
    parts, bands, experts, stem_ref, gain_ref, inner, outer, value_ref, meta_ref, coef_ref, pg_ref, pu_ref,
    *refs,
):
    cot_refs, refs = refs[: parts * bands], refs[parts * bands :]
    saved, refs = refs[: 3 + parts], refs[3 + parts :]
    proj_ref, ggp_ref, gup_ref, hg_ref, sem = refs
    step = pl.program_id(0)
    model = stem_ref.shape[1]
    chunk = GROUP * CAP
    here = pl.ds(pl.multiple_of(step * chunk, chunk), chunk)
    sources = [ggp_ref, gup_ref, hg_ref]
    targets = [ref.at[here, :] for ref in saved[:3]]
    for n, ref in enumerate(cot_refs):
        if bands == 1:
            sources.append(ref.at[here, :])
            targets.append(saved[3 + n].at[here, :])
        else:
            deep = ref.shape[0]
            sources.append(ref)
            targets.append(saved[3 + n // bands].at[pl.ds(n % bands * deep, deep), :])
    saves = [
        pltpu.make_async_copy(a, b, sem.at[n]) for n, (a, b) in enumerate(zip(sources, targets))
    ]
    for save in saves[3:]:
        save.start()
    gate = meta_ref[here, 0:1]
    scale = meta_ref[here, 1:2]
    raw = 0.0
    for k, (a, n) in enumerate(cuts([r.shape[1] for r in cot_refs[::bands]])):
        if bands == 1:
            cot = cot_refs[k][here, :]
        else:
            cot = jnp.concatenate([r[...] for r in cot_refs[k * bands : (k + 1) * bands]], axis=0)
        raw = raw + mm_t(cot, outer[:, a : a + n])
    pre_gate = pg_ref[here, :].astype(F32)
    pre_up = pu_ref[here, :].astype(F32)
    sigma = jax.nn.sigmoid(pre_gate)
    silu = pre_gate * sigma
    hidden = silu * pre_up
    grad_gates = jnp.sum(raw * hidden, axis=1, keepdims=True)
    hg_ref[...] = (gate * hidden).astype(BF16)
    grad_hidden = gate * raw
    ggp = (grad_hidden * pre_up * sigma * (1.0 + pre_gate - silu)).astype(BF16)
    gup = (grad_hidden * silu).astype(BF16)
    ggp_ref[...] = ggp
    gup_ref[...] = gup
    for save in saves[:3]:
        save.start()
    grad_logits = grad_gates * coef_ref[here, :]
    high = grad_logits.astype(BF16)
    low = (grad_logits - high.astype(F32)).astype(BF16)
    lane = lax.broadcasted_iota(jnp.int32, grad_logits.shape, 1)
    mix = jnp.where(lane < experts, high.astype(F32), low.astype(F32)).astype(BF16)
    back = mm_t(jnp.concatenate([ggp, gup, mix], axis=1), inner[...]) * gain_ref[...]
    value = value_ref[here, :].astype(F32)
    along = jnp.sum(back * value, axis=1, keepdims=True) * (scale * scale * scale) / model
    grad = (scale * back - along * value).astype(BF16)
    proj_ref[here, :] = mm_t(grad, stem_ref[...]).astype(BF16)
    for save in saves:
        save.wait()


def backward(stem, gain, inner, outer, acts, cots, experts):
    slots, model = acts[0].shape
    size, chunk = outer.shape[0], GROUP * CAP
    taps = stem.shape[0]
    parts, bands = len(cots), len(cots[0])
    operands = [stem, gain, inner, outer] + list(acts) + [c for part in cots for c in part]
    return kernel_call(
        functools.partial(backward_kernel, parts, bands, experts),
        2 * slots * model * size * 4,
        slots * (4 * model + 12 * size) + 6 * model * size,
        [near(a) for a in operands],
        [pltpu.HBM((slots, size), BF16)] * 3
        + [pltpu.HBM((slots, part[0].shape[1]), BF16) for part in cots]
        + [fast((slots, taps), BF16)]
        + [fast((chunk, size), BF16)] * 3,
        "backward",
        mib=20,
        steps=slots // chunk,
        out_specs=[hbm()] * (3 + parts) + [vmem()] * 4,
        scratch=[pltpu.SemaphoreType.DMA((3 + parts * bands,))],
    )


def image_kernel(paired, width, place_ref, proj_ref, sel_ref, stem_ref, cot_ref, *refs):
    out_refs, terms = refs[:-1], refs[-1]
    pairs = sel_ref.shape[0]
    tok = cot_ref.shape[0]
    channels = out_refs[0].shape[1]
    count = 2 * pairs * tok
    own = mm_t(stem_ref[:, : cot_ref.shape[1]], cot_ref[...])
    me = place_ref[1]
    even = (me & 1) == 0
    proj = proj_ref[...].astype(F32)
    for q in range(pairs):
        if paired:
            same = proj[CAP * q : CAP * (q + 1)]
            other = proj[CAP * (pairs + q) : CAP * (pairs + q + 1)]
            both = [jnp.where(even, same, other), jnp.where(even, other, same)]
            pair = jnp.concatenate(both, axis=0)
        else:
            pair = proj[2 * CAP * q : 2 * CAP * (q + 1)]
        block = t_mm(pair.astype(BF16), sel_ref[q])
        terms[:, 2 * q * tok : (2 * q + 1) * tok] = block[:, :tok] + jnp.where(2 * q == me, own, 0.0)
        terms[:, (2 * q + 1) * tok : (2 * q + 2) * tok] = block[:, tok:] + jnp.where(
            2 * q + 1 == me, own, 0.0
        )
    lane = lax.broadcasted_iota(jnp.int32, (channels, count), 1)
    total = jnp.zeros((channels, count), F32)
    for i in range(3):
        for j in range(3):
            k = (3 * i + j) * channels
            shift = (i - 1) * width + j - 1
            piece = pltpu.roll(terms[k : k + channels, :], shift % count, 1)
            column = lane % width + (1 - j)
            token = lane - shift
            keep = (column >= 0) & (column < width) & (token >= 0) & (token < count)
            total = total + jnp.where(keep, piece, 0.0)
    for q in range(pairs):
        low = total[:, 2 * q * tok : (2 * q + 1) * tok]
        high = total[:, (2 * q + 1) * tok : (2 * q + 2) * tok]
        if paired:
            out_refs[0][q] = jnp.where(even, low, high)
            out_refs[1][q] = jnp.where(even, high, low).astype(BF16)
        else:
            out_refs[0][2 * q] = low
            out_refs[0][2 * q + 1] = high


def to_image(place, proj, sel, stem, cot, paired, width, channels):
    pairs = sel.shape[0]
    blocks, tok = 2 * pairs, cot.shape[0]
    taps, half = stem.shape[0], cot.shape[1]
    return kernel_call(
        functools.partial(image_kernel, paired, width),
        2 * proj.shape[0] * 2 * tok * taps,
        4 * taps * blocks * tok,
        [near(a) for a in (proj, sel, stem, cot)],
        [fast((pairs, channels, tok), F32), fast((pairs, channels, tok), BF16)]
        if paired
        else [fast((blocks, channels, tok), F32)],
        "to_image",
        place=place,
        scratch=[pltpu.VMEM((taps, blocks * tok), F32)],
    )


def far_grads_kernel(normed, ggp, gup, hg, *refs):
    cots, (gate_out, up_out, down_out) = refs[:-3], refs[-3:]
    half = cots[0].shape[1]
    far = normed[:, half:]
    gate_out[...] = t_mm(far, ggp[...]).astype(BF16)
    up_out[...] = t_mm(far, gup[...]).astype(BF16)
    cot = jnp.concatenate([ref[...] for ref in cots], axis=0)
    down_out[...] = t_mm(hg[...], cot).astype(BF16)


def far_grads(normed, ggp, gup, hg, cots):
    slots, size = ggp.shape
    half = cots[0].shape[1]
    return kernel_call(
        far_grads_kernel,
        6 * slots * size * half,
        20 * slots * size,
        [near(a) for a in [normed, ggp, gup, hg] + list(cots)],
        [fast((half, size), BF16)] * 2 + [fast((size, half), BF16)],
        "far_grads",
    )


def near_grads_kernel(
    place_ref, normed, ggp, gup, hg, cot, after_ref, gate_out, up_out, down_out,
    left, right, own, sem, own_sem,
):
    half = cot.shape[1]
    size = ggp.shape[1]
    here = pl.multiple_of(place_ref[2] * size, LANES)
    sources = (normed.at[:, pl.ds(0, half)], ggp, gup, hg, cot)
    targets = (left.at[0], right.at[0], right.at[1], left.at[1], right.at[2])
    loads = [pltpu.make_async_copy(a, b, sem.at[n]) for n, (a, b) in enumerate(zip(sources, targets))]
    places = (
        gate_out.at[:, pl.ds(here, size)],
        up_out.at[:, pl.ds(here, size)],
        down_out.at[pl.ds(here, size), :],
    )
    results = [pieces(own.at[n], a, own_sem, n * PIECES) for n, a in enumerate(places)]
    for load in loads:
        load.start()
    for load in loads[:2]:
        load.wait()
    own[0] = t_mm(left[0], right[0])
    for copy in results[0]:
        copy.start()
    loads[2].wait()
    own[1] = t_mm(left[0], right[1])
    for copy in results[1]:
        copy.start()
    loads[3].wait()
    loads[4].wait()
    own[2] = t_mm(left[1], right[2])
    for copy in results[2]:
        copy.start()
    for copy in results[0] + results[1] + results[2]:
        copy.wait()


def near_grads(place, normed, ggp, gup, hg, cot, after):
    slots, size = ggp.shape
    half = cot.shape[1]
    return kernel_call(
        near_grads_kernel,
        100_000_000_000,
        LANES,
        [far_off(a) for a in (normed, ggp, gup, hg, cot)] + [after],
        [pltpu.HBM((half, 2 * size), F32)] * 2
        + [pltpu.HBM((2 * size, half), F32)],
        "near_grads",
        mib=20,
        place=place,
        specs=[hbm()] * 6,
        out_specs=[hbm()] * 3,
        scratch=[
            pltpu.VMEM((2, slots, half), BF16),
            pltpu.VMEM((3, slots, half), BF16),
            pltpu.VMEM((3, half, size), F32),
            pltpu.SemaphoreType.DMA((5,)),
            pltpu.SemaphoreType.DMA((3 * PIECES,)),
        ],
    )


def fill_kernel(
    place_ref, gate_in, up_in, down_in, gate_old, up_old, down_old,
    gate_out, up_out, down_out, done_ref, away, wide, in_sem, sem,
):
    size = gate_in.shape[1]
    there = pl.multiple_of((1 - place_ref[2]) * size, LANES)
    places = (
        gate_out.at[:, pl.ds(there, size)],
        up_out.at[:, pl.ds(there, size)],
        down_out.at[pl.ds(there, size), :],
    )
    loads = [
        pieces(a, away.at[n], in_sem, n * PIECES) for n, a in enumerate((gate_in, up_in, down_in))
    ]
    results = [pieces(wide.at[n], a, sem, n * PIECES) for n, a in enumerate(places)]
    deep = wide.shape[1] // PIECES
    done_ref[...] = jnp.zeros(done_ref.shape, F32)
    for load in loads[0] + loads[1] + loads[2]:
        load.start()
    for n in range(3):
        for k in range(PIECES):
            loads[n][k].wait()
            wide[n, k * deep : (k + 1) * deep] = away[n, k * deep : (k + 1) * deep].astype(F32)
            results[n][k].start()
    for copy in results[0] + results[1] + results[2]:
        copy.wait()


def fill(place, away, grads):
    shape = away[0].shape
    return pl.pallas_call(
        fill_kernel,
        compiler_params=pltpu.CompilerParams(vmem_limit_bytes=16 * MIB),
        cost_estimate=pl.CostEstimate(
            flops=100_000_000_000, bytes_accessed=LANES, transcendentals=0
        ),
        grid_spec=pltpu.PrefetchScalarGridSpec(
            num_scalar_prefetch=1,
            grid=(1,),
            in_specs=[hbm()] * 6,
            out_specs=[hbm()] * 3 + [vmem()],
            scratch_shapes=[
                pltpu.VMEM((3,) + shape, BF16),
                pltpu.VMEM((3,) + shape, F32),
                pltpu.SemaphoreType.DMA((3 * PIECES,)),
                pltpu.SemaphoreType.DMA((3 * PIECES,)),
            ],
        ),
        out_shape=[pltpu.HBM(g.shape, F32) for g in grads] + [fast((8, LANES), F32)],
        input_output_aliases={4: 0, 5: 1, 6: 2},
        name="fill",
    )(place, *[far_off(a) for a in away], *grads)


def gathered_grads(column, size, normed, ggp, gup, hg, cot):
    grads = []
    for g in (ggp[:, :size], gup[:, :size]):
        term = jnp.roll(t_mm(normed, g).astype(BF16), column, 0)
        grads.append(lax.all_to_all(term, "rep", split_axis=0, concat_axis=1, tiled=True))
    term = jnp.roll(t_mm(hg[:, :size], cot).astype(BF16), column, 1)
    grads.append(lax.all_to_all(term, "rep", split_axis=1, concat_axis=0, tiled=True))
    return [g.astype(F32) for g in grads]


def mixed_kernel(stem_ref, taken_ref, back_ref, after_ref, out_ref, *terms_refs):
    half = out_ref.shape[1]
    back = unpacked(back_ref, half).astype(BF16)
    total = stem_ref[...].astype(F32) + t_mm(taken_ref[...], back)
    out_ref[...] = total.astype(BF16)
    top = tiles_of(half) * CAP
    terms = back_ref[0, top:, :].astype(F32)
    for b in range(1, back_ref.shape[0]):
        terms = terms + back_ref[b, top:, :].astype(F32)
    for n, ref in enumerate(terms_refs):
        ref[...] = terms[n * ref.shape[0] : (n + 1) * ref.shape[0]]


def mix(stem, taken, back, after, channels):
    tok, half = stem.shape
    sides = (back.shape[1] - tiles_of(half) * CAP) // channels
    return kernel_call(
        mixed_kernel,
        2 * taken.shape[0] * tok * half,
        2 * back.size,
        [near(a) for a in (stem, taken, back, after)],
        [fast((tok, half), BF16)] + [fast((channels, tok), F32)] * sides,
        "mixed",
    )


def local(
    latent,
    stem_weight,
    norm_gain,
    router_weight,
    routes,
    gate_weight,
    up_weight,
    down_weight,
    grad_mixed,
):
    rows_here, channels, width = latent.shape
    half = gate_weight.shape[0]
    experts = router_weight.shape[1]
    tok = rows_here * width
    blocks = lax.axis_size("exp")
    cores = lax.axis_size("rep")
    shards = blocks // experts
    slots = blocks * CAP
    me = lax.axis_index("exp")
    core = lax.axis_index("rep")
    column = core * half
    place = jnp.stack([me // shards, me, core]).astype(jnp.int32)

    paired = cores == 2 and shards == 2
    given = grad_mixed
    if cores != 2:
        given = lax.dynamic_slice_in_dim(grad_mixed, column, half, 1)
    copies = 1 if paired else shards
    packed, taken, cot = pack(place, latent, routes.T, given, experts, copies, half)
    arrived = exchange(packed)

    stem, gain, router = stem_weight, norm_gain[None, :], router_weight
    if cores == 2:
        far = far_weights(place, gate_weight, up_weight, down_weight, packed)
        gate_parts, up_parts, down_parts = [
            (w, other_core(f)) for w, f in zip((gate_weight, up_weight, down_weight), far)
        ]
    else:
        turned = lax.all_to_all(gate_weight, "rep", split_axis=1, concat_axis=0, tiled=True)
        spare = -turned.shape[1] % LANES
        gate_parts = (jnp.pad(jnp.roll(turned, -column, 0), ((0, 0), (0, spare))),)
        turned = lax.all_to_all(up_weight, "rep", split_axis=1, concat_axis=0, tiled=True)
        up_parts = (jnp.pad(jnp.roll(turned, -column, 0), ((0, 0), (0, spare))),)
        turned = lax.all_to_all(down_weight, "rep", split_axis=0, concat_axis=1, tiled=True)
        down_parts = (jnp.pad(jnp.roll(turned, -column, 1), ((0, spare), (0, 0))),)
        stem = jnp.roll(stem, -column, 1)
        gain = jnp.roll(gain, -column, 1)
        router = jnp.roll(router, -column, 0)

    small = small_params(place, stem, gain, router, packed, cores == 2)
    same_cot, image = unpack(arrived, half, channels + 2, small[1])
    size = down_parts[-1].shape[0]
    gathered = gather(place, small, gate_parts, size)
    if paired:
        joined = other_core(same_cot)
        image = weave(place, image, other_shard(image), joined, gathered[1])
        cots = [same_cot, other_shard(same_cot)]
        cots = [cots, [joined, other_core(cots[1])]]
    elif cores == 2:
        cots = [[same_cot], [other_core(same_cot)]]
    else:
        joined = lax.all_gather(same_cot, "rep", axis=1, tiled=True)
        cots = [[jnp.roll(joined, -column, 1)]]
    weights = list(up_parts) + list(down_parts)
    columns = [w.shape[1] for w in down_parts]
    kept, own_stem, normed, value, meta, coef, sel, pg, pu, hidden, inner, outer, *outs = forward(
        place, image, gathered, weights, size, half, columns, paired, width, experts
    )
    stem, gain, _ = gathered
    if paired:
        own, away = outputs(meta, hidden, outer)
        over = other_shard(add_up(outs[0], other_core(outs[1]), own))
        away = other_core(away)
    elif cores == 2:
        own, away = outs[0], other_core(outs[1])
        over = own
    else:
        turned = jnp.roll(outs[0], column, 1)
        own = lax.psum_scatter(turned, "rep", scatter_dimension=1, tiled=True)
        away = over = jnp.zeros_like(own)
    acts = [value, meta, coef, pg, pu]
    ggp, gup, hg, *held, proj, ggp_here, gup_here, hg_here = backward(
        stem, gain, inner, outer, acts, cots, experts
    )
    terms = to_image(place, proj, sel, stem, cot, paired, width, channels)
    terms_over = other_shard(terms[1]) if paired else terms[0]
    if cores == 2:
        far = far_grads(normed, ggp_here, gup_here, hg_here, cots[1])
        away_grads = [other_core(f) for f in far]

    after = far[0] if cores == 2 else own
    sent = pack_back(own, away, over, terms[0], terms_over, after, paired)
    back = exchange(sent)

    if cores == 2:
        grads = near_grads(place, kept, ggp, gup, hg, held[0], sent)
        *grads, done = fill(place, away_grads, grads)
    else:
        done = jnp.zeros((8, LANES), F32)
        size = gate_weight.shape[1] // cores
        grads = gathered_grads(column, size, kept, ggp, gup, hg, held[0])
    grad_gate, grad_up, grad_down = grads

    mixed, lat_sum = mix(own_stem, taken, back, done, channels)
    if cores == 2:
        mixed, grad_latent = join(
            place, mixed, other_core(mixed), lat_sum, other_core(lat_sum), rows_here
        )
    else:
        mixed = lax.all_gather(mixed, "rep", axis=1, tiled=True)
        lat_sum = lax.psum(lat_sum, "rep")
        grad_latent = lat_sum.reshape(channels, rows_here, width).transpose(1, 0, 2)
    return (mixed, grad_latent, grad_gate, grad_up, grad_down)


def solution(mesh):
    return jax.shard_map(
        local,
        mesh=mesh,
        in_specs=(
            P("exp", None, None),
            P(),
            P(),
            P(),
            P("exp", None),
            P("rep", "exp"),
            P("rep", "exp"),
            P("exp", "rep"),
            P("exp", None),
        ),
        out_specs=(
            P("exp", None),
            P("exp", None, None),
            P("rep", "exp"),
            P("rep", "exp"),
            P("exp", "rep"),
        ),
        check_vma=False,
    )
```

```python
import functools

import jax
import jax.numpy as jnp
from jax import lax
from jax.experimental import pallas as pl
from jax.experimental.pallas import tpu as pltpu
from jax.sharding import PartitionSpec as P

CAP = 40
LANES = 128
GROUP = 16
FORWARD_FLOPS = 100_000_000_000
F32 = jnp.float32
BF16 = jnp.bfloat16
MIB = 1024 * 1024


def dot(a, b, contract, batch=((), ())):
    return lax.dot_general(a, b, (contract, batch), preferred_element_type=F32)


def mm(a, b):
    return dot(a, b, ((1,), (0,)))


def mm_t(a, b):
    return dot(a, b, ((1,), (1,)))


def t_mm(a, b):
    return dot(a, b, ((0,), (0,)))


def call(kernel, flops, moved, mib=12, **kw):
    return pl.pallas_call(
        kernel,
        compiler_params=pltpu.CompilerParams(vmem_limit_bytes=mib * MIB),
        cost_estimate=pl.CostEstimate(flops=flops, bytes_accessed=moved, transcendentals=0),
        **kw,
    )


def whole(shape):
    return pl.BlockSpec(shape, lambda *_: (0,) * len(shape))


def rows(count, columns, at=0):
    return pl.BlockSpec((count, columns), lambda g, *_: (g, at))


def shape_of(shape, dtype):
    return jax.ShapeDtypeStruct(shape, dtype)


def lane_column(shape, width):
    return lax.broadcasted_iota(jnp.int32, shape, 1) % width


def shifted(window, shift, start, count):
    size = window.shape[1]
    return pltpu.roll(window, (-shift) % size, 1)[:, start : start + count]


def other_core(values):
    return lax.ppermute(values, "rep", [(0, 1), (1, 0)])


def other_shard(values):
    return lax.ppermute(values, "exp", [(i, i ^ 1) for i in range(lax.axis_size("exp"))])


def exchange(values):
    count = lax.axis_size("exp")
    shards = count // values.shape[0]
    groups = None
    if shards > 1:
        groups = [[s + shards * e for e in range(values.shape[0])] for s in range(shards)]
    return lax.all_to_all(
        values, "exp", split_axis=0, concat_axis=0, tiled=True, axis_index_groups=groups
    )


def hbm():
    return pl.BlockSpec(memory_space=pl.ANY)


def vmem():
    return pl.BlockSpec(memory_space=pltpu.VMEM)


def fast(shape, dtype):
    return pltpu.VMEM(shape, dtype)


def near(values):
    return pltpu.with_memory_space_constraint(values, pltpu.VMEM)


def far_off(values):
    return pltpu.with_memory_space_constraint(values, pltpu.HBM)


def kernel_call(kernel, flops, moved, operands, outs, name, mib=12, place=None, steps=1, scratch=(), specs=None, out_specs=None):
    specs = specs or [vmem() for _ in operands]
    out_specs = out_specs or [vmem() for _ in outs]
    return call(
        kernel,
        flops,
        moved,
        mib,
        grid_spec=pltpu.PrefetchScalarGridSpec(
            num_scalar_prefetch=0 if place is None else 1,
            grid=(steps,),
            in_specs=specs,
            out_specs=out_specs,
            scratch_shapes=list(scratch),
        ),
        out_shape=outs,
        name=name,
    )(*(() if place is None else (place,)), *operands)


def tiles_of(columns):
    return -(-columns // LANES)


def stacked(values):
    columns = values.shape[1]
    spare = tiles_of(columns) * LANES - columns
    if spare:
        values = jnp.concatenate([values, jnp.zeros((values.shape[0], spare), F32)], axis=1)
    parts = [values[:, k * LANES : (k + 1) * LANES] for k in range(tiles_of(columns))]
    return jnp.concatenate(parts, axis=0)


def own_selection(routes, experts):
    tok = routes.shape[1]
    expert = lax.broadcasted_iota(jnp.int32, (experts, tok), 0).astype(F32)
    named = jnp.where((expert == routes[0:1]) | (expert == routes[1:2]), 1.0, 0.0)
    first = lax.broadcasted_iota(jnp.int32, (tok, tok), 0)
    second = lax.broadcasted_iota(jnp.int32, (tok, tok), 1)
    before = jnp.where(first <= second, 1.0, 0.0).astype(BF16)
    at = mm(named.astype(BF16), before) - 1.0
    slot = lax.broadcasted_iota(jnp.int32, (CAP, tok), 0).astype(F32)
    return [
        jnp.where((at[e : e + 1] == slot) & (named[e : e + 1] > 0.0), 1.0, 0.0)
        for e in range(experts)
    ]


def own_columns(cot, half):
    if cot.shape[1] == half:
        return cot
    return jnp.where(lax.axis_index("rep") == 0, cot[:, :half], cot[:, half:])


def pack_kernel(shards, half, latent_ref, routes_ref, cot_ref, out_ref, held, sem):
    rows_here = latent_ref.shape[0]
    experts = held.shape[0]
    cells = jnp.concatenate([latent_ref[r].astype(F32) for r in range(rows_here)], axis=1)
    routes = routes_ref[...].astype(F32)
    payload = jnp.concatenate([cells, routes], axis=0)
    sel = own_selection(routes, experts)
    cot = own_columns(cot_ref[...], half)
    cots = mm(jnp.concatenate(sel, axis=0).astype(BF16), cot)
    copies = []
    for e in range(experts):
        slots = stacked(cots[e * CAP : (e + 1) * CAP])
        held[e] = jnp.concatenate([slots, payload], axis=0).astype(BF16)
        for n in range(shards):
            block = e * shards + n
            copies.append(pltpu.make_async_copy(held.at[e], out_ref.at[block], sem.at[block]))
            copies[-1].start()
    for copy in copies:
        copy.wait()


def pack(latent, routes_t, cot, experts, shards, half):
    rows_here, channels, width = latent.shape
    top, tok = routes_t.shape
    blocks = experts * shards
    depth = tiles_of(half) * CAP + channels + top
    operands = [latent, routes_t, cot]
    return kernel_call(
        functools.partial(pack_kernel, shards, half),
        2 * blocks * CAP * tok * half,
        4 * blocks * depth * LANES,
        [far_off(a) for a in operands],
        [pltpu.HBM((blocks, depth, LANES), BF16)],
        "pack",
        specs=[whole(a.shape) for a in operands],
        out_specs=[hbm()],
        scratch=[pltpu.VMEM((experts, depth, LANES), BF16), pltpu.SemaphoreType.DMA((blocks,))],
    )[0]


def unpacked(ref, columns):
    tiles = tiles_of(columns)
    blocks = ref.shape[0]
    held = [ref[b, : tiles * CAP, :].astype(F32) for b in range(blocks)]
    parts = [
        jnp.concatenate([one[k * CAP : (k + 1) * CAP] for one in held], axis=0)
        for k in range(tiles)
    ]
    return jnp.concatenate(parts, axis=1)[:, :columns]


def unpack_kernel(packed_ref, after_ref, cot_ref, image_ref):
    cot_ref[...] = unpacked(packed_ref, cot_ref.shape[1]).astype(BF16)
    top = packed_ref.shape[1] - image_ref.shape[1]
    for b in range(packed_ref.shape[0]):
        image_ref[b] = packed_ref[b, top:, :]


def unpack(packed, half, lines, after):
    blocks, _, tok = packed.shape
    return kernel_call(
        unpack_kernel,
        100_000_000_000,
        4 * packed.size,
        [near(packed), far_off(after)],
        [fast((blocks * CAP, half), BF16), fast((blocks, lines, tok), BF16)],
        "unpack",
        specs=[vmem(), hbm()],
    )


def weave_kernel(place_ref, same_ref, other_ref, after_ref, then_ref, out_ref):
    even = (place_ref[1] & 1) == 0
    for e in range(same_ref.shape[0]):
        same, other = same_ref[e], other_ref[e]
        out_ref[2 * e] = jnp.where(even, same, other)
        out_ref[2 * e + 1] = jnp.where(even, other, same)


def weave(place, same, other, after, then):
    shape = (2 * same.shape[0],) + same.shape[1:]
    return kernel_call(
        weave_kernel,
        0,
        8 * same.size,
        [near(same), near(other), near(after), near(then)],
        [fast(shape, same.dtype)],
        "weave",
        place=place,
    )[0]


def sum_kernel(a_ref, b_ref, after_ref, out_ref):
    out_ref[...] = (a_ref[...].astype(F32) + b_ref[...].astype(F32)).astype(out_ref.dtype)


def add_up(a, b, after):
    operands = [near(a), near(b), near(after)]
    outs = [fast(a.shape, a.dtype)]
    return kernel_call(sum_kernel, a.size, 6 * a.size, operands, outs, "add_up")[0]


def pack_back_kernel(paired, a_ref, b_ref, c_ref, terms_ref, over_ref, after_ref, out_ref):
    total = a_ref[...].astype(F32) + b_ref[...].astype(F32)
    if paired:
        total = total + c_ref[...].astype(F32)
    for b in range(out_ref.shape[0]):
        slots = stacked(total[b * CAP : (b + 1) * CAP])
        terms = terms_ref[b]
        if paired:
            terms = terms + over_ref[b].astype(F32)
        out_ref[b] = jnp.concatenate([slots, terms], axis=0).astype(BF16)


def pack_back(a, b, c, terms, over, after, paired):
    blocks, channels, tok = terms.shape
    depth = tiles_of(a.shape[1]) * CAP + channels
    return kernel_call(
        functools.partial(pack_back_kernel, paired),
        a.size,
        8 * a.size,
        [near(x) for x in (a, b, c, terms, over, after)],
        [shape_of((blocks, depth, LANES), BF16)],
        "pack_back",
    )[0]


PIECES = 4


def pieces(source, target, sem, at=0):
    deep = source.shape[0] // PIECES
    bands = [pl.ds(k * deep, deep) for k in range(PIECES)]
    return [
        pltpu.make_async_copy(source.at[band, :], target.at[band, :], sem.at[at + k])
        for k, band in enumerate(bands)
    ]


def far_kernel(place_ref, gate_ref, up_ref, down_ref, after_ref, gate_out, up_out, down_out, sem):
    size = gate_out.shape[1]
    at = pl.multiple_of((1 - place_ref[2]) * size, LANES)
    copies = (
        pieces(gate_ref.at[:, pl.ds(at, size)], gate_out, sem)
        + pieces(up_ref.at[:, pl.ds(at, size)], up_out, sem, PIECES)
        + pieces(down_ref.at[pl.ds(at, size), :], down_out, sem, 2 * PIECES)
    )
    for copy in copies:
        copy.start()
    for copy in copies:
        copy.wait()


def far_weights(place, gate, up, down, after):
    half, hid = gate.shape
    size = hid // 2
    return kernel_call(
        far_kernel,
        0,
        LANES,
        [far_off(gate), far_off(up), far_off(down), far_off(after)],
        [fast((half, size), BF16), fast((half, size), BF16), fast((size, half), BF16)],
        "far_weights",
        place=place,
        specs=[hbm()] * 4,
        scratch=[pltpu.SemaphoreType.DMA((3 * PIECES,))],
    )


def cuts(lengths):
    start, out = 0, []
    for n in lengths:
        out.append((start, n))
        start += n
    return out


def params_kernel(
    turn, experts, shards, place_ref, stem_in, gain_in, router_in, routes_ref, cot_ref, after,
    stem, gain, router, taken, cot,
):
    wide = router_in[...].astype(F32)
    model = wide.shape[0]
    blank = jnp.zeros((model, LANES - 2 * experts), F32)
    wide = jnp.concatenate([wide, wide, blank], axis=1)
    values, gains = stem_in[...], gain_in[...]
    if turn:
        half = model // 2
        first = place_ref[2] == 0
        wide = jnp.where(first, wide, jnp.concatenate([wide[half:], wide[:half]], axis=0))
        turned = jnp.concatenate([values[:, half:], values[:, :half]], axis=1)
        values = jnp.where(first, values, turned)
        turned = jnp.concatenate([gains[:, half:], gains[:, :half]], axis=1)
        gains = jnp.where(first, gains, turned)
    stem[...] = values
    gain[...] = gains
    router[...] = wide.astype(BF16)
    sel = own_selection(routes_ref[...].astype(F32), experts)
    taken[...] = jnp.concatenate([one for one in sel for _ in range(shards)], axis=0).astype(BF16)
    cot[...] = own_columns(cot_ref[...], cot.shape[1])


def small_params(place, stem, gain, router, routes_t, cot, half, shards, after, turn):
    model, experts = router.shape
    tok = cot.shape[0]
    small = [far_off(a) for a in (stem, gain, router, routes_t, cot)]
    shapes = [(stem.shape, BF16), (gain.shape, F32), ((model, LANES), BF16)]
    shapes += [((experts * shards * CAP, tok), BF16), ((tok, half), BF16)]
    return kernel_call(
        functools.partial(params_kernel, turn, experts, shards),
        0,
        LANES,
        small + [far_off(after)],
        [pltpu.HBM(*a) for a in shapes],
        "params",
        place=place,
        specs=[whole(a.shape) for a in small] + [hbm()],
        out_specs=[whole(shape) for shape, _ in shapes],
    )


def inner_copies(place_ref, refs, inner, size, at, sem):
    copies = []
    for n, (ref, (a, depth)) in enumerate(zip(refs, cuts([r.shape[0] for r in refs]))):
        if ref.shape[1] != size:
            ref = ref.at[:, pl.ds(pl.multiple_of(place_ref[2] * size, LANES), size)]
        copies += pieces(ref, inner.at[pl.ds(a, depth), pl.ds(at, size)], sem, n * PIECES)
    return copies


def outer_copies(place_ref, refs, outer, sem):
    copies = []
    size = outer.shape[0]
    for n, (ref, (a, depth)) in enumerate(zip(refs, cuts([r.shape[1] for r in refs]))):
        if ref.shape[0] != size:
            ref = ref.at[pl.ds(pl.multiple_of(place_ref[2] * size, LANES), size), :]
        copies += pieces(ref, outer.at[:, pl.ds(a, depth)], sem, n * PIECES)
    return copies


def gather_kernel(parts, place_ref, *refs):
    gates, (stem_in, gain_in, router_in) = refs[:parts], refs[parts : parts + 3]
    stem, gain, inner, small_sem, sem = refs[parts + 3 :]
    size = (inner.shape[1] - LANES) // 2
    copies = [
        pltpu.make_async_copy(stem_in, stem, small_sem.at[0]),
        pltpu.make_async_copy(gain_in, gain, small_sem.at[1]),
        pltpu.make_async_copy(router_in, inner.at[:, pl.ds(2 * size, LANES)], small_sem.at[2]),
    ]
    copies += inner_copies(place_ref, gates, inner, size, 0, sem)
    for copy in copies:
        copy.start()
    for copy in copies:
        copy.wait()


def gather(place, small, gates, size):
    stem, gain, router = small
    model = router.shape[0]
    operands = [far_off(a) for a in list(gates) + list(small)]
    return kernel_call(
        functools.partial(gather_kernel, len(gates)),
        0,
        LANES,
        operands,
        [
            fast(stem.shape, BF16),
            fast(gain.shape, F32),
            fast((model, 2 * size + LANES), BF16),
        ],
        "gather",
        place=place,
        specs=[hbm()] * len(operands),
        scratch=[
            pltpu.SemaphoreType.DMA((3,)),
            pltpu.SemaphoreType.DMA((len(gates) * PIECES,)),
        ],
    )


def join_kernel(place_ref, own_ref, away_ref, a_ref, b_ref, out_ref, latent_ref):
    half = own_ref.shape[1]
    first = place_ref[2] == 0
    own, away = own_ref[...], away_ref[...]
    out_ref[:, :half] = jnp.where(first, own, away)
    out_ref[:, half:] = jnp.where(first, away, own)
    total = a_ref[...] + b_ref[...]
    width = latent_ref.shape[2]
    for r in range(latent_ref.shape[0]):
        latent_ref[r] = total[:, r * width : (r + 1) * width]


def join(place, own, away, a, b, rows_here):
    count, half = own.shape
    channels, tok = a.shape
    return kernel_call(
        join_kernel,
        0,
        8 * count * half,
        [near(own), near(away), near(a), near(b)],
        [
            shape_of((count, 2 * half), BF16),
            shape_of((rows_here, channels, tok // rows_here), F32),
        ],
        "join",
        place=place,
    )


def pair_selection(named):
    lanes = named.shape[1]
    tok = lanes // 2
    first = lax.broadcasted_iota(jnp.int32, (lanes, lanes), 0)
    second = lax.broadcasted_iota(jnp.int32, (lanes, lanes), 1)
    before = ((first <= second) & (first // tok == second // tok)).astype(F32).astype(BF16)
    wide = jnp.broadcast_to(named, (8, lanes)).astype(BF16)
    place = mm(wide, before)[:1]
    lane = lax.broadcasted_iota(jnp.int32, (1, lanes), 1)
    place = place - 1.0 + jnp.where(lane >= tok, float(CAP), 0.0)
    slot = lax.broadcasted_iota(jnp.int32, (2 * CAP, lanes), 0).astype(F32)
    return jnp.where((place == slot) & (named > 0.0), 1.0, 0.0)


def pair_patches(image_ref, top, first, width, channels):
    blocks = image_ref.shape[0]
    before = image_ref[jnp.maximum(first - 1, 0), top : top + channels, :].astype(F32)
    after = image_ref[jnp.minimum(first + 2, blocks - 1), top : top + channels, :].astype(F32)
    window = jnp.concatenate(
        [
            jnp.where(first > 0, before, 0.0),
            image_ref[first, top : top + channels, :].astype(F32),
            image_ref[first + 1, top : top + channels, :].astype(F32),
            jnp.where(first + 2 < blocks, after, 0.0),
        ],
        axis=1,
    )
    tok = image_ref.shape[2]
    column = lane_column((channels, 2 * tok), width)
    pieces = []
    for i in range(3):
        for j in range(3):
            piece = shifted(window, (i - 1) * width + j - 1, tok, 2 * tok)
            source = column + (j - 1)
            pieces.append(jnp.where((source >= 0) & (source < width), piece, 0.0))
    return jnp.concatenate(pieces, axis=0)


def by_side(pairs, even):
    same = [jnp.where(even, p[:CAP], p[CAP:]) for p in pairs]
    other = [jnp.where(even, p[CAP:], p[:CAP]) for p in pairs]
    return same + other


def forward_kernel(
    paired, parts, width, experts, outs, place_ref, image_ref, stem_ref, gain_ref, _, *refs
):
    weights, refs = refs[: 2 * parts], refs[2 * parts :]
    saved_ref, own_out, normed_ref, value_ref, meta_ref, coef_ref, sel_ref, pg_ref, pu_ref = refs[:9]
    hidden_ref, inner, outer, *out_refs = refs[9:-4]
    own_ref, save_sem, up_sem, down_sem = refs[-4:]
    step = pl.program_id(0)
    size = outer.shape[0]
    up_copies = inner_copies(place_ref, weights[:parts], inner, size, size, up_sem)
    down_copies = outer_copies(place_ref, weights[parts:], outer, down_sem)

    def arrive(copies):
        @pl.when(step == 0)
        def _():
            for copy in copies:
                copy.wait()

    @pl.when(step == 0)
    def _():
        for copy in up_copies + down_copies:
            copy.start()

    chunk = GROUP * CAP
    here = pl.ds(pl.multiple_of(step * chunk, chunk), chunk)
    top = 0
    channels = image_ref.shape[1] - 2
    mine = place_ref[0].astype(F32)
    even = (place_ref[1] & 1) == 0
    taken, others = [], []
    for q in range(GROUP // 2):
        first = step * GROUP + 2 * q
        lines = [image_ref[first + n, top + channels :, :].astype(F32) for n in range(2)]
        named_by = [jnp.concatenate([line[k : k + 1] for line in lines], axis=1) for k in range(2)]
        named = jnp.where((named_by[0] == mine) | (named_by[1] == mine), 1.0, 0.0)
        sel = pair_selection(named)
        sel_ref[step * (GROUP // 2) + q] = sel.astype(BF16)
        other = named_by[0] + named_by[1] - mine
        others.append(jnp.sum(sel * other, axis=1, keepdims=True))
        patches = pair_patches(image_ref, top, first, width, channels)
        taken.append(mm_t(sel.astype(BF16), patches.astype(BF16)))
    bands = 2 if paired else 1
    deep = chunk // bands
    lines = [pl.ds(pl.multiple_of(step * chunk + k * deep, deep), deep) for k in range(bands)]
    held = [slice(k * deep, (k + 1) * deep) for k in range(bands)]
    if paired:
        taken, others = by_side(taken, even), by_side(others, even)
    each = len(taken) // bands
    patches = [
        jnp.concatenate(taken[k * each : (k + 1) * each], axis=0).astype(BF16) for k in range(bands)
    ]
    others = [jnp.concatenate(others[k * each : (k + 1) * each], axis=0) for k in range(bands)]
    stems = [mm(one, stem_ref[...]).astype(BF16) for one in patches]
    normeds, scales, gates, gated, upped, hiddens = [], [], [], [], [], []
    for line, band, stem in zip(lines, held, stems):
        value_ref[line, :] = stem
        value = stem.astype(F32)
        scale = lax.rsqrt(jnp.mean(value * value, axis=-1, keepdims=True) + 1e-06)
        normed = (value * scale * gain_ref[...]).astype(BF16)
        normed_ref[band, :] = normed
        normeds.append(normed)
        scales.append(scale)
    own_part = normed_ref.at[:, pl.ds(0, saved_ref.shape[1])]
    save = pltpu.make_async_copy(own_part, saved_ref.at[here, :], save_sem.at[0])
    save.start()
    own_save = pltpu.make_async_copy(own_ref, own_out, save_sem.at[1])

    @pl.when(step == 0)
    def _():
        me = place_ref[1]
        first = me // 2 * 2
        tok = image_ref.shape[2]
        own = pair_patches(image_ref, top, first, width, channels)
        own = jnp.where(me == first, own[:, :tok], own[:, tok:]).astype(BF16)
        own_ref[...] = t_mm(own, stem_ref[:, : own_ref.shape[1]]).astype(BF16)
        own_save.start()

    for normed in normeds:
        gated.append(mm(normed, inner[:, :size]))
    for line, normed, other, scale in zip(lines, normeds, others, scales):
        logits = mm(normed, inner[:, 2 * size :])
        lane = lax.broadcasted_iota(jnp.int32, logits.shape, 1)
        again = jnp.where(lane >= experts, lane - experts, lane).astype(F32)
        lane = lane.astype(F32)
        mine_logit = jnp.sum(jnp.where(lane == mine, logits, 0.0), axis=1, keepdims=True)
        other_logit = jnp.sum(jnp.where(lane == other, logits, 0.0), axis=1, keepdims=True)
        sig_mine, sig_other = jax.nn.sigmoid(mine_logit), jax.nn.sigmoid(other_logit)
        gate = sig_mine / (sig_mine + sig_other)
        rest = sig_other / (sig_mine + sig_other)
        both = gate * rest
        coef_ref[line, :] = jnp.where(again == mine, both * (1.0 - sig_mine), 0.0) - jnp.where(
            again == other, both * (1.0 - sig_other), 0.0
        )
        meta_ref[line, :] = jnp.where(lane == 0.0, gate, scale)
        gates.append(gate)
    arrive(up_copies)
    for normed in normeds:
        upped.append(mm(normed, inner[:, size : 2 * size]))
    arrive(down_copies)
    for line, pre_gate, pre_up in zip(lines, gated, upped):
        pg_ref[line, :] = pre_gate.astype(BF16)
        pu_ref[line, :] = pre_up.astype(BF16)
        hidden = (pre_gate * jax.nn.sigmoid(pre_gate) * pre_up).astype(BF16)
        hidden_ref[line, :] = hidden
        hiddens.append(hidden)
    for ref, (a, n) in zip(out_refs, cuts([r.shape[1] for r in out_refs])):
        part = (gates[-1] * mm(hiddens[-1], outer[:, a : a + n])).astype(BF16)
        if paired:
            ref[...] = part
        else:
            ref[here, :] = part
    save.wait()

    @pl.when(step == 0)
    def _():
        own_save.wait()


def forward(place, image, gathered, weights, size, half, columns, paired, width, experts):
    blocks, _, tok = image.shape
    slots, chunk = blocks * CAP, GROUP * CAP
    stem, gain, inner = gathered
    model = stem.shape[1]
    parts = len(weights) // 2
    operands = [near(image), near(stem), near(gain), near(inner)] + [far_off(w) for w in weights]
    outs = [
        pltpu.HBM((slots, columns[0]), BF16),
        pltpu.HBM((tok, half), BF16),
        fast((chunk, model), BF16),
        fast((slots, model), BF16),
        fast((slots, LANES), F32),
        fast((slots, LANES), F32),
        fast((blocks // 2, 2 * CAP, 2 * tok), BF16),
        fast((slots, size), BF16),
        fast((slots, size), BF16),
        fast((slots, size), BF16),
        fast(inner.shape, BF16),
        fast((size, model), BF16),
    ]
    outs += [fast((slots // 2 if paired else slots, n), BF16) for n in columns]
    return pl.pallas_call(
        functools.partial(forward_kernel, paired, parts, width, experts, columns),
        compiler_params=pltpu.CompilerParams(vmem_limit_bytes=20 * MIB),
        cost_estimate=pl.CostEstimate(
            flops=FORWARD_FLOPS, bytes_accessed=LANES, transcendentals=0
        ),
        grid_spec=pltpu.PrefetchScalarGridSpec(
            num_scalar_prefetch=1,
            grid=(blocks // GROUP,),
            in_specs=[vmem()] * 4 + [hbm()] * len(weights),
            out_specs=[hbm()] * 2 + [vmem()] * (len(outs) - 2),
            scratch_shapes=[
                pltpu.VMEM((tok, half), BF16),
                pltpu.SemaphoreType.DMA((2,)),
                pltpu.SemaphoreType.DMA((parts * PIECES,)),
                pltpu.SemaphoreType.DMA((parts * PIECES,)),
            ],
        ),
        out_shape=outs,
        input_output_aliases={4: 10},
        name="forward",
    )(place, *operands)


def outputs_kernel(meta_ref, hidden_ref, outer, near_ref, far_ref):
    count, half = near_ref.shape
    gate = meta_ref[:count, 0:1]
    hidden = hidden_ref[:count, :]
    near_ref[...] = (gate * mm(hidden, outer[:, :half])).astype(BF16)
    far_ref[...] = (gate * mm(hidden, outer[:, half:])).astype(BF16)


def outputs(meta, hidden, outer):
    count, half = hidden.shape[0] // 2, outer.shape[1] // 2
    return kernel_call(
        outputs_kernel,
        0,
        LANES,
        [near(meta), near(hidden), near(outer)],
        [fast((count, half), BF16)] * 2,
        "outputs",
    )


def backward_kernel(
    parts, bands, experts, stem_ref, gain_ref, inner, outer, value_ref, meta_ref, coef_ref, pg_ref, pu_ref,
    *refs,
):
    cot_refs, refs = refs[: parts * bands], refs[parts * bands :]
    saved, refs = refs[:4], refs[4:]
    proj_ref, ggp_ref, gup_ref, hg_ref, sem = refs
    step = pl.program_id(0)
    model = stem_ref.shape[1]
    chunk = GROUP * CAP
    here = pl.ds(pl.multiple_of(step * chunk, chunk), chunk)
    sources = [ggp_ref, gup_ref, hg_ref]
    targets = [ref.at[here, :] for ref in saved[:3]]
    for n, ref in enumerate(cot_refs[:bands]):
        if bands == 1:
            sources.append(ref.at[here, :])
            targets.append(saved[3].at[here, :])
        else:
            sources.append(ref)
            targets.append(saved[3].at[pl.ds(n * ref.shape[0], ref.shape[0]), :])
    saves = [
        pltpu.make_async_copy(a, b, sem.at[n]) for n, (a, b) in enumerate(zip(sources, targets))
    ]
    for save in saves[3:]:
        save.start()
    deep = chunk // bands
    places = cuts([r.shape[1] for r in cot_refs[::bands]])
    lines = [pl.ds(pl.multiple_of(step * chunk + k * deep, deep), deep) for k in range(bands)]
    held = [slice(k * deep, (k + 1) * deep) for k in range(bands)]
    gates = [meta_ref[line, 0:1] for line in lines]
    scales = [meta_ref[line, 1:2] for line in lines]
    raws, mixes, backs, grads = [], [], [], []
    for k, line in enumerate(lines):
        raw = 0.0
        for n, (a, m) in enumerate(places):
            cot = cot_refs[n * bands + k][...] if bands > 1 else cot_refs[n][line, :]
            raw = raw + mm_t(cot, outer[:, a : a + m])
        raws.append(raw)
    for line, band, gate, raw in zip(lines, held, gates, raws):
        pre_gate = pg_ref[line, :].astype(F32)
        pre_up = pu_ref[line, :].astype(F32)
        sigma = jax.nn.sigmoid(pre_gate)
        silu = pre_gate * sigma
        hidden = silu * pre_up
        grad_gates = jnp.sum(raw * hidden, axis=1, keepdims=True)
        hg_ref[band, :] = (gate * hidden).astype(BF16)
        grad_hidden = gate * raw
        ggp = (grad_hidden * pre_up * sigma * (1.0 + pre_gate - silu)).astype(BF16)
        gup = (grad_hidden * silu).astype(BF16)
        ggp_ref[band, :] = ggp
        gup_ref[band, :] = gup
        grad_logits = grad_gates * coef_ref[line, :]
        high = grad_logits.astype(BF16)
        low = (grad_logits - high.astype(F32)).astype(BF16)
        lane = lax.broadcasted_iota(jnp.int32, grad_logits.shape, 1)
        mix = jnp.where(lane < experts, high.astype(F32), low.astype(F32)).astype(BF16)
        mixes.append(jnp.concatenate([ggp, gup, mix], axis=1))
    for save in saves[:3]:
        save.start()
    for mix in mixes:
        backs.append(mm_t(mix, inner[...]))
    for line, scale, back in zip(lines, scales, backs):
        back = back * gain_ref[...]
        value = value_ref[line, :].astype(F32)
        along = jnp.sum(back * value, axis=1, keepdims=True) * (scale * scale * scale) / model
        grads.append((scale * back - along * value).astype(BF16))
    for line, grad in zip(lines, grads):
        proj_ref[line, :] = mm_t(grad, stem_ref[...]).astype(BF16)
    for save in saves:
        save.wait()


def backward(stem, gain, inner, outer, acts, cots, experts):
    slots, model = acts[0].shape
    size, chunk = outer.shape[0], GROUP * CAP
    taps = stem.shape[0]
    parts, bands = len(cots), len(cots[0])
    operands = [stem, gain, inner, outer] + list(acts) + [c for part in cots for c in part]
    return kernel_call(
        functools.partial(backward_kernel, parts, bands, experts),
        2 * slots * model * size * 4,
        slots * (4 * model + 12 * size) + 6 * model * size,
        [near(a) for a in operands],
        [pltpu.HBM((slots, size), BF16)] * 3
        + [pltpu.HBM((slots, cots[0][0].shape[1]), BF16)]
        + [fast((slots, taps), BF16)]
        + [fast((chunk, size), BF16)] * 3,
        "backward",
        mib=20,
        steps=slots // chunk,
        out_specs=[hbm()] * 4 + [vmem()] * 4,
        scratch=[pltpu.SemaphoreType.DMA((3 + bands,))],
    )


def image_kernel(paired, width, place_ref, proj_ref, sel_ref, stem_ref, cot_ref, *refs):
    out_refs, terms = refs[:-1], refs[-1]
    pairs = sel_ref.shape[0]
    tok = cot_ref.shape[0]
    channels = out_refs[0].shape[1]
    count = 2 * pairs * tok
    own = mm_t(stem_ref[:, : cot_ref.shape[1]], cot_ref[...])
    me = place_ref[1]
    even = (me & 1) == 0
    proj = proj_ref[...].astype(F32)
    for q in range(pairs):
        if paired:
            same = proj[CAP * q : CAP * (q + 1)]
            other = proj[CAP * (pairs + q) : CAP * (pairs + q + 1)]
            both = [jnp.where(even, same, other), jnp.where(even, other, same)]
            pair = jnp.concatenate(both, axis=0)
        else:
            pair = proj[2 * CAP * q : 2 * CAP * (q + 1)]
        block = t_mm(pair.astype(BF16), sel_ref[q])
        terms[:, 2 * q * tok : (2 * q + 1) * tok] = block[:, :tok] + jnp.where(2 * q == me, own, 0.0)
        terms[:, (2 * q + 1) * tok : (2 * q + 2) * tok] = block[:, tok:] + jnp.where(
            2 * q + 1 == me, own, 0.0
        )
    lane = lax.broadcasted_iota(jnp.int32, (channels, count), 1)
    total = jnp.zeros((channels, count), F32)
    for i in range(3):
        for j in range(3):
            k = (3 * i + j) * channels
            shift = (i - 1) * width + j - 1
            piece = pltpu.roll(terms[k : k + channels, :], shift % count, 1)
            column = lane % width + (1 - j)
            token = lane - shift
            keep = (column >= 0) & (column < width) & (token >= 0) & (token < count)
            total = total + jnp.where(keep, piece, 0.0)
    for q in range(pairs):
        low = total[:, 2 * q * tok : (2 * q + 1) * tok]
        high = total[:, (2 * q + 1) * tok : (2 * q + 2) * tok]
        if paired:
            out_refs[0][q] = jnp.where(even, low, high)
            out_refs[1][q] = jnp.where(even, high, low).astype(BF16)
        else:
            out_refs[0][2 * q] = low
            out_refs[0][2 * q + 1] = high


def to_image(place, proj, sel, stem, cot, paired, width, channels):
    pairs = sel.shape[0]
    blocks, tok = 2 * pairs, cot.shape[0]
    taps, half = stem.shape[0], cot.shape[1]
    return kernel_call(
        functools.partial(image_kernel, paired, width),
        2 * proj.shape[0] * 2 * tok * taps,
        4 * taps * blocks * tok,
        [near(a) for a in (proj, sel, stem, cot)],
        [fast((pairs, channels, tok), F32), fast((pairs, channels, tok), BF16)]
        if paired
        else [fast((blocks, channels, tok), F32)],
        "to_image",
        place=place,
        scratch=[pltpu.VMEM((taps, blocks * tok), F32)],
    )


def far_grads_kernel(normed, ggp, gup, hg, *refs):
    cots, (gate_out, up_out, down_out) = refs[:-3], refs[-3:]
    half = cots[0].shape[1]
    far = normed[:, half:]
    gate_out[...] = t_mm(far, ggp[...]).astype(BF16)
    up_out[...] = t_mm(far, gup[...]).astype(BF16)
    cot = jnp.concatenate([ref[...] for ref in cots], axis=0)
    down_out[...] = t_mm(hg[...], cot).astype(BF16)


def far_grads(normed, ggp, gup, hg, cots):
    slots, size = ggp.shape
    half = cots[0].shape[1]
    return kernel_call(
        far_grads_kernel,
        6 * slots * size * half,
        20 * slots * size,
        [near(a) for a in [normed, ggp, gup, hg] + list(cots)],
        [fast((half, size), BF16)] * 2 + [fast((size, half), BF16)],
        "far_grads",
    )


def near_grads_kernel(
    place_ref, normed, ggp, gup, hg, cot, after_ref, gate_out, up_out, down_out,
    left, right, own, sem, own_sem,
):
    half = cot.shape[1]
    size = ggp.shape[1]
    here = pl.multiple_of(place_ref[2] * size, LANES)
    sources = (normed, ggp, gup, hg, cot)
    targets = (left.at[0], right.at[0], right.at[1], left.at[1], right.at[2])
    loads = [pltpu.make_async_copy(a, b, sem.at[n]) for n, (a, b) in enumerate(zip(sources, targets))]
    places = (
        gate_out.at[:, pl.ds(here, size)],
        up_out.at[:, pl.ds(here, size)],
        down_out.at[pl.ds(here, size), :],
    )
    results = [pieces(own.at[n], a, own_sem, n * PIECES) for n, a in enumerate(places)]
    for load in loads:
        load.start()
    for load in loads[:2]:
        load.wait()
    own[0] = t_mm(left[0], right[0])
    for copy in results[0]:
        copy.start()
    loads[2].wait()
    own[1] = t_mm(left[0], right[1])
    for copy in results[1]:
        copy.start()
    loads[3].wait()
    loads[4].wait()
    own[2] = t_mm(left[1], right[2])
    for copy in results[2]:
        copy.start()
    for copy in results[0] + results[1] + results[2]:
        copy.wait()


def near_grads(place, normed, ggp, gup, hg, cot, after):
    slots, size = ggp.shape
    half = cot.shape[1]
    return kernel_call(
        near_grads_kernel,
        20_000_000_000,
        LANES,
        [far_off(a) for a in (normed, ggp, gup, hg, cot)] + [after],
        [pltpu.HBM((half, 2 * size), F32)] * 2
        + [pltpu.HBM((2 * size, half), F32)],
        "near_grads",
        mib=14,
        place=place,
        specs=[hbm()] * 6,
        out_specs=[hbm()] * 3,
        scratch=[
            pltpu.VMEM((2, slots, half), BF16),
            pltpu.VMEM((3, slots, half), BF16),
            pltpu.VMEM((3, half, size), F32),
            pltpu.SemaphoreType.DMA((5,)),
            pltpu.SemaphoreType.DMA((3 * PIECES,)),
        ],
    )


def fill_kernel(
    place_ref, gate_in, up_in, down_in, gate_old, up_old, down_old,
    gate_out, up_out, down_out, done_ref, away, wide, in_sem, sem,
):
    size = gate_in.shape[1]
    there = pl.multiple_of((1 - place_ref[2]) * size, LANES)
    places = (
        gate_out.at[:, pl.ds(there, size)],
        up_out.at[:, pl.ds(there, size)],
        down_out.at[pl.ds(there, size), :],
    )
    loads = [
        pieces(a, away.at[n], in_sem, n * PIECES) for n, a in enumerate((gate_in, up_in, down_in))
    ]
    results = [pieces(wide.at[n], a, sem, n * PIECES) for n, a in enumerate(places)]
    deep = wide.shape[1] // PIECES
    done_ref[...] = jnp.zeros(done_ref.shape, F32)
    for load in loads[0] + loads[1] + loads[2]:
        load.start()
    for n in range(3):
        for k in range(PIECES):
            loads[n][k].wait()
            wide[n, k * deep : (k + 1) * deep] = away[n, k * deep : (k + 1) * deep].astype(F32)
            results[n][k].start()
    for copy in results[0] + results[1] + results[2]:
        copy.wait()


def fill(place, away, grads):
    shape = away[0].shape
    return pl.pallas_call(
        fill_kernel,
        compiler_params=pltpu.CompilerParams(vmem_limit_bytes=12 * MIB),
        cost_estimate=pl.CostEstimate(
            flops=10_000_000_000, bytes_accessed=LANES, transcendentals=0
        ),
        grid_spec=pltpu.PrefetchScalarGridSpec(
            num_scalar_prefetch=1,
            grid=(1,),
            in_specs=[hbm()] * 6,
            out_specs=[hbm()] * 3 + [vmem()],
            scratch_shapes=[
                pltpu.VMEM((3,) + shape, BF16),
                pltpu.VMEM((3,) + shape, F32),
                pltpu.SemaphoreType.DMA((3 * PIECES,)),
                pltpu.SemaphoreType.DMA((3 * PIECES,)),
            ],
        ),
        out_shape=[pltpu.HBM(g.shape, F32) for g in grads] + [fast((8, LANES), F32)],
        input_output_aliases={4: 0, 5: 1, 6: 2},
        name="fill",
    )(place, *[far_off(a) for a in away], *grads)


def gathered_grads(column, size, normed, ggp, gup, hg, cot):
    grads = []
    for g in (ggp[:, :size], gup[:, :size]):
        term = jnp.roll(t_mm(normed, g).astype(BF16), column, 0)
        grads.append(lax.all_to_all(term, "rep", split_axis=0, concat_axis=1, tiled=True))
    term = jnp.roll(t_mm(hg[:, :size], cot).astype(BF16), column, 1)
    grads.append(lax.all_to_all(term, "rep", split_axis=1, concat_axis=0, tiled=True))
    return [g.astype(F32) for g in grads]


def mixed_kernel(stem_ref, taken_ref, back_ref, after_ref, out_ref, *terms_refs):
    half = out_ref.shape[1]
    back = unpacked(back_ref, half).astype(BF16)
    total = stem_ref[...].astype(F32) + t_mm(taken_ref[...], back)
    out_ref[...] = total.astype(BF16)
    top = tiles_of(half) * CAP
    terms = back_ref[0, top:, :].astype(F32)
    for b in range(1, back_ref.shape[0]):
        terms = terms + back_ref[b, top:, :].astype(F32)
    for n, ref in enumerate(terms_refs):
        ref[...] = terms[n * ref.shape[0] : (n + 1) * ref.shape[0]]


def mix(stem, taken, back, after, channels):
    tok, half = stem.shape
    sides = (back.shape[1] - tiles_of(half) * CAP) // channels
    return kernel_call(
        mixed_kernel,
        2 * taken.shape[0] * tok * half,
        2 * back.size,
        [near(a) for a in (stem, taken, back, after)],
        [fast((tok, half), BF16)] + [fast((channels, tok), F32)] * sides,
        "mixed",
    )


def local(
    latent,
    stem_weight,
    norm_gain,
    router_weight,
    routes,
    gate_weight,
    up_weight,
    down_weight,
    grad_mixed,
):
    rows_here, channels, width = latent.shape
    half = gate_weight.shape[0]
    experts = router_weight.shape[1]
    tok = rows_here * width
    blocks = lax.axis_size("exp")
    cores = lax.axis_size("rep")
    shards = blocks // experts
    slots = blocks * CAP
    me = lax.axis_index("exp")
    core = lax.axis_index("rep")
    column = core * half
    place = jnp.stack([me // shards, me, core]).astype(jnp.int32)

    paired = cores == 2 and shards == 2
    given = grad_mixed
    if cores != 2:
        given = lax.dynamic_slice_in_dim(grad_mixed, column, half, 1)
    copies = 1 if paired else shards
    routes_t = routes.T
    packed = pack(latent, routes_t, given, experts, copies, half)
    arrived = exchange(packed)

    stem, gain, router = stem_weight, norm_gain[None, :], router_weight
    if cores == 2:
        far = far_weights(place, gate_weight, up_weight, down_weight, packed)
        gate_parts, up_parts, down_parts = [
            (w, other_core(f)) for w, f in zip((gate_weight, up_weight, down_weight), far)
        ]
    else:
        turned = lax.all_to_all(gate_weight, "rep", split_axis=1, concat_axis=0, tiled=True)
        spare = -turned.shape[1] % LANES
        gate_parts = (jnp.pad(jnp.roll(turned, -column, 0), ((0, 0), (0, spare))),)
        turned = lax.all_to_all(up_weight, "rep", split_axis=1, concat_axis=0, tiled=True)
        up_parts = (jnp.pad(jnp.roll(turned, -column, 0), ((0, 0), (0, spare))),)
        turned = lax.all_to_all(down_weight, "rep", split_axis=0, concat_axis=1, tiled=True)
        down_parts = (jnp.pad(jnp.roll(turned, -column, 1), ((0, spare), (0, 0))),)
        stem = jnp.roll(stem, -column, 1)
        gain = jnp.roll(gain, -column, 1)
        router = jnp.roll(router, -column, 0)

    *small, taken, cot = small_params(
        place, stem, gain, router, routes_t, given, half, copies, packed, cores == 2
    )
    same_cot, image = unpack(arrived, half, channels + 2, small[1])
    size = down_parts[-1].shape[0]
    gathered = gather(place, small, gate_parts, size)
    if paired:
        joined = other_core(same_cot)
        image = weave(place, image, other_shard(image), joined, gathered[1])
        cots = [[same_cot], [joined]]
        far_cot = other_shard(same_cot)
    elif cores == 2:
        cots = [[same_cot], [other_core(same_cot)]]
    else:
        joined = lax.all_gather(same_cot, "rep", axis=1, tiled=True)
        cots = [[jnp.roll(joined, -column, 1)]]
    weights = list(up_parts) + list(down_parts)
    columns = [w.shape[1] for w in down_parts]
    kept, own_stem, normed, value, meta, coef, sel, pg, pu, hidden, inner, outer, *outs = forward(
        place, image, gathered, weights, size, half, columns, paired, width, experts
    )
    stem, gain, _ = gathered
    if paired:
        own, away = outputs(meta, hidden, outer)
        far_cot, own = lax.optimization_barrier((far_cot, own))
        cots[0].append(far_cot)
        cots[1].append(other_core(far_cot))
        over = other_shard(add_up(outs[0], other_core(outs[1]), own))
        away = other_core(away)
    elif cores == 2:
        own, away = outs[0], other_core(outs[1])
        over = own
    else:
        turned = jnp.roll(outs[0], column, 1)
        own = lax.psum_scatter(turned, "rep", scatter_dimension=1, tiled=True)
        away = over = jnp.zeros_like(own)
    acts = [value, meta, coef, pg, pu]
    ggp, gup, hg, held, proj, ggp_here, gup_here, hg_here = backward(
        stem, gain, inner, outer, acts, cots, experts
    )
    terms = to_image(place, proj, sel, stem, cot, paired, width, channels)
    terms_over = other_shard(terms[1]) if paired else terms[0]
    if cores == 2:
        far = far_grads(normed, ggp_here, gup_here, hg_here, cots[1])
        away_grads = [other_core(f) for f in far]

    after = far[0] if cores == 2 else own
    sent = pack_back(own, away, over, terms[0], terms_over, after, paired)
    back = exchange(sent)

    if cores == 2:
        grads = near_grads(place, kept, ggp, gup, hg, held, sent)
        *grads, done = fill(place, away_grads, grads)
    else:
        done = jnp.zeros((8, LANES), F32)
        size = gate_weight.shape[1] // cores
        grads = gathered_grads(column, size, kept, ggp, gup, hg, held)
    grad_gate, grad_up, grad_down = grads

    mixed, lat_sum = mix(own_stem, taken, back, done, channels)
    if cores == 2:
        mixed, grad_latent = join(
            place, mixed, other_core(mixed), lat_sum, other_core(lat_sum), rows_here
        )
    else:
        mixed = lax.all_gather(mixed, "rep", axis=1, tiled=True)
        lat_sum = lax.psum(lat_sum, "rep")
        grad_latent = lat_sum.reshape(channels, rows_here, width).transpose(1, 0, 2)
    return (mixed, grad_latent, grad_gate, grad_up, grad_down)


def solution(mesh):
    return jax.shard_map(
        local,
        mesh=mesh,
        in_specs=(
            P("exp", None, None),
            P(),
            P(),
            P(),
            P("exp", None),
            P("rep", "exp"),
            P("rep", "exp"),
            P("exp", "rep"),
            P("exp", None),
        ),
        out_specs=(
            P("exp", None),
            P("exp", None, None),
            P("rep", "exp"),
            P("rep", "exp"),
            P("exp", "rep"),
        ),
        check_vma=False,
    )
```

```python
import functools

import jax
import jax.numpy as jnp
from jax import lax
from jax.experimental import pallas as pl
from jax.experimental.pallas import tpu as pltpu
from jax.sharding import PartitionSpec as P

CAP = 40
LANES = 128
GROUP = 16
FORWARD_FLOPS = 100_000_000_000
F32 = jnp.float32
BF16 = jnp.bfloat16
MIB = 1024 * 1024


def dot(a, b, contract, batch=((), ())):
    return lax.dot_general(a, b, (contract, batch), preferred_element_type=F32)


def mm(a, b):
    return dot(a, b, ((1,), (0,)))


def mm_t(a, b):
    return dot(a, b, ((1,), (1,)))


def t_mm(a, b):
    return dot(a, b, ((0,), (0,)))


def call(kernel, flops, moved, mib=12, **kw):
    return pl.pallas_call(
        kernel,
        compiler_params=pltpu.CompilerParams(vmem_limit_bytes=mib * MIB),
        cost_estimate=pl.CostEstimate(flops=flops, bytes_accessed=moved, transcendentals=0),
        **kw,
    )


def whole(shape):
    return pl.BlockSpec(shape, lambda *_: (0,) * len(shape))


def rows(count, columns, at=0):
    return pl.BlockSpec((count, columns), lambda g, *_: (g, at))


def shape_of(shape, dtype):
    return jax.ShapeDtypeStruct(shape, dtype)


def lane_column(shape, width):
    return lax.broadcasted_iota(jnp.int32, shape, 1) % width


def shifted(window, shift, start, count):
    size = window.shape[1]
    return pltpu.roll(window, (-shift) % size, 1)[:, start : start + count]


def other_core(values):
    return lax.ppermute(values, "rep", [(0, 1), (1, 0)])


def other_shard(values):
    return lax.ppermute(values, "exp", [(i, i ^ 1) for i in range(lax.axis_size("exp"))])


def exchange(values):
    count = lax.axis_size("exp")
    shards = count // values.shape[0]
    groups = None
    if shards > 1:
        groups = [[s + shards * e for e in range(values.shape[0])] for s in range(shards)]
    return lax.all_to_all(
        values, "exp", split_axis=0, concat_axis=0, tiled=True, axis_index_groups=groups
    )


def hbm():
    return pl.BlockSpec(memory_space=pl.ANY)


def vmem():
    return pl.BlockSpec(memory_space=pltpu.VMEM)


def fast(shape, dtype):
    return pltpu.VMEM(shape, dtype)


def near(values):
    return pltpu.with_memory_space_constraint(values, pltpu.VMEM)


def far_off(values):
    return pltpu.with_memory_space_constraint(values, pltpu.HBM)


def kernel_call(kernel, flops, moved, operands, outs, name, mib=12, place=None, steps=1, scratch=(), specs=None, out_specs=None):
    specs = specs or [vmem() for _ in operands]
    out_specs = out_specs or [vmem() for _ in outs]
    return call(
        kernel,
        flops,
        moved,
        mib,
        grid_spec=pltpu.PrefetchScalarGridSpec(
            num_scalar_prefetch=0 if place is None else 1,
            grid=(steps,),
            in_specs=specs,
            out_specs=out_specs,
            scratch_shapes=list(scratch),
        ),
        out_shape=outs,
        name=name,
    )(*(() if place is None else (place,)), *operands)


def tiles_of(columns):
    return -(-columns // LANES)


def stacked(values):
    columns = values.shape[1]
    spare = tiles_of(columns) * LANES - columns
    if spare:
        values = jnp.concatenate([values, jnp.zeros((values.shape[0], spare), F32)], axis=1)
    parts = [values[:, k * LANES : (k + 1) * LANES] for k in range(tiles_of(columns))]
    return jnp.concatenate(parts, axis=0)


def own_selection(routes, experts):
    tok = routes.shape[1]
    expert = lax.broadcasted_iota(jnp.int32, (experts, tok), 0).astype(F32)
    named = jnp.where((expert == routes[0:1]) | (expert == routes[1:2]), 1.0, 0.0)
    first = lax.broadcasted_iota(jnp.int32, (tok, tok), 0)
    second = lax.broadcasted_iota(jnp.int32, (tok, tok), 1)
    before = jnp.where(first <= second, 1.0, 0.0).astype(BF16)
    at = mm(named.astype(BF16), before) - 1.0
    slot = lax.broadcasted_iota(jnp.int32, (CAP, tok), 0).astype(F32)
    return [
        jnp.where((at[e : e + 1] == slot) & (named[e : e + 1] > 0.0), 1.0, 0.0)
        for e in range(experts)
    ]


def own_columns(cot, half):
    if cot.shape[1] == half:
        return cot
    return jnp.where(lax.axis_index("rep") == 0, cot[:, :half], cot[:, half:])


def pack_kernel(shards, half, latent_ref, routes_ref, cot_ref, out_ref, held, sem):
    rows_here = latent_ref.shape[0]
    experts = held.shape[0]
    cells = jnp.concatenate([latent_ref[r].astype(F32) for r in range(rows_here)], axis=1)
    routes = routes_ref[...].astype(F32)
    payload = jnp.concatenate([cells, routes], axis=0)
    sel = own_selection(routes, experts)
    cot = own_columns(cot_ref[...], half)
    cots = mm(jnp.concatenate(sel, axis=0).astype(BF16), cot)
    copies = []
    for e in range(experts):
        slots = stacked(cots[e * CAP : (e + 1) * CAP])
        held[e] = jnp.concatenate([slots, payload], axis=0).astype(BF16)
        for n in range(shards):
            block = e * shards + n
            copies.append(pltpu.make_async_copy(held.at[e], out_ref.at[block], sem.at[block]))
            copies[-1].start()
    for copy in copies:
        copy.wait()


def pack(latent, routes_t, cot, experts, shards, half):
    rows_here, channels, width = latent.shape
    top, tok = routes_t.shape
    blocks = experts * shards
    depth = tiles_of(half) * CAP + channels + top
    operands = [latent, routes_t, cot]
    return kernel_call(
        functools.partial(pack_kernel, shards, half),
        2 * blocks * CAP * tok * half,
        4 * blocks * depth * LANES,
        [far_off(a) for a in operands],
        [pltpu.HBM((blocks, depth, LANES), BF16)],
        "pack",
        specs=[whole(a.shape) for a in operands],
        out_specs=[hbm()],
        scratch=[pltpu.VMEM((experts, depth, LANES), BF16), pltpu.SemaphoreType.DMA((blocks,))],
    )[0]


def unpacked(ref, columns):
    tiles = tiles_of(columns)
    blocks = ref.shape[0]
    held = [ref[b, : tiles * CAP, :].astype(F32) for b in range(blocks)]
    parts = [
        jnp.concatenate([one[k * CAP : (k + 1) * CAP] for one in held], axis=0)
        for k in range(tiles)
    ]
    return jnp.concatenate(parts, axis=1)[:, :columns]


def unpack_kernel(packed_ref, after_ref, cot_ref, image_ref):
    cot_ref[...] = unpacked(packed_ref, cot_ref.shape[1]).astype(BF16)
    top = packed_ref.shape[1] - image_ref.shape[1]
    for b in range(packed_ref.shape[0]):
        image_ref[b] = packed_ref[b, top:, :]


def unpack(packed, half, lines, after):
    blocks, _, tok = packed.shape
    return kernel_call(
        unpack_kernel,
        100_000_000_000,
        4 * packed.size,
        [near(packed), far_off(after)],
        [fast((blocks * CAP, half), BF16), fast((blocks, lines, tok), BF16)],
        "unpack",
        specs=[vmem(), hbm()],
    )


def sum_kernel(a_ref, b_ref, after_ref, out_ref):
    out_ref[...] = (a_ref[...].astype(F32) + b_ref[...].astype(F32)).astype(out_ref.dtype)


def add_up(a, b, after):
    operands = [near(a), near(b), near(after)]
    outs = [fast(a.shape, a.dtype)]
    return kernel_call(sum_kernel, a.size, 6 * a.size, operands, outs, "add_up")[0]


def pack_back_kernel(
    paired, a_ref, b_ref, c_ref, terms_ref, over_ref, after_ref, out_ref, held, sem
):
    total = a_ref[...].astype(F32) + b_ref[...].astype(F32)
    if paired:
        total = total + c_ref[...].astype(F32)
    copies = []
    for b in range(out_ref.shape[0]):
        slots = stacked(total[b * CAP : (b + 1) * CAP])
        terms = terms_ref[b]
        if paired:
            terms = terms + over_ref[b].astype(F32)
        held[b] = jnp.concatenate([slots, terms], axis=0).astype(BF16)
        copies.append(pltpu.make_async_copy(held.at[b], out_ref.at[b], sem.at[b]))
        copies[-1].start()
    for copy in copies:
        copy.wait()


def pack_back(a, b, c, terms, over, after, paired):
    blocks, channels, tok = terms.shape
    depth = tiles_of(a.shape[1]) * CAP + channels
    return kernel_call(
        functools.partial(pack_back_kernel, paired),
        a.size,
        8 * a.size,
        [near(x) for x in (a, b, c, terms, over, after)],
        [pltpu.HBM((blocks, depth, LANES), BF16)],
        "pack_back",
        out_specs=[hbm()],
        scratch=[pltpu.VMEM((blocks, depth, LANES), BF16), pltpu.SemaphoreType.DMA((blocks,))],
    )[0]


PIECES = 4


def pieces(source, target, sem, at=0):
    deep = source.shape[0] // PIECES
    bands = [pl.ds(k * deep, deep) for k in range(PIECES)]
    return [
        pltpu.make_async_copy(source.at[band, :], target.at[band, :], sem.at[at + k])
        for k, band in enumerate(bands)
    ]


def far_kernel(place_ref, gate_ref, up_ref, down_ref, after_ref, gate_out, up_out, down_out, sem):
    size = gate_out.shape[1]
    at = pl.multiple_of((1 - place_ref[2]) * size, LANES)
    copies = (
        pieces(gate_ref.at[:, pl.ds(at, size)], gate_out, sem)
        + pieces(up_ref.at[:, pl.ds(at, size)], up_out, sem, PIECES)
        + pieces(down_ref.at[pl.ds(at, size), :], down_out, sem, 2 * PIECES)
    )
    for copy in copies:
        copy.start()
    for copy in copies:
        copy.wait()


def far_weights(place, gate, up, down, after):
    half, hid = gate.shape
    size = hid // 2
    return kernel_call(
        far_kernel,
        0,
        LANES,
        [far_off(gate), far_off(up), far_off(down), far_off(after)],
        [fast((half, size), BF16), fast((half, size), BF16), fast((size, half), BF16)],
        "far_weights",
        place=place,
        specs=[hbm()] * 4,
        scratch=[pltpu.SemaphoreType.DMA((3 * PIECES,))],
    )


def cuts(lengths):
    start, out = 0, []
    for n in lengths:
        out.append((start, n))
        start += n
    return out


def params_kernel(
    turn, experts, shards, place_ref, stem_in, gain_in, router_in, routes_ref, cot_ref, after,
    stem, gain, router, taken, cot,
):
    wide = router_in[...].astype(F32)
    model = wide.shape[0]
    blank = jnp.zeros((model, LANES - 2 * experts), F32)
    wide = jnp.concatenate([wide, wide, blank], axis=1)
    values, gains = stem_in[...], gain_in[...]
    if turn:
        half = model // 2
        first = place_ref[2] == 0
        wide = jnp.where(first, wide, jnp.concatenate([wide[half:], wide[:half]], axis=0))
        turned = jnp.concatenate([values[:, half:], values[:, :half]], axis=1)
        values = jnp.where(first, values, turned)
        turned = jnp.concatenate([gains[:, half:], gains[:, :half]], axis=1)
        gains = jnp.where(first, gains, turned)
    stem[...] = values
    gain[...] = gains
    router[...] = wide.astype(BF16)
    sel = own_selection(routes_ref[...].astype(F32), experts)
    taken[...] = jnp.concatenate([one for one in sel for _ in range(shards)], axis=0).astype(BF16)
    cot[...] = own_columns(cot_ref[...], cot.shape[1])


def small_params(place, stem, gain, router, routes_t, cot, half, shards, after, turn):
    model, experts = router.shape
    tok = cot.shape[0]
    small = [far_off(a) for a in (stem, gain, router, routes_t, cot)]
    shapes = [(stem.shape, BF16), (gain.shape, F32), ((model, LANES), BF16)]
    shapes += [((experts * shards * CAP, tok), BF16), ((tok, half), BF16)]
    return kernel_call(
        functools.partial(params_kernel, turn, experts, shards),
        0,
        LANES,
        small + [far_off(after)],
        [pltpu.HBM(*a) for a in shapes],
        "params",
        place=place,
        specs=[whole(a.shape) for a in small] + [hbm()],
        out_specs=[whole(shape) for shape, _ in shapes],
    )


def inner_copies(place_ref, refs, inner, size, at, sem):
    copies = []
    for n, (ref, (a, depth)) in enumerate(zip(refs, cuts([r.shape[0] for r in refs]))):
        if ref.shape[1] != size:
            ref = ref.at[:, pl.ds(pl.multiple_of(place_ref[2] * size, LANES), size)]
        copies += pieces(ref, inner.at[pl.ds(a, depth), pl.ds(at, size)], sem, n * PIECES)
    return copies


def outer_copies(place_ref, refs, outer, sem):
    copies = []
    size = outer.shape[0]
    for n, (ref, (a, depth)) in enumerate(zip(refs, cuts([r.shape[1] for r in refs]))):
        if ref.shape[0] != size:
            ref = ref.at[pl.ds(pl.multiple_of(place_ref[2] * size, LANES), size), :]
        copies += pieces(ref, outer.at[:, pl.ds(a, depth)], sem, n * PIECES)
    return copies


def gather_kernel(parts, place_ref, *refs):
    gates, (stem_in, gain_in, router_in) = refs[:parts], refs[parts : parts + 3]
    stem, gain, inner, small_sem, sem = refs[parts + 3 :]
    size = inner.shape[1] - LANES
    copies = [
        pltpu.make_async_copy(stem_in, stem, small_sem.at[0]),
        pltpu.make_async_copy(gain_in, gain, small_sem.at[1]),
        pltpu.make_async_copy(router_in, inner.at[:, pl.ds(size, LANES)], small_sem.at[2]),
    ]
    copies += inner_copies(place_ref, gates, inner, size, 0, sem)
    for copy in copies:
        copy.start()
    for copy in copies:
        copy.wait()


def gather(place, small, gates, size):
    stem, gain, router = small
    model = router.shape[0]
    operands = [far_off(gates[0])] + list(gates[1:]) + [far_off(a) for a in small]
    return kernel_call(
        functools.partial(gather_kernel, len(gates)),
        0,
        LANES,
        operands,
        [
            fast(stem.shape, BF16),
            fast(gain.shape, F32),
            fast((model, size + LANES), BF16),
        ],
        "gather",
        place=place,
        specs=[hbm()] * len(operands),
        scratch=[
            pltpu.SemaphoreType.DMA((3,)),
            pltpu.SemaphoreType.DMA((len(gates) * PIECES,)),
        ],
    )


def join_kernel(place_ref, own_ref, away_ref, a_ref, b_ref, out_ref, latent_ref):
    half = own_ref.shape[1]
    first = place_ref[2] == 0
    own, away = own_ref[...], away_ref[...]
    out_ref[:, :half] = jnp.where(first, own, away)
    out_ref[:, half:] = jnp.where(first, away, own)
    total = a_ref[...] + b_ref[...]
    width = latent_ref.shape[2]
    for r in range(latent_ref.shape[0]):
        latent_ref[r] = total[:, r * width : (r + 1) * width]


def join(place, own, away, a, b, rows_here):
    count, half = own.shape
    channels, tok = a.shape
    return kernel_call(
        join_kernel,
        0,
        8 * count * half,
        [near(own), near(away), near(a), near(b)],
        [
            shape_of((count, 2 * half), BF16),
            shape_of((rows_here, channels, tok // rows_here), F32),
        ],
        "join",
        place=place,
    )


def pair_selection(named):
    lanes = named.shape[1]
    tok = lanes // 2
    first = lax.broadcasted_iota(jnp.int32, (lanes, lanes), 0)
    second = lax.broadcasted_iota(jnp.int32, (lanes, lanes), 1)
    before = ((first <= second) & (first // tok == second // tok)).astype(F32).astype(BF16)
    wide = jnp.broadcast_to(named, (8, lanes)).astype(BF16)
    place = mm(wide, before)[:1]
    lane = lax.broadcasted_iota(jnp.int32, (1, lanes), 1)
    place = place - 1.0 + jnp.where(lane >= tok, float(CAP), 0.0)
    slot = lax.broadcasted_iota(jnp.int32, (2 * CAP, lanes), 0).astype(F32)
    return jnp.where((place == slot) & (named > 0.0), 1.0, 0.0)


def block_getter(paired, place_ref, image_refs):
    if not paired:
        return lambda pair, parity: image_refs[0][2 * pair + parity].astype(F32)
    side = place_ref[1] & 1

    def get(pair, parity):
        same, other = [ref[pair].astype(F32) for ref in image_refs]
        return jnp.where(side == parity, same, other)

    return get


def pair_patches(get, pair, pairs, width, channels):
    before = get(jnp.maximum(pair - 1, 0), 1)[:channels]
    after = get(jnp.minimum(pair + 1, pairs - 1), 0)[:channels]
    window = jnp.concatenate(
        [
            jnp.where(pair > 0, before, 0.0),
            get(pair, 0)[:channels],
            get(pair, 1)[:channels],
            jnp.where(pair + 1 < pairs, after, 0.0),
        ],
        axis=1,
    )
    tok = window.shape[1] // 4
    column = lane_column((channels, 2 * tok), width)
    pieces_of = []
    for i in range(3):
        for j in range(3):
            piece = shifted(window, (i - 1) * width + j - 1, tok, 2 * tok)
            source = column + (j - 1)
            pieces_of.append(jnp.where((source >= 0) & (source < width), piece, 0.0))
    return jnp.concatenate(pieces_of, axis=0)


def by_side(pairs, even):
    same = [jnp.where(even, p[:CAP], p[CAP:]) for p in pairs]
    other = [jnp.where(even, p[CAP:], p[:CAP]) for p in pairs]
    return same + other


def forward_kernel(
    paired, parts, width, experts, outs, place_ref, *refs
):
    images = 2 if paired else 1
    image_refs, (stem_ref, gain_ref, first_ref), refs = refs[:images], refs[images : images + 3], refs[images + 3 :]
    weights, router_in, refs = refs[: 3 * parts], refs[3 * parts], refs[3 * parts + 1 :]
    refs = refs[1:] if paired else refs
    saved_ref, normed_ref, value_ref, meta_ref, coef_ref, sel_ref, pg_ref, pu_ref = refs[:8]
    hidden_ref, inner, outer, *out_refs = refs[8:-4]
    save_sem, up_sem, down_sem, gate_sem = refs[-4:]
    step = pl.program_id(0)
    size = outer.shape[0]
    up_copies = inner_copies(place_ref, weights[:parts], inner, size, size, up_sem)
    down_copies = outer_copies(place_ref, weights[parts : 2 * parts], outer, down_sem)
    later = inner_copies(place_ref, weights[2 * parts :], inner, size, 0, gate_sem)
    wide = inner.at[:, pl.ds(2 * size, LANES)]
    later.append(pltpu.make_async_copy(router_in, wide, gate_sem.at[parts * PIECES]))

    def arrive(copies):
        @pl.when(step == 0)
        def _():
            for copy in copies:
                copy.wait()

    @pl.when(step == 0)
    def _():
        for copy in up_copies + down_copies + later:
            copy.start()

    chunk = GROUP * CAP
    here = pl.ds(pl.multiple_of(step * chunk, chunk), chunk)
    channels = image_refs[0].shape[1] - 2
    pairs = images * image_refs[0].shape[0] // 2
    get = block_getter(paired, place_ref, image_refs)
    mine = place_ref[0].astype(F32)
    even = (place_ref[1] & 1) == 0
    taken, others = [], []
    for q in range(GROUP // 2):
        pair = step * (GROUP // 2) + q
        lines = [get(pair, n)[channels:] for n in range(2)]
        named_by = [jnp.concatenate([line[k : k + 1] for line in lines], axis=1) for k in range(2)]
        named = jnp.where((named_by[0] == mine) | (named_by[1] == mine), 1.0, 0.0)
        sel = pair_selection(named)
        sel_ref[step * (GROUP // 2) + q] = sel.astype(BF16)
        other = named_by[0] + named_by[1] - mine
        others.append(jnp.sum(sel * other, axis=1, keepdims=True))
        patches = pair_patches(get, pair, pairs, width, channels)
        taken.append(mm_t(sel.astype(BF16), patches.astype(BF16)))
    bands = 2 if paired else 1
    deep = chunk // bands
    lines = [pl.ds(pl.multiple_of(step * chunk + k * deep, deep), deep) for k in range(bands)]
    held = [slice(k * deep, (k + 1) * deep) for k in range(bands)]
    if paired:
        taken, others = by_side(taken, even), by_side(others, even)
    each = len(taken) // bands
    patches = [
        jnp.concatenate(taken[k * each : (k + 1) * each], axis=0).astype(BF16) for k in range(bands)
    ]
    others = [jnp.concatenate(others[k * each : (k + 1) * each], axis=0) for k in range(bands)]
    stems = [mm(one, stem_ref[...]).astype(BF16) for one in patches]
    normeds, scales, gates, gated, upped, hiddens = [], [], [], [], [], []
    for line, band, stem in zip(lines, held, stems):
        value_ref[line, :] = stem
        value = stem.astype(F32)
        scale = lax.rsqrt(jnp.mean(value * value, axis=-1, keepdims=True) + 1e-06)
        normed = (value * scale * gain_ref[...]).astype(BF16)
        normed_ref[band, :] = normed
        normeds.append(normed)
        scales.append(scale)
    own_part = normed_ref.at[:, pl.ds(0, saved_ref.shape[1])]
    save = pltpu.make_async_copy(own_part, saved_ref.at[here, :], save_sem.at[0])
    save.start()
    for normed in normeds:
        gated.append(mm(normed, first_ref[:, :size]))
    for line, normed, other, scale in zip(lines, normeds, others, scales):
        logits = mm(normed, first_ref[:, size:])
        lane = lax.broadcasted_iota(jnp.int32, logits.shape, 1)
        again = jnp.where(lane >= experts, lane - experts, lane).astype(F32)
        lane = lane.astype(F32)
        mine_logit = jnp.sum(jnp.where(lane == mine, logits, 0.0), axis=1, keepdims=True)
        other_logit = jnp.sum(jnp.where(lane == other, logits, 0.0), axis=1, keepdims=True)
        sig_mine, sig_other = jax.nn.sigmoid(mine_logit), jax.nn.sigmoid(other_logit)
        gate = sig_mine / (sig_mine + sig_other)
        rest = sig_other / (sig_mine + sig_other)
        both = gate * rest
        coef_ref[line, :] = jnp.where(again == mine, both * (1.0 - sig_mine), 0.0) - jnp.where(
            again == other, both * (1.0 - sig_other), 0.0
        )
        meta_ref[line, :] = jnp.where(lane == 0.0, gate, scale)
        gates.append(gate)
    arrive(up_copies)
    for normed in normeds:
        upped.append(mm(normed, inner[:, size : 2 * size]))
    arrive(down_copies)
    for line, pre_gate, pre_up in zip(lines, gated, upped):
        pg_ref[line, :] = pre_gate.astype(BF16)
        pu_ref[line, :] = pre_up.astype(BF16)
        hidden = (pre_gate * jax.nn.sigmoid(pre_gate) * pre_up).astype(BF16)
        hidden_ref[line, :] = hidden
        hiddens.append(hidden)
    for ref, (a, n) in zip(out_refs, cuts([r.shape[1] for r in out_refs])):
        part = (gates[-1] * mm(hiddens[-1], outer[:, a : a + n])).astype(BF16)
        if paired:
            ref[...] = part
        else:
            ref[here, :] = part
    save.wait()
    arrive(later)


def forward(place, images, gathered, router, weights, size, columns, after, paired, width, experts):
    blocks = sum(image.shape[0] for image in images)
    tok = images[0].shape[2]
    slots, chunk = blocks * CAP, GROUP * CAP
    stem, gain, inner = gathered
    model = stem.shape[1]
    parts = len(weights) // 3
    operands = [near(a) for a in list(images) + [stem, gain, inner]]
    specs = [vmem()] * len(operands) + [hbm()] * (len(weights) + 1)
    operands += [far_off(w) if k % parts == 0 else w for k, w in enumerate(weights)]
    operands.append(far_off(router))
    if paired:
        operands.append(near(after))
        specs.append(vmem())
    outs = [
        pltpu.HBM((slots, columns[0]), BF16),
        fast((chunk, model), BF16),
        fast((slots, model), BF16),
        fast((slots, LANES), F32),
        fast((slots, LANES), F32),
        fast((blocks // 2, 2 * CAP, 2 * tok), BF16),
        fast((slots, size), BF16),
        fast((slots, size), BF16),
        fast((slots, size), BF16),
        fast((model, 2 * size + LANES), BF16),
        fast((size, model), BF16),
    ]
    outs += [fast((slots // 2 if paired else slots, n), BF16) for n in columns]
    return pl.pallas_call(
        functools.partial(forward_kernel, paired, parts, width, experts, columns),
        compiler_params=pltpu.CompilerParams(vmem_limit_bytes=20 * MIB),
        cost_estimate=pl.CostEstimate(
            flops=FORWARD_FLOPS, bytes_accessed=LANES, transcendentals=0
        ),
        grid_spec=pltpu.PrefetchScalarGridSpec(
            num_scalar_prefetch=1,
            grid=(blocks // GROUP,),
            in_specs=specs,
            out_specs=[hbm()] + [vmem()] * (len(outs) - 1),
            scratch_shapes=[
                pltpu.SemaphoreType.DMA((1,)),
                pltpu.SemaphoreType.DMA((parts * PIECES,)),
                pltpu.SemaphoreType.DMA((parts * PIECES,)),
                pltpu.SemaphoreType.DMA((parts * PIECES + 1,)),
            ],
        ),
        out_shape=outs,
        name="forward",
    )(place, *operands)


def own_stem_kernel(paired, width, place_ref, *refs):
    image_refs, (stem_ref, own_ref) = refs[:-2], refs[-2:]
    me = place_ref[1]
    channels = image_refs[0].shape[1] - 2
    tok = image_refs[0].shape[2]
    pairs = len(image_refs) * image_refs[0].shape[0] // 2
    own = pair_patches(block_getter(paired, place_ref, image_refs), me // 2, pairs, width, channels)
    own = jnp.where(me % 2 == 0, own[:, :tok], own[:, tok:]).astype(BF16)
    own_ref[...] = t_mm(own, stem_ref[:, : own_ref.shape[1]]).astype(BF16)


def own_stem_of(place, images, stem, half, paired, width):
    tok = images[0].shape[2]
    return kernel_call(
        functools.partial(own_stem_kernel, paired, width),
        0,
        LANES,
        [near(a) for a in list(images) + [stem]],
        [pltpu.HBM((tok, half), BF16)],
        "own_stem",
        place=place,
        out_specs=[whole((tok, half))],
    )[0]


def outputs_kernel(width, place_ref, meta_ref, hidden_ref, outer, same_ref, other_ref, stem_ref, near_ref, far_ref, own_ref):
    own_stem_kernel(True, width, place_ref, same_ref, other_ref, stem_ref, own_ref)
    count, half = near_ref.shape
    gate = meta_ref[:count, 0:1]
    hidden = hidden_ref[:count, :]
    near_ref[...] = (gate * mm(hidden, outer[:, :half])).astype(BF16)
    far_ref[...] = (gate * mm(hidden, outer[:, half:])).astype(BF16)


def outputs(place, meta, hidden, outer, images, stem, width):
    count, half = hidden.shape[0] // 2, outer.shape[1] // 2
    tok = images[0].shape[2]
    return kernel_call(
        functools.partial(outputs_kernel, width),
        0,
        LANES,
        [near(a) for a in [meta, hidden, outer] + list(images) + [stem]],
        [fast((count, half), BF16)] * 2 + [pltpu.HBM((tok, half), BF16)],
        "outputs",
        place=place,
        out_specs=[vmem()] * 2 + [whole((tok, half))],
    )


def backward_kernel(
    parts, bands, experts, stem_ref, gain_ref, inner, outer, value_ref, meta_ref, coef_ref, pg_ref, pu_ref,
    *refs,
):
    cot_refs, refs = refs[: parts * bands], refs[parts * bands :]
    saved, refs = refs[:4], refs[4:]
    proj_ref, ggp_ref, gup_ref, hg_ref, sem = refs
    step = pl.program_id(0)
    model = stem_ref.shape[1]
    chunk = GROUP * CAP
    here = pl.ds(pl.multiple_of(step * chunk, chunk), chunk)
    sources = [ggp_ref, gup_ref, hg_ref]
    targets = [ref.at[here, :] for ref in saved[:3]]
    for n, ref in enumerate(cot_refs[:bands]):
        if bands == 1:
            sources.append(ref.at[here, :])
            targets.append(saved[3].at[here, :])
        else:
            sources.append(ref)
            targets.append(saved[3].at[pl.ds(n * ref.shape[0], ref.shape[0]), :])
    saves = [
        pltpu.make_async_copy(a, b, sem.at[n]) for n, (a, b) in enumerate(zip(sources, targets))
    ]
    for save in saves[3:]:
        save.start()
    deep = chunk // bands
    places = cuts([r.shape[1] for r in cot_refs[::bands]])
    lines = [pl.ds(pl.multiple_of(step * chunk + k * deep, deep), deep) for k in range(bands)]
    held = [slice(k * deep, (k + 1) * deep) for k in range(bands)]
    gates = [meta_ref[line, 0:1] for line in lines]
    scales = [meta_ref[line, 1:2] for line in lines]
    raws, mixes, backs, grads = [], [], [], []
    for k, line in enumerate(lines):
        raw = 0.0
        for n, (a, m) in enumerate(places):
            cot = cot_refs[n * bands + k][...] if bands > 1 else cot_refs[n][line, :]
            raw = raw + mm_t(cot, outer[:, a : a + m])
        raws.append(raw)
    for line, band, gate, raw in zip(lines, held, gates, raws):
        pre_gate = pg_ref[line, :].astype(F32)
        pre_up = pu_ref[line, :].astype(F32)
        sigma = jax.nn.sigmoid(pre_gate)
        silu = pre_gate * sigma
        hidden = silu * pre_up
        grad_gates = jnp.sum(raw * hidden, axis=1, keepdims=True)
        hg_ref[band, :] = (gate * hidden).astype(BF16)
        grad_hidden = gate * raw
        ggp = (grad_hidden * pre_up * sigma * (1.0 + pre_gate - silu)).astype(BF16)
        gup = (grad_hidden * silu).astype(BF16)
        ggp_ref[band, :] = ggp
        gup_ref[band, :] = gup
        grad_logits = grad_gates * coef_ref[line, :]
        high = grad_logits.astype(BF16)
        low = (grad_logits - high.astype(F32)).astype(BF16)
        lane = lax.broadcasted_iota(jnp.int32, grad_logits.shape, 1)
        mix = jnp.where(lane < experts, high.astype(F32), low.astype(F32)).astype(BF16)
        mixes.append(jnp.concatenate([ggp, gup, mix], axis=1))
    for save in saves[:3]:
        save.start()
    for mix in mixes:
        backs.append(mm_t(mix, inner[...]))
    for line, scale, back in zip(lines, scales, backs):
        back = back * gain_ref[...]
        value = value_ref[line, :].astype(F32)
        along = jnp.sum(back * value, axis=1, keepdims=True) * (scale * scale * scale) / model
        grads.append((scale * back - along * value).astype(BF16))
    for line, grad in zip(lines, grads):
        proj_ref[line, :] = mm_t(grad, stem_ref[...]).astype(BF16)
    for save in saves:
        save.wait()


def backward(stem, gain, inner, outer, acts, cots, experts):
    slots, model = acts[0].shape
    size, chunk = outer.shape[0], GROUP * CAP
    taps = stem.shape[0]
    parts, bands = len(cots), len(cots[0])
    operands = [stem, gain, inner, outer] + list(acts) + [c for part in cots for c in part]
    return kernel_call(
        functools.partial(backward_kernel, parts, bands, experts),
        2 * slots * model * size * 4,
        slots * (4 * model + 12 * size) + 6 * model * size,
        [near(a) for a in operands],
        [pltpu.HBM((slots, size), BF16)] * 3
        + [pltpu.HBM((slots, cots[0][0].shape[1]), BF16)]
        + [fast((slots, taps), BF16)]
        + [fast((chunk, size), BF16)] * 3,
        "backward",
        mib=20,
        steps=slots // chunk,
        out_specs=[hbm()] * 4 + [vmem()] * 4,
        scratch=[pltpu.SemaphoreType.DMA((3 + bands,))],
    )


def image_kernel(paired, width, place_ref, proj_ref, sel_ref, stem_ref, cot_ref, *refs):
    out_refs, terms = refs[:-1], refs[-1]
    pairs = sel_ref.shape[0]
    tok = cot_ref.shape[0]
    channels = out_refs[0].shape[1]
    count = 2 * pairs * tok
    own = mm_t(stem_ref[:, : cot_ref.shape[1]], cot_ref[...])
    me = place_ref[1]
    even = (me & 1) == 0
    proj = proj_ref[...].astype(F32)
    for q in range(pairs):
        if paired:
            same = proj[CAP * q : CAP * (q + 1)]
            other = proj[CAP * (pairs + q) : CAP * (pairs + q + 1)]
            both = [jnp.where(even, same, other), jnp.where(even, other, same)]
            pair = jnp.concatenate(both, axis=0)
        else:
            pair = proj[2 * CAP * q : 2 * CAP * (q + 1)]
        block = t_mm(pair.astype(BF16), sel_ref[q])
        terms[:, 2 * q * tok : (2 * q + 1) * tok] = block[:, :tok] + jnp.where(2 * q == me, own, 0.0)
        terms[:, (2 * q + 1) * tok : (2 * q + 2) * tok] = block[:, tok:] + jnp.where(
            2 * q + 1 == me, own, 0.0
        )
    lane = lax.broadcasted_iota(jnp.int32, (channels, count), 1)
    total = jnp.zeros((channels, count), F32)
    for i in range(3):
        for j in range(3):
            k = (3 * i + j) * channels
            shift = (i - 1) * width + j - 1
            piece = pltpu.roll(terms[k : k + channels, :], shift % count, 1)
            column = lane % width + (1 - j)
            token = lane - shift
            keep = (column >= 0) & (column < width) & (token >= 0) & (token < count)
            total = total + jnp.where(keep, piece, 0.0)
    for q in range(pairs):
        low = total[:, 2 * q * tok : (2 * q + 1) * tok]
        high = total[:, (2 * q + 1) * tok : (2 * q + 2) * tok]
        if paired:
            out_refs[0][q] = jnp.where(even, low, high)
            out_refs[1][q] = jnp.where(even, high, low).astype(BF16)
        else:
            out_refs[0][2 * q] = low
            out_refs[0][2 * q + 1] = high


def to_image(place, proj, sel, stem, cot, paired, width, channels):
    pairs = sel.shape[0]
    blocks, tok = 2 * pairs, cot.shape[0]
    taps, half = stem.shape[0], cot.shape[1]
    return kernel_call(
        functools.partial(image_kernel, paired, width),
        2 * proj.shape[0] * 2 * tok * taps,
        4 * taps * blocks * tok,
        [near(a) for a in (proj, sel, stem, cot)],
        [fast((pairs, channels, tok), F32), fast((pairs, channels, tok), BF16)]
        if paired
        else [fast((blocks, channels, tok), F32)],
        "to_image",
        place=place,
        scratch=[pltpu.VMEM((taps, blocks * tok), F32)],
    )


def far_grads_kernel(normed, ggp, gup, hg, *refs):
    cots, (gate_out, up_out, down_out) = refs[:-3], refs[-3:]
    half = cots[0].shape[1]
    far = normed[:, half:]
    gate_out[...] = t_mm(far, ggp[...]).astype(BF16)
    up_out[...] = t_mm(far, gup[...]).astype(BF16)
    cot = jnp.concatenate([ref[...] for ref in cots], axis=0)
    down_out[...] = t_mm(hg[...], cot).astype(BF16)


def far_grads(normed, ggp, gup, hg, cots):
    slots, size = ggp.shape
    half = cots[0].shape[1]
    return kernel_call(
        far_grads_kernel,
        6 * slots * size * half,
        20 * slots * size,
        [near(a) for a in [normed, ggp, gup, hg] + list(cots)],
        [fast((half, size), BF16)] * 2 + [fast((size, half), BF16)],
        "far_grads",
    )


def near_grads_kernel(
    place_ref, normed, ggp, gup, hg, cot, after_ref, gate_out, up_out, down_out,
    left, right, own, sem, own_sem,
):
    half = cot.shape[1]
    size = ggp.shape[1]
    here = pl.multiple_of(place_ref[2] * size, LANES)
    sources = (normed, ggp, gup, hg, cot)
    targets = (left.at[0], right.at[0], right.at[1], left.at[1], right.at[2])
    loads = [pltpu.make_async_copy(a, b, sem.at[n]) for n, (a, b) in enumerate(zip(sources, targets))]
    places = (
        gate_out.at[:, pl.ds(here, size)],
        up_out.at[:, pl.ds(here, size)],
        down_out.at[pl.ds(here, size), :],
    )
    results = [pieces(own.at[n], a, own_sem, n * PIECES) for n, a in enumerate(places)]
    for load in loads:
        load.start()
    for load in loads[:2]:
        load.wait()
    own[0] = t_mm(left[0], right[0])
    for copy in results[0]:
        copy.start()
    loads[2].wait()
    own[1] = t_mm(left[0], right[1])
    for copy in results[1]:
        copy.start()
    loads[3].wait()
    loads[4].wait()
    own[2] = t_mm(left[1], right[2])
    for copy in results[2]:
        copy.start()
    for copy in results[0] + results[1] + results[2]:
        copy.wait()


def near_grads(place, normed, ggp, gup, hg, cot, after):
    slots, size = ggp.shape
    half = cot.shape[1]
    return kernel_call(
        near_grads_kernel,
        20_000_000_000,
        LANES,
        [far_off(a) for a in (normed, ggp, gup, hg, cot, after)],
        [pltpu.HBM((half, 2 * size), F32)] * 2
        + [pltpu.HBM((2 * size, half), F32)],
        "near_grads",
        mib=14,
        place=place,
        specs=[hbm()] * 6,
        out_specs=[hbm()] * 3,
        scratch=[
            pltpu.VMEM((2, slots, half), BF16),
            pltpu.VMEM((3, slots, half), BF16),
            pltpu.VMEM((3, half, size), F32),
            pltpu.SemaphoreType.DMA((5,)),
            pltpu.SemaphoreType.DMA((3 * PIECES,)),
        ],
    )


def fill_kernel(
    place_ref, gate_in, up_in, down_in, gate_old, up_old, down_old,
    gate_out, up_out, down_out, done_ref, away, wide, in_sem, sem,
):
    size = gate_in.shape[1]
    there = pl.multiple_of((1 - place_ref[2]) * size, LANES)
    places = (
        gate_out.at[:, pl.ds(there, size)],
        up_out.at[:, pl.ds(there, size)],
        down_out.at[pl.ds(there, size), :],
    )
    loads = [
        pieces(a, away.at[n], in_sem, n * PIECES) for n, a in enumerate((gate_in, up_in, down_in))
    ]
    results = [pieces(wide.at[n], a, sem, n * PIECES) for n, a in enumerate(places)]
    deep = wide.shape[1] // PIECES
    done_ref[...] = jnp.zeros(done_ref.shape, F32)
    for load in loads[0] + loads[1] + loads[2]:
        load.start()
    for n in range(3):
        for k in range(PIECES):
            loads[n][k].wait()
            wide[n, k * deep : (k + 1) * deep] = away[n, k * deep : (k + 1) * deep].astype(F32)
            results[n][k].start()
    for copy in results[0] + results[1] + results[2]:
        copy.wait()


def fill(place, away, grads):
    shape = away[0].shape
    return pl.pallas_call(
        fill_kernel,
        compiler_params=pltpu.CompilerParams(vmem_limit_bytes=12 * MIB),
        cost_estimate=pl.CostEstimate(
            flops=10_000_000_000, bytes_accessed=LANES, transcendentals=0
        ),
        grid_spec=pltpu.PrefetchScalarGridSpec(
            num_scalar_prefetch=1,
            grid=(1,),
            in_specs=[hbm()] * 6,
            out_specs=[hbm()] * 3 + [vmem()],
            scratch_shapes=[
                pltpu.VMEM((3,) + shape, BF16),
                pltpu.VMEM((3,) + shape, F32),
                pltpu.SemaphoreType.DMA((3 * PIECES,)),
                pltpu.SemaphoreType.DMA((3 * PIECES,)),
            ],
        ),
        out_shape=[pltpu.HBM(g.shape, F32) for g in grads] + [fast((8, LANES), F32)],
        input_output_aliases={4: 0, 5: 1, 6: 2},
        name="fill",
    )(place, *[far_off(a) for a in away], *grads)


def gathered_grads(column, size, normed, ggp, gup, hg, cot):
    grads = []
    for g in (ggp[:, :size], gup[:, :size]):
        term = jnp.roll(t_mm(normed, g).astype(BF16), column, 0)
        grads.append(lax.all_to_all(term, "rep", split_axis=0, concat_axis=1, tiled=True))
    term = jnp.roll(t_mm(hg[:, :size], cot).astype(BF16), column, 1)
    grads.append(lax.all_to_all(term, "rep", split_axis=1, concat_axis=0, tiled=True))
    return [g.astype(F32) for g in grads]


def mixed_kernel(stem_ref, taken_ref, back_ref, after_ref, out_ref, *terms_refs):
    half = out_ref.shape[1]
    back = unpacked(back_ref, half).astype(BF16)
    total = stem_ref[...].astype(F32) + t_mm(taken_ref[...], back)
    out_ref[...] = total.astype(BF16)
    top = tiles_of(half) * CAP
    terms = back_ref[0, top:, :].astype(F32)
    for b in range(1, back_ref.shape[0]):
        terms = terms + back_ref[b, top:, :].astype(F32)
    for n, ref in enumerate(terms_refs):
        ref[...] = terms[n * ref.shape[0] : (n + 1) * ref.shape[0]]


def mix(stem, taken, back, after, channels):
    tok, half = stem.shape
    sides = (back.shape[1] - tiles_of(half) * CAP) // channels
    return kernel_call(
        mixed_kernel,
        2 * taken.shape[0] * tok * half,
        2 * back.size,
        [near(a) for a in (stem, taken, back, after)],
        [fast((tok, half), BF16)] + [fast((channels, tok), F32)] * sides,
        "mixed",
    )


def local(
    latent,
    stem_weight,
    norm_gain,
    router_weight,
    routes,
    gate_weight,
    up_weight,
    down_weight,
    grad_mixed,
):
    rows_here, channels, width = latent.shape
    half = gate_weight.shape[0]
    experts = router_weight.shape[1]
    tok = rows_here * width
    blocks = lax.axis_size("exp")
    cores = lax.axis_size("rep")
    shards = blocks // experts
    slots = blocks * CAP
    me = lax.axis_index("exp")
    core = lax.axis_index("rep")
    column = core * half
    place = jnp.stack([me // shards, me, core]).astype(jnp.int32)

    paired = cores == 2 and shards == 2
    given = grad_mixed
    if cores != 2:
        given = lax.dynamic_slice_in_dim(grad_mixed, column, half, 1)
    copies = 1 if paired else shards
    routes_t = routes.T
    packed = pack(latent, routes_t, given, experts, copies, half)
    arrived = exchange(packed)

    stem, gain, router = stem_weight, norm_gain[None, :], router_weight
    if cores == 2:
        far = far_weights(place, gate_weight, up_weight, down_weight, packed)
        gate_parts, up_parts, down_parts = [
            (w, other_core(f)) for w, f in zip((gate_weight, up_weight, down_weight), far)
        ]
    else:
        turned = lax.all_to_all(gate_weight, "rep", split_axis=1, concat_axis=0, tiled=True)
        spare = -turned.shape[1] % LANES
        gate_parts = (jnp.pad(jnp.roll(turned, -column, 0), ((0, 0), (0, spare))),)
        turned = lax.all_to_all(up_weight, "rep", split_axis=1, concat_axis=0, tiled=True)
        up_parts = (jnp.pad(jnp.roll(turned, -column, 0), ((0, 0), (0, spare))),)
        turned = lax.all_to_all(down_weight, "rep", split_axis=0, concat_axis=1, tiled=True)
        down_parts = (jnp.pad(jnp.roll(turned, -column, 1), ((0, spare), (0, 0))),)
        stem = jnp.roll(stem, -column, 1)
        gain = jnp.roll(gain, -column, 1)
        router = jnp.roll(router, -column, 0)

    *small, taken, cot = small_params(
        place, stem, gain, router, routes_t, given, half, copies, packed, cores == 2
    )
    same_cot, image = unpack(arrived, half, channels + 2, small[1])
    size = down_parts[-1].shape[0]
    gathered = gather(place, small, gate_parts, size)
    if paired:
        joined = other_core(same_cot)
        images = [image, other_shard(image)]
        cots = [[same_cot], [joined]]
        far_cot = other_shard(same_cot)
    elif cores == 2:
        images, joined = [image], other_core(same_cot)
        cots = [[same_cot], [joined]]
    else:
        images = [image]
        joined = lax.all_gather(same_cot, "rep", axis=1, tiled=True)
        cots = [[jnp.roll(joined, -column, 1)]]
    weights = list(up_parts) + list(down_parts) + list(gate_parts)
    columns = [w.shape[1] for w in down_parts]
    kept, normed, value, meta, coef, sel, pg, pu, hidden, inner, outer, *outs = forward(
        place, images, gathered, small[2], weights, size, columns, joined, paired, width, experts
    )
    stem, gain, _ = gathered
    if paired:
        own, away, own_stem = outputs(place, meta, hidden, outer, images, stem, width)
        far_cot, own = lax.optimization_barrier((far_cot, own))
        cots[0].append(far_cot)
        cots[1].append(other_core(far_cot))
        over = other_shard(add_up(outs[0], other_core(outs[1]), own))
        away = other_core(away)
    elif cores == 2:
        own, away = outs[0], other_core(outs[1])
        over = own
        own_stem = own_stem_of(place, images, stem, half, paired, width)
    else:
        turned = jnp.roll(outs[0], column, 1)
        own = lax.psum_scatter(turned, "rep", scatter_dimension=1, tiled=True)
        away = over = jnp.zeros_like(own)
        own_stem = own_stem_of(place, images, stem, half, paired, width)
    acts = [value, meta, coef, pg, pu]
    ggp, gup, hg, held, proj, ggp_here, gup_here, hg_here = backward(
        stem, gain, inner, outer, acts, cots, experts
    )
    terms = to_image(place, proj, sel, stem, cot, paired, width, channels)
    terms_over = other_shard(terms[1]) if paired else terms[0]
    if cores == 2:
        far = far_grads(normed, ggp_here, gup_here, hg_here, cots[1])
        away_grads = [other_core(f) for f in far]

    after = far[0] if cores == 2 else own
    sent = pack_back(own, away, over, terms[0], terms_over, after, paired)
    back = exchange(sent)

    if cores == 2:
        grads = near_grads(place, kept, ggp, gup, hg, held, sent)
        *grads, done = fill(place, away_grads, grads)
    else:
        done = jnp.zeros((8, LANES), F32)
        size = gate_weight.shape[1] // cores
        grads = gathered_grads(column, size, kept, ggp, gup, hg, held)
    grad_gate, grad_up, grad_down = grads

    mixed, lat_sum = mix(own_stem, taken, back, done, channels)
    if cores == 2:
        mixed, grad_latent = join(
            place, mixed, other_core(mixed), lat_sum, other_core(lat_sum), rows_here
        )
    else:
        mixed = lax.all_gather(mixed, "rep", axis=1, tiled=True)
        lat_sum = lax.psum(lat_sum, "rep")
        grad_latent = lat_sum.reshape(channels, rows_here, width).transpose(1, 0, 2)
    return (mixed, grad_latent, grad_gate, grad_up, grad_down)


def solution(mesh):
    return jax.shard_map(
        local,
        mesh=mesh,
        in_specs=(
            P("exp", None, None),
            P(),
            P(),
            P(),
            P("exp", None),
            P("rep", "exp"),
            P("rep", "exp"),
            P("exp", "rep"),
            P("exp", None),
        ),
        out_specs=(
            P("exp", None),
            P("exp", None, None),
            P("rep", "exp"),
            P("rep", "exp"),
            P("exp", "rep"),
        ),
        check_vma=False,
    )
```

```python
import functools

import jax
import jax.numpy as jnp
from jax import lax
from jax.experimental import pallas as pl
from jax.experimental.pallas import tpu as pltpu
from jax.sharding import PartitionSpec as P

CAP = 40
LANES = 128
GROUP = 16
FORWARD_FLOPS = 100_000_000_000
F32 = jnp.float32
BF16 = jnp.bfloat16
MIB = 1024 * 1024


def dot(a, b, contract, batch=((), ())):
    return lax.dot_general(a, b, (contract, batch), preferred_element_type=F32)


def mm(a, b):
    return dot(a, b, ((1,), (0,)))


def mm_t(a, b):
    return dot(a, b, ((1,), (1,)))


def t_mm(a, b):
    return dot(a, b, ((0,), (0,)))


def call(kernel, flops, moved, mib=12, **kw):
    return pl.pallas_call(
        kernel,
        compiler_params=pltpu.CompilerParams(vmem_limit_bytes=mib * MIB),
        cost_estimate=pl.CostEstimate(flops=flops, bytes_accessed=moved, transcendentals=0),
        **kw,
    )


def whole(shape):
    return pl.BlockSpec(shape, lambda *_: (0,) * len(shape))


def rows(count, columns, at=0):
    return pl.BlockSpec((count, columns), lambda g, *_: (g, at))


def shape_of(shape, dtype):
    return jax.ShapeDtypeStruct(shape, dtype)


def lane_column(shape, width):
    return lax.broadcasted_iota(jnp.int32, shape, 1) % width


def shifted(window, shift, start, count):
    size = window.shape[1]
    return pltpu.roll(window, (-shift) % size, 1)[:, start : start + count]


def other_core(values):
    return lax.ppermute(values, "rep", [(0, 1), (1, 0)])


def other_shard(values):
    return lax.ppermute(values, "exp", [(i, i ^ 1) for i in range(lax.axis_size("exp"))])


def exchange(values):
    count = lax.axis_size("exp")
    shards = count // values.shape[0]
    groups = None
    if shards > 1:
        groups = [[s + shards * e for e in range(values.shape[0])] for s in range(shards)]
    return lax.all_to_all(
        values, "exp", split_axis=0, concat_axis=0, tiled=True, axis_index_groups=groups
    )


def hbm():
    return pl.BlockSpec(memory_space=pl.ANY)


def vmem():
    return pl.BlockSpec(memory_space=pltpu.VMEM)


def fast(shape, dtype):
    return pltpu.VMEM(shape, dtype)


def near(values):
    return pltpu.with_memory_space_constraint(values, pltpu.VMEM)


def far_off(values):
    return pltpu.with_memory_space_constraint(values, pltpu.HBM)


def kernel_call(kernel, flops, moved, operands, outs, name, mib=12, place=None, steps=1, scratch=(), specs=None, out_specs=None):
    specs = specs or [vmem() for _ in operands]
    out_specs = out_specs or [vmem() for _ in outs]
    return call(
        kernel,
        flops,
        moved,
        mib,
        grid_spec=pltpu.PrefetchScalarGridSpec(
            num_scalar_prefetch=0 if place is None else 1,
            grid=(steps,),
            in_specs=specs,
            out_specs=out_specs,
            scratch_shapes=list(scratch),
        ),
        out_shape=outs,
        name=name,
    )(*(() if place is None else (place,)), *operands)


def tiles_of(columns):
    return -(-columns // LANES)


def stacked(values):
    columns = values.shape[1]
    spare = tiles_of(columns) * LANES - columns
    if spare:
        values = jnp.concatenate([values, jnp.zeros((values.shape[0], spare), F32)], axis=1)
    parts = [values[:, k * LANES : (k + 1) * LANES] for k in range(tiles_of(columns))]
    return jnp.concatenate(parts, axis=0)


def own_selection(routes, experts):
    tok = routes.shape[1]
    expert = lax.broadcasted_iota(jnp.int32, (experts, tok), 0).astype(F32)
    named = jnp.where((expert == routes[0:1]) | (expert == routes[1:2]), 1.0, 0.0)
    first = lax.broadcasted_iota(jnp.int32, (tok, tok), 0)
    second = lax.broadcasted_iota(jnp.int32, (tok, tok), 1)
    before = jnp.where(first <= second, 1.0, 0.0).astype(BF16)
    at = mm(named.astype(BF16), before) - 1.0
    slot = lax.broadcasted_iota(jnp.int32, (CAP, tok), 0).astype(F32)
    return [
        jnp.where((at[e : e + 1] == slot) & (named[e : e + 1] > 0.0), 1.0, 0.0)
        for e in range(experts)
    ]


def own_columns(cot, half):
    if cot.shape[1] == half:
        return cot
    return jnp.where(lax.axis_index("rep") == 0, cot[:, :half], cot[:, half:])


def pack_kernel(shards, half, latent_ref, routes_ref, cot_ref, out_ref, held, sem):
    rows_here = latent_ref.shape[0]
    experts = held.shape[0]
    cells = jnp.concatenate([latent_ref[r].astype(F32) for r in range(rows_here)], axis=1)
    routes = routes_ref[...].astype(F32)
    payload = jnp.concatenate([cells, routes], axis=0)
    sel = own_selection(routes, experts)
    cot = own_columns(cot_ref[...], half)
    cots = mm(jnp.concatenate(sel, axis=0).astype(BF16), cot)
    copies = []
    for e in range(experts):
        slots = stacked(cots[e * CAP : (e + 1) * CAP])
        held[e] = jnp.concatenate([slots, payload], axis=0).astype(BF16)
        for n in range(shards):
            block = e * shards + n
            copies.append(pltpu.make_async_copy(held.at[e], out_ref.at[block], sem.at[block]))
            copies[-1].start()
    for copy in copies:
        copy.wait()


def pack(latent, routes_t, cot, experts, shards, half):
    rows_here, channels, width = latent.shape
    top, tok = routes_t.shape
    blocks = experts * shards
    depth = tiles_of(half) * CAP + channels + top
    operands = [latent, routes_t, cot]
    return kernel_call(
        functools.partial(pack_kernel, shards, half),
        2 * blocks * CAP * tok * half,
        4 * blocks * depth * LANES,
        [far_off(a) for a in operands],
        [pltpu.HBM((blocks, depth, LANES), BF16)],
        "pack",
        specs=[whole(a.shape) for a in operands],
        out_specs=[hbm()],
        scratch=[pltpu.VMEM((experts, depth, LANES), BF16), pltpu.SemaphoreType.DMA((blocks,))],
    )[0]


def unpacked(ref, columns):
    tiles = tiles_of(columns)
    blocks = ref.shape[0]
    held = [ref[b, : tiles * CAP, :].astype(F32) for b in range(blocks)]
    parts = [
        jnp.concatenate([one[k * CAP : (k + 1) * CAP] for one in held], axis=0)
        for k in range(tiles)
    ]
    return jnp.concatenate(parts, axis=1)[:, :columns]


def unpack_kernel(packed_ref, after_ref, cot_ref, image_ref):
    cot_ref[...] = unpacked(packed_ref, cot_ref.shape[1]).astype(BF16)
    top = packed_ref.shape[1] - image_ref.shape[1]
    for b in range(packed_ref.shape[0]):
        image_ref[b] = packed_ref[b, top:, :]


def unpack(packed, half, lines, after):
    blocks, _, tok = packed.shape
    return kernel_call(
        unpack_kernel,
        100_000_000_000,
        4 * packed.size,
        [near(packed), far_off(after)],
        [fast((blocks * CAP, half), BF16), fast((blocks, lines, tok), BF16)],
        "unpack",
        specs=[vmem(), hbm()],
    )


def sum_kernel(a_ref, b_ref, after_ref, out_ref):
    out_ref[...] = (a_ref[...].astype(F32) + b_ref[...].astype(F32)).astype(out_ref.dtype)


def add_up(a, b, after):
    operands = [near(a), near(b), near(after)]
    outs = [fast(a.shape, a.dtype)]
    return kernel_call(sum_kernel, a.size, 6 * a.size, operands, outs, "add_up")[0]


def pack_back_kernel(
    paired, a_ref, b_ref, c_ref, terms_ref, over_ref, after_ref, out_ref, held, sem
):
    total = a_ref[...].astype(F32) + b_ref[...].astype(F32)
    if paired:
        total = total + c_ref[...].astype(F32)
    copies = []
    for b in range(out_ref.shape[0]):
        slots = stacked(total[b * CAP : (b + 1) * CAP])
        terms = terms_ref[b]
        if paired:
            terms = terms + over_ref[b].astype(F32)
        held[b] = jnp.concatenate([slots, terms], axis=0).astype(BF16)
        copies.append(pltpu.make_async_copy(held.at[b], out_ref.at[b], sem.at[b]))
        copies[-1].start()
    for copy in copies:
        copy.wait()


def pack_back(a, b, c, terms, over, after, paired):
    blocks, channels, tok = terms.shape
    depth = tiles_of(a.shape[1]) * CAP + channels
    return kernel_call(
        functools.partial(pack_back_kernel, paired),
        a.size,
        8 * a.size,
        [near(x) for x in (a, b, c, terms, over, after)],
        [pltpu.HBM((blocks, depth, LANES), BF16)],
        "pack_back",
        out_specs=[hbm()],
        scratch=[pltpu.VMEM((blocks, depth, LANES), BF16), pltpu.SemaphoreType.DMA((blocks,))],
    )[0]


PIECES = 4


def pieces(source, target, sem, at=0):
    deep = source.shape[0] // PIECES
    bands = [pl.ds(k * deep, deep) for k in range(PIECES)]
    return [
        pltpu.make_async_copy(source.at[band, :], target.at[band, :], sem.at[at + k])
        for k, band in enumerate(bands)
    ]


def far_kernel(place_ref, gate_ref, up_ref, down_ref, after_ref, gate_out, up_out, down_out, sem):
    size = gate_out.shape[1]
    at = pl.multiple_of((1 - place_ref[2]) * size, LANES)
    copies = (
        pieces(gate_ref.at[:, pl.ds(at, size)], gate_out, sem)
        + pieces(up_ref.at[:, pl.ds(at, size)], up_out, sem, PIECES)
        + pieces(down_ref.at[pl.ds(at, size), :], down_out, sem, 2 * PIECES)
    )
    for copy in copies:
        copy.start()
    for copy in copies:
        copy.wait()


def far_weights(place, gate, up, down, after):
    half, hid = gate.shape
    size = hid // 2
    return kernel_call(
        far_kernel,
        0,
        LANES,
        [far_off(gate), far_off(up), far_off(down), far_off(after)],
        [fast((half, size), BF16), fast((half, size), BF16), fast((size, half), BF16)],
        "far_weights",
        place=place,
        specs=[hbm()] * 4,
        scratch=[pltpu.SemaphoreType.DMA((3 * PIECES,))],
    )


def cuts(lengths):
    start, out = 0, []
    for n in lengths:
        out.append((start, n))
        start += n
    return out


def params_kernel(
    turn, experts, shards, place_ref, stem_in, gain_in, router_in, routes_ref, cot_ref, after,
    stem, gain, router, taken, cot,
):
    wide = router_in[...].astype(F32)
    model = wide.shape[0]
    blank = jnp.zeros((model, LANES - 2 * experts), F32)
    wide = jnp.concatenate([wide, wide, blank], axis=1)
    values, gains = stem_in[...], gain_in[...]
    if turn:
        half = model // 2
        first = place_ref[2] == 0
        wide = jnp.where(first, wide, jnp.concatenate([wide[half:], wide[:half]], axis=0))
        turned = jnp.concatenate([values[:, half:], values[:, :half]], axis=1)
        values = jnp.where(first, values, turned)
        turned = jnp.concatenate([gains[:, half:], gains[:, :half]], axis=1)
        gains = jnp.where(first, gains, turned)
    stem[...] = values
    gain[...] = gains
    router[...] = wide.astype(BF16)
    sel = own_selection(routes_ref[...].astype(F32), experts)
    taken[...] = jnp.concatenate([one for one in sel for _ in range(shards)], axis=0).astype(BF16)
    cot[...] = own_columns(cot_ref[...], cot.shape[1])


def small_params(place, stem, gain, router, routes_t, cot, half, shards, after, turn):
    model, experts = router.shape
    tok = cot.shape[0]
    small = [far_off(a) for a in (stem, gain, router, routes_t, cot)]
    shapes = [(stem.shape, BF16), (gain.shape, F32), ((model, LANES), BF16)]
    shapes += [((experts * shards * CAP, tok), BF16), ((tok, half), BF16)]
    return kernel_call(
        functools.partial(params_kernel, turn, experts, shards),
        0,
        LANES,
        small + [far_off(after)],
        [pltpu.HBM(*a) for a in shapes],
        "params",
        place=place,
        specs=[whole(a.shape) for a in small] + [hbm()],
        out_specs=[whole(shape) for shape, _ in shapes],
    )


def inner_copies(place_ref, refs, inner, size, at, sem):
    copies = []
    for n, (ref, (a, depth)) in enumerate(zip(refs, cuts([r.shape[0] for r in refs]))):
        if ref.shape[1] != size:
            ref = ref.at[:, pl.ds(pl.multiple_of(place_ref[2] * size, LANES), size)]
        copies += pieces(ref, inner.at[pl.ds(a, depth), pl.ds(at, size)], sem, n * PIECES)
    return copies


def outer_copies(place_ref, refs, outer, sem):
    copies = []
    size = outer.shape[0]
    for n, (ref, (a, depth)) in enumerate(zip(refs, cuts([r.shape[1] for r in refs]))):
        if ref.shape[0] != size:
            ref = ref.at[pl.ds(pl.multiple_of(place_ref[2] * size, LANES), size), :]
        copies += pieces(ref, outer.at[:, pl.ds(a, depth)], sem, n * PIECES)
    return copies


def gather_kernel(parts, place_ref, *refs):
    gates, (stem_in, gain_in, router_in) = refs[:parts], refs[parts : parts + 3]
    stem, gain, inner, small_sem, sem = refs[parts + 3 :]
    size = inner.shape[1] - LANES
    copies = [
        pltpu.make_async_copy(stem_in, stem, small_sem.at[0]),
        pltpu.make_async_copy(gain_in, gain, small_sem.at[1]),
        pltpu.make_async_copy(router_in, inner.at[:, pl.ds(size, LANES)], small_sem.at[2]),
    ]
    copies += inner_copies(place_ref, gates, inner, size, 0, sem)
    for copy in copies:
        copy.start()
    for copy in copies:
        copy.wait()


def gather(place, small, gates, size):
    stem, gain, router = small
    model = router.shape[0]
    operands = [far_off(gates[0])] + list(gates[1:]) + [far_off(a) for a in small]
    return kernel_call(
        functools.partial(gather_kernel, len(gates)),
        0,
        LANES,
        operands,
        [
            fast(stem.shape, BF16),
            fast(gain.shape, F32),
            fast((model, size + LANES), BF16),
        ],
        "gather",
        place=place,
        specs=[hbm()] * len(operands),
        scratch=[
            pltpu.SemaphoreType.DMA((3,)),
            pltpu.SemaphoreType.DMA((len(gates) * PIECES,)),
        ],
    )


def join_kernel(place_ref, own_ref, away_ref, a_ref, b_ref, out_ref, latent_ref):
    half = own_ref.shape[1]
    first = place_ref[2] == 0
    own, away = own_ref[...], away_ref[...]
    out_ref[:, :half] = jnp.where(first, own, away)
    out_ref[:, half:] = jnp.where(first, away, own)
    total = a_ref[...] + b_ref[...]
    width = latent_ref.shape[2]
    for r in range(latent_ref.shape[0]):
        latent_ref[r] = total[:, r * width : (r + 1) * width]


def join(place, own, away, a, b, rows_here):
    count, half = own.shape
    channels, tok = a.shape
    return kernel_call(
        join_kernel,
        0,
        8 * count * half,
        [near(own), near(away), near(a), near(b)],
        [
            shape_of((count, 2 * half), BF16),
            shape_of((rows_here, channels, tok // rows_here), F32),
        ],
        "join",
        place=place,
    )


def pair_selection(named):
    lanes = named.shape[1]
    tok = lanes // 2
    first = lax.broadcasted_iota(jnp.int32, (lanes, lanes), 0)
    second = lax.broadcasted_iota(jnp.int32, (lanes, lanes), 1)
    before = ((first <= second) & (first // tok == second // tok)).astype(F32).astype(BF16)
    wide = jnp.broadcast_to(named, (8, lanes)).astype(BF16)
    place = mm(wide, before)[:1]
    lane = lax.broadcasted_iota(jnp.int32, (1, lanes), 1)
    place = place - 1.0 + jnp.where(lane >= tok, float(CAP), 0.0)
    slot = lax.broadcasted_iota(jnp.int32, (2 * CAP, lanes), 0).astype(F32)
    return jnp.where((place == slot) & (named > 0.0), 1.0, 0.0)


def block_getter(paired, place_ref, image_refs):
    if not paired:
        return lambda pair, parity: image_refs[0][2 * pair + parity].astype(F32)
    side = place_ref[1] & 1

    def get(pair, parity):
        same, other = [ref[pair].astype(F32) for ref in image_refs]
        return jnp.where(side == parity, same, other)

    return get


def pair_patches(get, pair, pairs, width, channels):
    before = get(jnp.maximum(pair - 1, 0), 1)[:channels]
    after = get(jnp.minimum(pair + 1, pairs - 1), 0)[:channels]
    window = jnp.concatenate(
        [
            jnp.where(pair > 0, before, 0.0),
            get(pair, 0)[:channels],
            get(pair, 1)[:channels],
            jnp.where(pair + 1 < pairs, after, 0.0),
        ],
        axis=1,
    )
    tok = window.shape[1] // 4
    column = lane_column((channels, 2 * tok), width)
    pieces_of = []
    for i in range(3):
        for j in range(3):
            piece = shifted(window, (i - 1) * width + j - 1, tok, 2 * tok)
            source = column + (j - 1)
            pieces_of.append(jnp.where((source >= 0) & (source < width), piece, 0.0))
    return jnp.concatenate(pieces_of, axis=0)


def by_side(pairs, even):
    same = [jnp.where(even, p[:CAP], p[CAP:]) for p in pairs]
    other = [jnp.where(even, p[CAP:], p[:CAP]) for p in pairs]
    return same + other


def forward_kernel(
    paired, parts, width, experts, outs, place_ref, *refs
):
    images = 2 if paired else 1
    image_refs, (stem_ref, gain_ref, first_ref), refs = refs[:images], refs[images : images + 3], refs[images + 3 :]
    weights, router_in, refs = refs[: 3 * parts], refs[3 * parts], refs[3 * parts + 1 :]
    refs = refs[1:] if paired else refs
    saved_ref, normed_ref, value_ref, meta_ref, coef_ref, sel_ref, pg_ref, pu_ref = refs[:8]
    hidden_ref, inner, outer, *out_refs = refs[8:-4]
    save_sem, up_sem, down_sem, gate_sem = refs[-4:]
    step = pl.program_id(0)
    size = outer.shape[0]
    up_copies = inner_copies(place_ref, weights[:parts], inner, size, size, up_sem)
    down_copies = outer_copies(place_ref, weights[parts : 2 * parts], outer, down_sem)
    later = inner_copies(place_ref, weights[2 * parts :], inner, size, 0, gate_sem)
    wide = inner.at[:, pl.ds(2 * size, LANES)]
    later.append(pltpu.make_async_copy(router_in, wide, gate_sem.at[parts * PIECES]))

    def arrive(copies):
        @pl.when(step == 0)
        def _():
            for copy in copies:
                copy.wait()

    @pl.when(step == 0)
    def _():
        for copy in up_copies + down_copies + later:
            copy.start()

    chunk = GROUP * CAP
    here = pl.ds(pl.multiple_of(step * chunk, chunk), chunk)
    channels = image_refs[0].shape[1] - 2
    pairs = images * image_refs[0].shape[0] // 2
    get = block_getter(paired, place_ref, image_refs)
    mine = place_ref[0].astype(F32)
    even = (place_ref[1] & 1) == 0
    taken, others = [], []
    for q in range(GROUP // 2):
        pair = step * (GROUP // 2) + q
        lines = [get(pair, n)[channels:] for n in range(2)]
        named_by = [jnp.concatenate([line[k : k + 1] for line in lines], axis=1) for k in range(2)]
        named = jnp.where((named_by[0] == mine) | (named_by[1] == mine), 1.0, 0.0)
        sel = pair_selection(named)
        sel_ref[step * (GROUP // 2) + q] = sel.astype(BF16)
        other = named_by[0] + named_by[1] - mine
        others.append(jnp.sum(sel * other, axis=1, keepdims=True))
        patches = pair_patches(get, pair, pairs, width, channels)
        taken.append(mm_t(sel.astype(BF16), patches.astype(BF16)))
    bands = 2 if paired else 1
    deep = chunk // bands
    lines = [pl.ds(pl.multiple_of(step * chunk + k * deep, deep), deep) for k in range(bands)]
    held = [slice(k * deep, (k + 1) * deep) for k in range(bands)]
    if paired:
        taken, others = by_side(taken, even), by_side(others, even)
    each = len(taken) // bands
    patches = [
        jnp.concatenate(taken[k * each : (k + 1) * each], axis=0).astype(BF16) for k in range(bands)
    ]
    others = [jnp.concatenate(others[k * each : (k + 1) * each], axis=0) for k in range(bands)]
    stems = [mm(one, stem_ref[...]).astype(BF16) for one in patches]
    normeds, scales, gates, gated, upped, hiddens = [], [], [], [], [], []
    for line, band, stem in zip(lines, held, stems):
        value_ref[line, :] = stem
        value = stem.astype(F32)
        scale = lax.rsqrt(jnp.mean(value * value, axis=-1, keepdims=True) + 1e-06)
        normed = (value * scale * gain_ref[...]).astype(BF16)
        normed_ref[band, :] = normed
        normeds.append(normed)
        scales.append(scale)
    own_part = normed_ref.at[:, pl.ds(0, saved_ref.shape[1])]
    save = pltpu.make_async_copy(own_part, saved_ref.at[here, :], save_sem.at[0])
    save.start()
    for normed in normeds:
        gated.append(mm(normed, first_ref[:, :size]))
    for line, normed, other, scale in zip(lines, normeds, others, scales):
        logits = mm(normed, first_ref[:, size:])
        lane = lax.broadcasted_iota(jnp.int32, logits.shape, 1)
        again = jnp.where(lane >= experts, lane - experts, lane).astype(F32)
        lane = lane.astype(F32)
        mine_logit = jnp.sum(jnp.where(lane == mine, logits, 0.0), axis=1, keepdims=True)
        other_logit = jnp.sum(jnp.where(lane == other, logits, 0.0), axis=1, keepdims=True)
        sig_mine, sig_other = jax.nn.sigmoid(mine_logit), jax.nn.sigmoid(other_logit)
        gate = sig_mine / (sig_mine + sig_other)
        rest = sig_other / (sig_mine + sig_other)
        both = gate * rest
        coef_ref[line, :] = jnp.where(again == mine, both * (1.0 - sig_mine), 0.0) - jnp.where(
            again == other, both * (1.0 - sig_other), 0.0
        )
        meta_ref[line, :] = jnp.where(lane == 0.0, gate, scale)
        gates.append(gate)
    arrive(up_copies)
    for normed in normeds:
        upped.append(mm(normed, inner[:, size : 2 * size]))
    arrive(down_copies)
    for line, pre_gate, pre_up in zip(lines, gated, upped):
        pg_ref[line, :] = pre_gate.astype(BF16)
        pu_ref[line, :] = pre_up.astype(BF16)
        hidden = (pre_gate * jax.nn.sigmoid(pre_gate) * pre_up).astype(BF16)
        hidden_ref[line, :] = hidden
        hiddens.append(hidden)
    for ref, (a, n) in zip(out_refs, cuts([r.shape[1] for r in out_refs])):
        part = (gates[-1] * mm(hiddens[-1], outer[:, a : a + n])).astype(BF16)
        if paired:
            ref[...] = part
        else:
            ref[here, :] = part
    save.wait()
    arrive(later)


def forward(place, images, gathered, router, weights, size, columns, after, paired, width, experts):
    blocks = sum(image.shape[0] for image in images)
    tok = images[0].shape[2]
    slots, chunk = blocks * CAP, GROUP * CAP
    stem, gain, inner = gathered
    model = stem.shape[1]
    parts = len(weights) // 3
    operands = [near(a) for a in list(images) + [stem, gain, inner]]
    specs = [vmem()] * len(operands) + [hbm()] * (len(weights) + 1)
    operands += [far_off(w) if k % parts == 0 else w for k, w in enumerate(weights)]
    operands.append(far_off(router))
    if paired:
        operands.append(near(after))
        specs.append(vmem())
    outs = [
        pltpu.HBM((slots, columns[0]), BF16),
        fast((chunk, model), BF16),
        fast((slots, model), BF16),
        fast((slots, LANES), F32),
        fast((slots, LANES), F32),
        fast((blocks // 2, 2 * CAP, 2 * tok), BF16),
        fast((slots, size), BF16),
        fast((slots, size), BF16),
        fast((slots, size), BF16),
        fast((model, 2 * size + LANES), BF16),
        fast((size, model), BF16),
    ]
    outs += [fast((slots // 2 if paired else slots, n), BF16) for n in columns]
    return pl.pallas_call(
        functools.partial(forward_kernel, paired, parts, width, experts, columns),
        compiler_params=pltpu.CompilerParams(vmem_limit_bytes=20 * MIB),
        cost_estimate=pl.CostEstimate(
            flops=FORWARD_FLOPS, bytes_accessed=LANES, transcendentals=0
        ),
        grid_spec=pltpu.PrefetchScalarGridSpec(
            num_scalar_prefetch=1,
            grid=(blocks // GROUP,),
            in_specs=specs,
            out_specs=[hbm()] + [vmem()] * (len(outs) - 1),
            scratch_shapes=[
                pltpu.SemaphoreType.DMA((1,)),
                pltpu.SemaphoreType.DMA((parts * PIECES,)),
                pltpu.SemaphoreType.DMA((parts * PIECES,)),
                pltpu.SemaphoreType.DMA((parts * PIECES + 1,)),
            ],
        ),
        out_shape=outs,
        name="forward",
    )(place, *operands)


def own_stem_kernel(paired, width, place_ref, *refs):
    image_refs, (stem_ref, own_ref) = refs[:-2], refs[-2:]
    me = place_ref[1]
    channels = image_refs[0].shape[1] - 2
    tok = image_refs[0].shape[2]
    pairs = len(image_refs) * image_refs[0].shape[0] // 2
    own = pair_patches(block_getter(paired, place_ref, image_refs), me // 2, pairs, width, channels)
    own = jnp.where(me % 2 == 0, own[:, :tok], own[:, tok:]).astype(BF16)
    own_ref[...] = t_mm(own, stem_ref[:, : own_ref.shape[1]]).astype(BF16)


def own_stem_of(place, images, stem, half, paired, width):
    tok = images[0].shape[2]
    return kernel_call(
        functools.partial(own_stem_kernel, paired, width),
        0,
        LANES,
        [near(a) for a in list(images) + [stem]],
        [pltpu.HBM((tok, half), BF16)],
        "own_stem",
        place=place,
        out_specs=[whole((tok, half))],
    )[0]


def outputs_kernel(width, place_ref, meta_ref, hidden_ref, outer, same_ref, other_ref, stem_ref, near_ref, far_ref, own_ref):
    own_stem_kernel(True, width, place_ref, same_ref, other_ref, stem_ref, own_ref)
    count, half = near_ref.shape
    gate = meta_ref[:count, 0:1]
    hidden = hidden_ref[:count, :]
    near_ref[...] = (gate * mm(hidden, outer[:, :half])).astype(BF16)
    far_ref[...] = (gate * mm(hidden, outer[:, half:])).astype(BF16)


def outputs(place, meta, hidden, outer, images, stem, width):
    count, half = hidden.shape[0] // 2, outer.shape[1] // 2
    tok = images[0].shape[2]
    return kernel_call(
        functools.partial(outputs_kernel, width),
        0,
        LANES,
        [near(a) for a in [meta, hidden, outer] + list(images) + [stem]],
        [fast((count, half), BF16)] * 2 + [pltpu.HBM((tok, half), BF16)],
        "outputs",
        place=place,
        out_specs=[vmem()] * 2 + [whole((tok, half))],
    )


def backward_kernel(
    parts, bands, experts, stem_ref, gain_ref, inner, outer, value_ref, meta_ref, coef_ref, pg_ref, pu_ref,
    *refs,
):
    cot_refs, refs = refs[: parts * bands], refs[parts * bands :]
    saved, refs = refs[:4], refs[4:]
    proj_ref, ggp_ref, gup_ref, hg_ref, sem = refs
    step = pl.program_id(0)
    model = stem_ref.shape[1]
    chunk = GROUP * CAP
    here = pl.ds(pl.multiple_of(step * chunk, chunk), chunk)
    sources = [ggp_ref, gup_ref, hg_ref]
    targets = [ref.at[here, :] for ref in saved[:3]]
    for n, ref in enumerate(cot_refs[:bands]):
        if bands == 1:
            sources.append(ref.at[here, :])
            targets.append(saved[3].at[here, :])
        else:
            sources.append(ref)
            targets.append(saved[3].at[pl.ds(n * ref.shape[0], ref.shape[0]), :])
    saves = [
        pltpu.make_async_copy(a, b, sem.at[n]) for n, (a, b) in enumerate(zip(sources, targets))
    ]
    for save in saves[3:]:
        save.start()
    deep = chunk // bands
    places = cuts([r.shape[1] for r in cot_refs[::bands]])
    lines = [pl.ds(pl.multiple_of(step * chunk + k * deep, deep), deep) for k in range(bands)]
    held = [slice(k * deep, (k + 1) * deep) for k in range(bands)]
    gates = [meta_ref[line, 0:1] for line in lines]
    scales = [meta_ref[line, 1:2] for line in lines]
    raws, mixes, backs, grads = [], [], [], []
    for k, line in enumerate(lines):
        raw = 0.0
        for n, (a, m) in enumerate(places):
            cot = cot_refs[n * bands + k][...] if bands > 1 else cot_refs[n][line, :]
            raw = raw + mm_t(cot, outer[:, a : a + m])
        raws.append(raw)
    for line, band, gate, raw in zip(lines, held, gates, raws):
        pre_gate = pg_ref[line, :].astype(F32)
        pre_up = pu_ref[line, :].astype(F32)
        sigma = jax.nn.sigmoid(pre_gate)
        silu = pre_gate * sigma
        hidden = silu * pre_up
        grad_gates = jnp.sum(raw * hidden, axis=1, keepdims=True)
        hg_ref[band, :] = (gate * hidden).astype(BF16)
        grad_hidden = gate * raw
        ggp = (grad_hidden * pre_up * sigma * (1.0 + pre_gate - silu)).astype(BF16)
        gup = (grad_hidden * silu).astype(BF16)
        ggp_ref[band, :] = ggp
        gup_ref[band, :] = gup
        grad_logits = grad_gates * coef_ref[line, :]
        high = grad_logits.astype(BF16)
        low = (grad_logits - high.astype(F32)).astype(BF16)
        lane = lax.broadcasted_iota(jnp.int32, grad_logits.shape, 1)
        mix = jnp.where(lane < experts, high.astype(F32), low.astype(F32)).astype(BF16)
        mixes.append(jnp.concatenate([ggp, gup, mix], axis=1))
    for save in saves[:3]:
        save.start()
    for mix in mixes:
        backs.append(mm_t(mix, inner[...]))
    for line, scale, back in zip(lines, scales, backs):
        back = back * gain_ref[...]
        value = value_ref[line, :].astype(F32)
        along = jnp.sum(back * value, axis=1, keepdims=True) * (scale * scale * scale) / model
        grads.append((scale * back - along * value).astype(BF16))
    for line, grad in zip(lines, grads):
        proj_ref[line, :] = mm_t(grad, stem_ref[...]).astype(BF16)
    for save in saves:
        save.wait()


def backward(stem, gain, inner, outer, acts, cots, experts):
    slots, model = acts[0].shape
    size, chunk = outer.shape[0], GROUP * CAP
    taps = stem.shape[0]
    parts, bands = len(cots), len(cots[0])
    operands = [stem, gain, inner, outer] + list(acts) + [c for part in cots for c in part]
    return kernel_call(
        functools.partial(backward_kernel, parts, bands, experts),
        2 * slots * model * size * 4,
        slots * (4 * model + 12 * size) + 6 * model * size,
        [near(a) for a in operands],
        [pltpu.HBM((slots, size), BF16)] * 3
        + [pltpu.HBM((slots, cots[0][0].shape[1]), BF16)]
        + [fast((slots, taps), BF16)]
        + [fast((chunk, size), BF16)] * 3,
        "backward",
        mib=20,
        steps=slots // chunk,
        out_specs=[hbm()] * 4 + [vmem()] * 4,
        scratch=[pltpu.SemaphoreType.DMA((3 + bands,))],
    )


def image_kernel(paired, width, place_ref, proj_ref, sel_ref, stem_ref, cot_ref, *refs):
    out_refs, terms = refs[:-1], refs[-1]
    pairs = sel_ref.shape[0]
    tok = cot_ref.shape[0]
    channels = out_refs[0].shape[1]
    count = 2 * pairs * tok
    own = mm_t(stem_ref[:, : cot_ref.shape[1]], cot_ref[...])
    me = place_ref[1]
    even = (me & 1) == 0
    proj = proj_ref[...].astype(F32)
    for q in range(pairs):
        if paired:
            same = proj[CAP * q : CAP * (q + 1)]
            other = proj[CAP * (pairs + q) : CAP * (pairs + q + 1)]
            both = [jnp.where(even, same, other), jnp.where(even, other, same)]
            pair = jnp.concatenate(both, axis=0)
        else:
            pair = proj[2 * CAP * q : 2 * CAP * (q + 1)]
        block = t_mm(pair.astype(BF16), sel_ref[q])
        terms[:, 2 * q * tok : (2 * q + 1) * tok] = block[:, :tok] + jnp.where(2 * q == me, own, 0.0)
        terms[:, (2 * q + 1) * tok : (2 * q + 2) * tok] = block[:, tok:] + jnp.where(
            2 * q + 1 == me, own, 0.0
        )
    lane = lax.broadcasted_iota(jnp.int32, (channels, count), 1)
    total = jnp.zeros((channels, count), F32)
    for i in range(3):
        for j in range(3):
            k = (3 * i + j) * channels
            shift = (i - 1) * width + j - 1
            piece = pltpu.roll(terms[k : k + channels, :], shift % count, 1)
            column = lane % width + (1 - j)
            token = lane - shift
            keep = (column >= 0) & (column < width) & (token >= 0) & (token < count)
            total = total + jnp.where(keep, piece, 0.0)
    for q in range(pairs):
        low = total[:, 2 * q * tok : (2 * q + 1) * tok]
        high = total[:, (2 * q + 1) * tok : (2 * q + 2) * tok]
        if paired:
            out_refs[0][q] = jnp.where(even, low, high)
            out_refs[1][q] = jnp.where(even, high, low).astype(BF16)
        else:
            out_refs[0][2 * q] = low
            out_refs[0][2 * q + 1] = high


def to_image(place, proj, sel, stem, cot, paired, width, channels):
    pairs = sel.shape[0]
    blocks, tok = 2 * pairs, cot.shape[0]
    taps, half = stem.shape[0], cot.shape[1]
    return kernel_call(
        functools.partial(image_kernel, paired, width),
        2 * proj.shape[0] * 2 * tok * taps,
        4 * taps * blocks * tok,
        [near(a) for a in (proj, sel, stem, cot)],
        [fast((pairs, channels, tok), F32), fast((pairs, channels, tok), BF16)]
        if paired
        else [fast((blocks, channels, tok), F32)],
        "to_image",
        place=place,
        scratch=[pltpu.VMEM((taps, blocks * tok), F32)],
    )


def far_grads_kernel(normed, ggp, gup, hg, *refs):
    cots, (gate_out, up_out, down_out) = refs[:-3], refs[-3:]
    half = cots[0].shape[1]
    far = normed[:, half:]
    gate_out[...] = t_mm(far, ggp[...]).astype(BF16)
    up_out[...] = t_mm(far, gup[...]).astype(BF16)
    cot = jnp.concatenate([ref[...] for ref in cots], axis=0)
    down_out[...] = t_mm(hg[...], cot).astype(BF16)


def far_grads(normed, ggp, gup, hg, cots):
    slots, size = ggp.shape
    half = cots[0].shape[1]
    return kernel_call(
        far_grads_kernel,
        6 * slots * size * half,
        20 * slots * size,
        [near(a) for a in [normed, ggp, gup, hg] + list(cots)],
        [fast((half, size), BF16)] * 2 + [fast((size, half), BF16)],
        "far_grads",
    )


def near_grads_kernel(
    place_ref, normed, ggp, gup, hg, cot, after_ref, gate_out, up_out, down_out,
    left, right, own, sem, own_sem,
):
    half = cot.shape[1]
    size = ggp.shape[1]
    here = pl.multiple_of(place_ref[2] * size, LANES)
    sources = (normed, ggp, gup, hg, cot)
    targets = (left.at[0], right.at[0], right.at[1], left.at[1], right.at[2])
    loads = [pltpu.make_async_copy(a, b, sem.at[n]) for n, (a, b) in enumerate(zip(sources, targets))]
    places = (
        gate_out.at[:, pl.ds(here, size)],
        up_out.at[:, pl.ds(here, size)],
        down_out.at[pl.ds(here, size), :],
    )
    results = [pieces(own.at[n], a, own_sem, n * PIECES) for n, a in enumerate(places)]
    for load in loads:
        load.start()
    for load in loads[:2]:
        load.wait()
    own[0] = t_mm(left[0], right[0])
    for copy in results[0]:
        copy.start()
    loads[2].wait()
    own[1] = t_mm(left[0], right[1])
    for copy in results[1]:
        copy.start()
    loads[3].wait()
    loads[4].wait()
    own[2] = t_mm(left[1], right[2])
    for copy in results[2]:
        copy.start()
    for copy in results[0] + results[1] + results[2]:
        copy.wait()


def near_grads(place, normed, ggp, gup, hg, cot, after):
    slots, size = ggp.shape
    half = cot.shape[1]
    return kernel_call(
        near_grads_kernel,
        14_000_000_000,
        LANES,
        [far_off(a) for a in (normed, ggp, gup, hg, cot, after)],
        [pltpu.HBM((half, 2 * size), F32)] * 2
        + [pltpu.HBM((2 * size, half), F32)],
        "near_grads",
        mib=14,
        place=place,
        specs=[hbm()] * 6,
        out_specs=[hbm()] * 3,
        scratch=[
            pltpu.VMEM((2, slots, half), BF16),
            pltpu.VMEM((3, slots, half), BF16),
            pltpu.VMEM((3, half, size), F32),
            pltpu.SemaphoreType.DMA((5,)),
            pltpu.SemaphoreType.DMA((3 * PIECES,)),
        ],
    )


def fill_kernel(
    place_ref, gate_in, up_in, down_in, gate_old, up_old, down_old,
    gate_out, up_out, down_out, done_ref, away, wide, in_sem, sem,
):
    size = gate_in.shape[1]
    there = pl.multiple_of((1 - place_ref[2]) * size, LANES)
    places = (
        gate_out.at[:, pl.ds(there, size)],
        up_out.at[:, pl.ds(there, size)],
        down_out.at[pl.ds(there, size), :],
    )
    loads = [
        pieces(a, away.at[n], in_sem, n * PIECES) for n, a in enumerate((gate_in, up_in, down_in))
    ]
    results = [pieces(wide.at[n], a, sem, n * PIECES) for n, a in enumerate(places)]
    deep = wide.shape[1] // PIECES
    done_ref[...] = jnp.zeros(done_ref.shape, F32)
    for load in loads[0] + loads[1] + loads[2]:
        load.start()
    for n in range(3):
        for k in range(PIECES):
            loads[n][k].wait()
            wide[n, k * deep : (k + 1) * deep] = away[n, k * deep : (k + 1) * deep].astype(F32)
            results[n][k].start()
    for copy in results[0] + results[1] + results[2]:
        copy.wait()


def fill(place, away, grads):
    shape = away[0].shape
    return pl.pallas_call(
        fill_kernel,
        compiler_params=pltpu.CompilerParams(vmem_limit_bytes=12 * MIB),
        cost_estimate=pl.CostEstimate(
            flops=7_000_000_000, bytes_accessed=LANES, transcendentals=0
        ),
        grid_spec=pltpu.PrefetchScalarGridSpec(
            num_scalar_prefetch=1,
            grid=(1,),
            in_specs=[hbm()] * 6,
            out_specs=[hbm()] * 3 + [vmem()],
            scratch_shapes=[
                pltpu.VMEM((3,) + shape, BF16),
                pltpu.VMEM((3,) + shape, F32),
                pltpu.SemaphoreType.DMA((3 * PIECES,)),
                pltpu.SemaphoreType.DMA((3 * PIECES,)),
            ],
        ),
        out_shape=[pltpu.HBM(g.shape, F32) for g in grads] + [fast((8, LANES), F32)],
        input_output_aliases={4: 0, 5: 1, 6: 2},
        name="fill",
    )(place, *[far_off(a) for a in away], *grads)


def gathered_grads(column, size, normed, ggp, gup, hg, cot):
    grads = []
    for g in (ggp[:, :size], gup[:, :size]):
        term = jnp.roll(t_mm(normed, g).astype(BF16), column, 0)
        grads.append(lax.all_to_all(term, "rep", split_axis=0, concat_axis=1, tiled=True))
    term = jnp.roll(t_mm(hg[:, :size], cot).astype(BF16), column, 1)
    grads.append(lax.all_to_all(term, "rep", split_axis=1, concat_axis=0, tiled=True))
    return [g.astype(F32) for g in grads]


def mixed_kernel(stem_ref, taken_ref, back_ref, after_ref, out_ref, *terms_refs):
    half = out_ref.shape[1]
    back = unpacked(back_ref, half).astype(BF16)
    total = stem_ref[...].astype(F32) + t_mm(taken_ref[...], back)
    out_ref[...] = total.astype(BF16)
    top = tiles_of(half) * CAP
    terms = back_ref[0, top:, :].astype(F32)
    for b in range(1, back_ref.shape[0]):
        terms = terms + back_ref[b, top:, :].astype(F32)
    for n, ref in enumerate(terms_refs):
        ref[...] = terms[n * ref.shape[0] : (n + 1) * ref.shape[0]]


def mix(stem, taken, back, after, channels):
    tok, half = stem.shape
    sides = (back.shape[1] - tiles_of(half) * CAP) // channels
    return kernel_call(
        mixed_kernel,
        2 * taken.shape[0] * tok * half,
        2 * back.size,
        [near(a) for a in (stem, taken, back, after)],
        [fast((tok, half), BF16)] + [fast((channels, tok), F32)] * sides,
        "mixed",
    )


def local(
    latent,
    stem_weight,
    norm_gain,
    router_weight,
    routes,
    gate_weight,
    up_weight,
    down_weight,
    grad_mixed,
):
    rows_here, channels, width = latent.shape
    half = gate_weight.shape[0]
    experts = router_weight.shape[1]
    tok = rows_here * width
    blocks = lax.axis_size("exp")
    cores = lax.axis_size("rep")
    shards = blocks // experts
    slots = blocks * CAP
    me = lax.axis_index("exp")
    core = lax.axis_index("rep")
    column = core * half
    place = jnp.stack([me // shards, me, core]).astype(jnp.int32)

    paired = cores == 2 and shards == 2
    given = grad_mixed
    if cores != 2:
        given = lax.dynamic_slice_in_dim(grad_mixed, column, half, 1)
    copies = 1 if paired else shards
    routes_t = routes.T
    packed = pack(latent, routes_t, given, experts, copies, half)
    arrived = exchange(packed)

    stem, gain, router = stem_weight, norm_gain[None, :], router_weight
    if cores == 2:
        far = far_weights(place, gate_weight, up_weight, down_weight, packed)
        gate_parts, up_parts, down_parts = [
            (w, other_core(f)) for w, f in zip((gate_weight, up_weight, down_weight), far)
        ]
    else:
        turned = lax.all_to_all(gate_weight, "rep", split_axis=1, concat_axis=0, tiled=True)
        spare = -turned.shape[1] % LANES
        gate_parts = (jnp.pad(jnp.roll(turned, -column, 0), ((0, 0), (0, spare))),)
        turned = lax.all_to_all(up_weight, "rep", split_axis=1, concat_axis=0, tiled=True)
        up_parts = (jnp.pad(jnp.roll(turned, -column, 0), ((0, 0), (0, spare))),)
        turned = lax.all_to_all(down_weight, "rep", split_axis=0, concat_axis=1, tiled=True)
        down_parts = (jnp.pad(jnp.roll(turned, -column, 1), ((0, spare), (0, 0))),)
        stem = jnp.roll(stem, -column, 1)
        gain = jnp.roll(gain, -column, 1)
        router = jnp.roll(router, -column, 0)

    *small, taken, cot = small_params(
        place, stem, gain, router, routes_t, given, half, copies, packed, cores == 2
    )
    same_cot, image = unpack(arrived, half, channels + 2, small[1])
    size = down_parts[-1].shape[0]
    gathered = gather(place, small, gate_parts, size)
    if paired:
        joined = other_core(same_cot)
        images = [image, other_shard(image)]
        cots = [[same_cot], [joined]]
        far_cot = other_shard(same_cot)
    elif cores == 2:
        images, joined = [image], other_core(same_cot)
        cots = [[same_cot], [joined]]
    else:
        images = [image]
        joined = lax.all_gather(same_cot, "rep", axis=1, tiled=True)
        cots = [[jnp.roll(joined, -column, 1)]]
    weights = list(up_parts) + list(down_parts) + list(gate_parts)
    columns = [w.shape[1] for w in down_parts]
    kept, normed, value, meta, coef, sel, pg, pu, hidden, inner, outer, *outs = forward(
        place, images, gathered, small[2], weights, size, columns, joined, paired, width, experts
    )
    stem, gain, _ = gathered
    if paired:
        own, away, own_stem = outputs(place, meta, hidden, outer, images, stem, width)
        far_cot, own = lax.optimization_barrier((far_cot, own))
        cots[0].append(far_cot)
        cots[1].append(other_core(far_cot))
        over = other_shard(add_up(outs[0], other_core(outs[1]), own))
        away = other_core(away)
    elif cores == 2:
        own, away = outs[0], other_core(outs[1])
        over = own
        own_stem = own_stem_of(place, images, stem, half, paired, width)
    else:
        turned = jnp.roll(outs[0], column, 1)
        own = lax.psum_scatter(turned, "rep", scatter_dimension=1, tiled=True)
        away = over = jnp.zeros_like(own)
        own_stem = own_stem_of(place, images, stem, half, paired, width)
    acts = [value, meta, coef, pg, pu]
    ggp, gup, hg, held, proj, ggp_here, gup_here, hg_here = backward(
        stem, gain, inner, outer, acts, cots, experts
    )
    terms = to_image(place, proj, sel, stem, cot, paired, width, channels)
    terms_over = other_shard(terms[1]) if paired else terms[0]
    if cores == 2:
        far = far_grads(normed, ggp_here, gup_here, hg_here, cots[1])
        away_grads = [other_core(f) for f in far]

    after = far[0] if cores == 2 else own
    sent = pack_back(own, away, over, terms[0], terms_over, after, paired)
    back = exchange(sent)

    if cores == 2:
        grads = near_grads(place, kept, ggp, gup, hg, held, sent)
        *grads, done = fill(place, away_grads, grads)
    else:
        done = jnp.zeros((8, LANES), F32)
        size = gate_weight.shape[1] // cores
        grads = gathered_grads(column, size, kept, ggp, gup, hg, held)
    grad_gate, grad_up, grad_down = grads

    mixed, lat_sum = mix(own_stem, taken, back, done, channels)
    if cores == 2:
        mixed, grad_latent = join(
            place, mixed, other_core(mixed), lat_sum, other_core(lat_sum), rows_here
        )
    else:
        mixed = lax.all_gather(mixed, "rep", axis=1, tiled=True)
        lat_sum = lax.psum(lat_sum, "rep")
        grad_latent = lat_sum.reshape(channels, rows_here, width).transpose(1, 0, 2)
    return (mixed, grad_latent, grad_gate, grad_up, grad_down)


def solution(mesh):
    return jax.shard_map(
        local,
        mesh=mesh,
        in_specs=(
            P("exp", None, None),
            P(),
            P(),
            P(),
            P("exp", None),
            P("rep", "exp"),
            P("rep", "exp"),
            P("exp", "rep"),
            P("exp", None),
        ),
        out_specs=(
            P("exp", None),
            P("exp", None, None),
            P("rep", "exp"),
            P("rep", "exp"),
            P("exp", "rep"),
        ),
        check_vma=False,
    )
```
